256 devices in a mesh: gx: 16 (over x, z_hi), gy: 8 (over z_lo, y), gz: 2 (over core).
Axes of the slice: x: 4, y: 4, z: 8 (z_hi: 4, z_lo: 2; z = z_hi * 2 + z_lo), core: 2. Of those that a mesh axis runs over, the one named last changes fastest.
Arguments:
- efield: float32 [3, 128, 192, 256], P(None, 'gx', 'gy', 'gz'), may hold values from -6 to 6
- hfield: float32 [3, 128, 192, 256], P(None, 'gx', 'gy', 'gz'), may hold values from -6 to 6
- inv_eps: float32 [128, 192, 256], P('gx', 'gy', 'gz'), may hold values from 0.15 to 1
- gain_state: float32 [16, 8, 2, 32, 10, 128], P('gx', 'gy', 'gz'), as said below
- pump: float32 [16, 8, 2, 32, 128], P('gx', 'gy', 'gz'), may hold values from 0.01 to 0.3
- gain_offsets: int32 [16, 8, 2, 32, 128], P('gx', 'gy', 'gz'), may hold values from 0 to 24575, as said below
- gain_count: int32 [16, 8, 2], P('gx', 'gy', 'gz'), may hold values from 1 to 32, as said below
- block_owner: int32 [16, 8, 2, 32], P('gx', 'gy', 'gz'), may hold values from 0 to 31, each once within a row
- surf_offsets: int32 [16, 8, 2, 128], P('gx', 'gy', 'gz'), may hold values from 0 to 24575, as said below
- far_acc: float32 [64, 12, 128], P('gz'), may hold values from -6 to 6
Outputs:
- efield_out: float32 [3, 128, 192, 256], P(None, 'gx', 'gy', 'gz')
- hfield_out: float32 [3, 128, 192, 256], P(None, 'gx', 'gy', 'gz')
- state_out: float32 [16, 8, 2, 32, 10, 128], P('gx', 'gy', 'gz')
- far_out: float32 [64, 12, 128], P('gz')
The draws below stay inside these ranges and needn't reach their ends.
Inputs may be any that keep to these rules, and one draw needn't show every extreme that they name: `gain_offsets`: within one brick all offsets are distinct. `gain_count`: some brick holds 32 live blocks in every draw. `block_owner`: each brick's codes are a permutation of 0 to 31. `surf_offsets`: within one brick all offsets are distinct. `gain_state`: populations lie in 0.05 to 1.
All inputs are finite; a program needn't handle non-finite values.
Results may differ from the reference program's by a relative error of at most 0.00022.
Values sent between devices are 32-bit elements; how exact they have to be, the bound alone decides.
No kernel may reach another device: no remote copies, remote signals or barrier semaphores. Data moves between devices by JAX's collectives and lax.ppermute only.
A program may use at most 64 MiB of HBM per device.

```python
import math
import jax
import jax.numpy as jnp
from jax import lax

CX = 8
CY = 24
CZ = 128
BLOCK = 128
CAP = 2
FREQ = 64
DIRS = 128
SURF = 128
STEPS = 2
NX = 128
NY = 192
NZ = 256
BRX = 16
BRY = 8
BRZ = 2
SLOTS = 32


def first_cells(key, count):
    keys = jax.random.split(key, BRX * BRY * BRZ)
    picks = jax.vmap(lambda single: jax.random.permutation(single, CX * CY * CZ)[:count])(keys)
    return picks.astype(jnp.int32)


def draw_gain_state(key, part):
    key = jax.random.fold_in(key, 11)
    first, second = jax.random.split(key)
    shape = (BRX, BRY, BRZ, SLOTS, 6, BLOCK)
    moments = 0.5 * jax.random.normal(first, shape, jnp.float32)
    levels = jax.random.uniform(second, (BRX, BRY, BRZ, SLOTS, 4, BLOCK), jnp.float32, 0.05, 1.0)
    return jnp.concatenate([moments, levels], axis=4)


def draw_gain_offsets(key, part):
    key = jax.random.fold_in(key, 21)
    return first_cells(key, SLOTS * BLOCK).reshape(BRX, BRY, BRZ, SLOTS, BLOCK)


def draw_gain_count(key, part):
    key = jax.random.fold_in(key, 31)
    first, second = jax.random.split(key)
    rich = jax.random.randint(first, (), 0, 4)
    sparse = jax.random.randint(second, (BRX, BRY, BRZ), 1, SLOTS // 4 + 1)
    column = jnp.arange(BRX, dtype=jnp.int32)[:, None, None] % 4
    return jnp.where(column == rich, SLOTS, sparse).astype(jnp.int32)


def draw_surf_offsets(key, part):
    key = jax.random.fold_in(key, 41)
    return first_cells(key, SURF).reshape(BRX, BRY, BRZ, SURF)


def steps_of(stream_key, shape, cuts, low, top_value):
    loudness, own = 1.0, jax.random.fold_in(stream_key, 6)
    for dim, blocks in cuts:
        draws = jnp.exp(jax.random.uniform(jax.random.fold_in(own, dim), (blocks,), jnp.float32, low / len(cuts), top_value / len(cuts)))
        loudness = loudness * jnp.repeat(draws, shape[dim] // blocks).reshape([-1 if axis == dim else 1 for axis in range(len(shape))])
    return loudness


def gaussian(key, dims, spread, most, cuts=(), held_as=jnp.bfloat16):
    result = spread * jax.random.normal(key, dims, jnp.float32)
    if cuts:
        result = result * steps_of(key, dims, cuts, -0.22, 0.18)
    return jnp.clip(result, -most, most).astype(held_as)


def setup_inputs(seed: int = 0) -> dict:
    key_of = jax.random.split(jax.random.key(seed), 11)
    efield = gaussian(key_of[0], (3, NX, NY, NZ), 1.0, 6.0, ((1, 16), (2, 8), (3, 2)), jnp.float32)
    hfield = gaussian(key_of[1], (3, NX, NY, NZ), 1.0, 6.0, ((1, 16), (2, 8), (3, 2)), jnp.float32)
    inv_eps = jnp.clip(jnp.exp(math.log(1.0) - 1.89712 * jax.random.uniform(key_of[2], (NX, NY, NZ), jnp.float32) ** steps_of(key_of[2], (NX, NY, NZ), ((0, 16), (1, 8), (2, 2)), -0.2, 0.2)), 0.15, 1.0)
    gain_state = draw_gain_state(jax.random.fold_in(key_of[10], 71), 0)
    pump = jnp.clip(jnp.exp(math.log(0.3) - 3.4011974 * jax.random.uniform(key_of[4], (BRX, BRY, BRZ, SLOTS, BLOCK), jnp.float32) ** steps_of(key_of[4], (BRX, BRY, BRZ, SLOTS, BLOCK), ((0, 16), (1, 8), (2, 2)), -0.2, 0.2)), 0.01, 0.3)
    gain_offsets = draw_gain_offsets(jax.random.fold_in(key_of[10], 71), 0)
    gain_count = draw_gain_count(jax.random.fold_in(key_of[10], 71), 0)
    block_owner = jax.vmap(lambda own: jax.random.permutation(own, SLOTS))(jax.random.split(key_of[7], BRX * BRY * BRZ)).reshape((BRX, BRY, BRZ, SLOTS)).astype(jnp.int32)
    surf_offsets = draw_surf_offsets(jax.random.fold_in(key_of[10], 71), 0)
    far_acc = gaussian(key_of[9], (FREQ, 12, DIRS), 1.0, 6.0, ((0, 2),), jnp.float32)
    return dict(efield=efield, hfield=hfield, inv_eps=inv_eps, gain_state=gain_state, pump=pump, gain_offsets=gain_offsets, gain_count=gain_count, block_owner=block_owner, surf_offsets=surf_offsets, far_acc=far_acc)


time_step = 0.5
damping = 0.1
omega_rest = 1.0
coupling = 0.5
cross_rate = 0.3
upper_life = 2.0
lasing_life = 20.0
lower_life = 2.0
freq_low = 0.3
freq_pitch = 0.01
golden = 2.399963229728653

def bloch_update(state, drive, pump):
    polar = state[:, 0:3]
    rate = state[:, 3:6]
    ground = state[:, 6]
    lower = state[:, 7]
    lasing = state[:, 8]
    upper = state[:, 9]
    inversion = (lasing - lower)[:, None]
    half = 0.5 * damping * time_step
    rate_new = ((1.0 - half) * rate + time_step * (coupling * inversion * drive - omega_rest * omega_rest * polar)) / (1.0 + half)
    polar_new = polar + time_step * rate_new
    power = lax.optimization_barrier(jnp.sum(drive * rate_new, axis=1))
    upper_new = upper + time_step * (pump * ground - upper / upper_life)
    lasing_new = lasing + time_step * (upper / upper_life - lasing / lasing_life + cross_rate * power)
    lower_new = lower + time_step * (lasing / lasing_life - lower / lower_life - cross_rate * power)
    ground_new = ground + time_step * (lower / lower_life - pump * ground)
    levels = jnp.stack([ground_new, lower_new, lasing_new, upper_new], axis=1)
    return (jnp.concatenate([polar_new, rate_new, levels], axis=1), rate_new)

def directions(count):
    index = jnp.arange(count, dtype=jnp.float32)
    cosine = 1.0 - 2.0 * (index + 0.5) / count
    sine = jnp.sqrt(1.0 - cosine * cosine)
    azimuth = golden * index
    return (sine * jnp.cos(azimuth), sine * jnp.sin(azimuth), cosine)

def ahead(values, axis):
    widths = [(0, 0), (0, 0), (0, 0)]
    widths[axis] = (0, 1)
    return jnp.diff(jnp.pad(values, widths), axis=axis)

def behind(values, axis):
    widths = [(0, 0), (0, 0), (0, 0)]
    widths[axis] = (1, 0)
    return jnp.diff(jnp.pad(values, widths), axis=axis)

def curl(field, differ):
    first = differ(field[2], 1) - differ(field[1], 2)
    second = differ(field[0], 2) - differ(field[2], 0)
    third = differ(field[1], 0) - differ(field[0], 1)
    return jnp.stack([first, second, third])

def split_offsets(offsets, brick_x, brick_y, brick_z):
    cell_x = brick_x * CX + offsets // (CY * CZ)
    cell_y = brick_y * CY + offsets // CZ % CY
    cell_z = brick_z * CZ + offsets % CZ
    return (cell_x.astype(jnp.int32), cell_y.astype(jnp.int32), cell_z.astype(jnp.int32))

def reference(efield, hfield, inv_eps, gain_state, pump, gain_offsets, gain_count, block_owner, surf_offsets, far_acc):
    brick_x = jnp.arange(BRX, dtype=jnp.int32)[:, None, None, None]
    brick_y = jnp.arange(BRY, dtype=jnp.int32)[None, :, None, None]
    brick_z = jnp.arange(BRZ, dtype=jnp.int32)[None, None, :, None]
    flat_gain = gain_offsets.reshape(BRX, BRY, BRZ, SLOTS * BLOCK)
    cell_x, cell_y, cell_z = split_offsets(flat_gain, brick_x, brick_y, brick_z)
    gain_index = ((cell_x * NY + cell_y) * NZ + cell_z).reshape(-1).astype(jnp.int32)
    live = jnp.arange(SLOTS, dtype=jnp.int32)[None, None, None, :] < gain_count[..., None]
    live_mask = live.astype(jnp.float32).reshape(-1)[:, None, None]
    target = block_owner // CAP
    place = block_owner % CAP
    slot_index = (((target * BRY + brick_y) * BRZ + brick_z) * SLOTS + brick_x * CAP + place).reshape(-1).astype(jnp.int32)
    states = gain_state.reshape(-1, 10, BLOCK)
    pumps = pump.reshape(-1, BLOCK)
    surf_x, surf_y, surf_z = split_offsets(surf_offsets, brick_x, brick_y, brick_z)
    surf_index = ((surf_x * NY + surf_y) * NZ + surf_z).reshape(-1).astype(jnp.int32)
    pos_x = surf_x.reshape(-1).astype(jnp.float32) - 0.5 * (NX - 1)
    pos_y = surf_y.reshape(-1).astype(jnp.float32) - 0.5 * (NY - 1)
    pos_z = surf_z.reshape(-1).astype(jnp.float32) - 0.5 * (NZ - 1)
    omega = freq_low + freq_pitch * jnp.arange(FREQ, dtype=jnp.float32)
    total = pos_x.shape[0]
    spec_re = jnp.zeros((FREQ, 6, total), jnp.float32)
    spec_im = jnp.zeros((FREQ, 6, total), jnp.float32)
    for step in range(STEPS):
        hnew = hfield - time_step * curl(efield, ahead)
        samples = efield.reshape(3, -1)[:, gain_index].reshape(3, -1, BLOCK).transpose(1, 0, 2) * live_mask
        drive = jnp.zeros_like(samples).at[slot_index].set(samples)
        states, rate = bloch_update(states, drive, pumps)
        current = rate[slot_index] * live_mask
        source = jnp.zeros((3, NX * NY * NZ), jnp.float32).at[:, gain_index].add(current.transpose(1, 0, 2).reshape(3, -1))
        source = source.reshape(3, NX, NY, NZ)
        efield = efield + time_step * inv_eps[None] * (curl(hnew, behind) - source)
        hfield = hnew
        sampled = jnp.concatenate([efield, hfield], axis=0).reshape(6, -1)[:, surf_index]
        moment = omega * ((step + 1) * time_step)
        spec_re = spec_re + jnp.cos(moment)[:, None, None] * sampled[None]
        spec_im = spec_im - jnp.sin(moment)[:, None, None] * sampled[None]
    unit_x, unit_y, unit_z = directions(DIRS)
    along = pos_x[:, None] * unit_x[None] + pos_y[:, None] * unit_y[None] + pos_z[:, None] * unit_z[None]

    def one_frequency(pieces):
        part_re, part_im, freq = pieces
        table_re = jnp.cos(freq * along)
        table_im = jnp.sin(freq * along)
        high = lax.Precision.HIGHEST
        real = jnp.dot(part_re, table_re, precision=high) - jnp.dot(part_im, table_im, precision=high)
        imag = jnp.dot(part_re, table_im, precision=high) + jnp.dot(part_im, table_re, precision=high)
        return jnp.concatenate([real, imag], axis=0)
    terms = lax.map(one_frequency, (spec_re, spec_im, omega))
    scale = 1.0 / jnp.sqrt(jnp.float32(STEPS * SURF * BRX * BRY * BRZ))
    far_out = far_acc + scale * terms
    return (efield, hfield, states.reshape(BRX, BRY, BRZ, SLOTS, 10, BLOCK), far_out)
```

```python
import math

import jax
import jax.numpy as jnp
import numpy as np
from jax import lax
from jax.experimental import pallas as pl
from jax.experimental.pallas import tpu as pltpu
from jax.sharding import PartitionSpec as P

FREQ = 64
STEPS = 2
CX = 8
CY = 24
CZ = 128
ROWS = CX * CY
SLOTS = 32
DIRS = 128

time_step = 0.5
damping = 0.1
omega_rest = 1.0
coupling = 0.5
cross_rate = 0.3
upper_life = 2.0
lasing_life = 20.0
lower_life = 2.0
freq_low = 0.3
freq_pitch = 0.01
golden = 2.399963229728653

half = 0.5 * damping * time_step
keep_rate = (1.0 - half) / (1.0 + half)
spring = time_step * omega_rest * omega_rest / (1.0 + half)
gain_push = time_step * coupling / (1.0 + half)

F32 = jnp.float32
BF16 = jnp.bfloat16
MIB = 1 << 20


def shape(*dims, dtype=F32):
    return jax.ShapeDtypeStruct(dims, dtype)


def call(kernel, outs, args, in_specs=None, scratch=(), vmem=16, flops=0, moved=2 * MIB, name=None):
    return pl.pallas_call(
        kernel,
        out_shape=outs,
        in_specs=in_specs or [pl.BlockSpec(memory_space=pltpu.VMEM)] * len(args),
        scratch_shapes=scratch,
        compiler_params=pltpu.CompilerParams(vmem_limit_bytes=vmem * MIB),
        cost_estimate=pl.CostEstimate(flops=flops, bytes_accessed=moved, transcendentals=0),
        name=name,
    )(*args)


def split_parts(value):
    high = value.astype(BF16)
    low = (value - high.astype(F32)).astype(BF16)
    return high, low


def row_index(count, width):
    return lax.broadcasted_iota(jnp.int32, (count, width), 0)


def lane_index(count):
    return lax.broadcasted_iota(jnp.int32, (count, CZ), 1)


def ahead_x(field, face):
    return jnp.concatenate([field[CY:], face], axis=0)


def behind_x(field, face):
    return jnp.concatenate([face, field[:-CY]], axis=0)


def spread(face):
    return jnp.broadcast_to(face[:, None, :], (CX, CY, CZ)).reshape(ROWS, CZ)


def ahead_y(field, face, last):
    return jnp.where(last, spread(face), pltpu.roll(field, ROWS - 1, 0))


def behind_y(field, face, first):
    return jnp.where(first, spread(face), pltpu.roll(field, 1, 0))


def ahead_z(field, other, lane):
    return pltpu.roll(jnp.where(lane == 0, other, field), CZ - 1, 1)


def behind_z(field, other, lane):
    return pltpu.roll(jnp.where(lane == CZ - 1, other, field), 1, 1)


def row_in_brick():
    rows = row_index(ROWS, CZ)
    return rows - CY * ((rows * 2731) >> 16)


def first_layers(field_ref, out_x, out_y, out_z):
    out_x[0] = field_ref[1, 0:CY]
    out_x[1] = field_ref[2, 0:CY]
    for place, comp in ((0, 0), (1, 2)):
        for layer in range(CX):
            out_y[place, layer : layer + 1] = field_ref[comp, layer * CY : layer * CY + 1]
    if out_z is not None:
        out_z[0] = field_ref[0]
        out_z[1] = field_ref[1]


def last_layers(field_ref, out_x, out_y, out_z):
    out_x[0] = field_ref[1, ROWS - CY : ROWS]
    out_x[1] = field_ref[2, ROWS - CY : ROWS]
    for place, comp in ((0, 0), (1, 2)):
        for layer in range(CX):
            row = layer * CY + CY - 1
            out_y[place, layer : layer + 1] = field_ref[comp, row : row + 1]
    out_z[0] = field_ref[0]
    out_z[1] = field_ref[1]


def prepare_kernel(e_ref, state_ref, out_x, out_y, out_z, packed):
    first_layers(e_ref, out_x, out_y, out_z)
    lower = state_ref[:, 7]
    lasing = state_ref[:, 8]
    upper = state_ref[:, 9]
    for comp in range(3):
        polar = state_ref[:, comp]
        packed[:, comp] = keep_rate * state_ref[:, 3 + comp] - spring * polar
        packed[:, 3 + comp] = polar
    packed[:, 6] = lasing - lower
    lasing_free = lasing + time_step * (upper / upper_life - lasing / lasing_life)
    lower_free = lower + time_step * (lasing / lasing_life - lower / lower_life)
    packed[:, 7] = lasing_free - lower_free


def magnetic_kernel(e_ref, h_ref, face_x, face_y, face_z, h_out, out_x, out_y, out_z):
    lane = lane_index(ROWS)
    last = row_in_brick() == CY - 1
    ex, ey, ez = e_ref[0], e_ref[1], e_ref[2]
    first = (ahead_y(ez, face_y[1], last) - ez) - (ahead_z(ey, face_z[1], lane) - ey)
    second = (ahead_z(ex, face_z[0], lane) - ex) - (ahead_x(ez, face_x[1]) - ez)
    third = (ahead_x(ey, face_x[0]) - ey) - (ahead_y(ex, face_y[0], last) - ex)
    h_out[0] = h_ref[0] - time_step * first
    h_out[1] = h_ref[1] - time_step * second
    h_out[2] = h_ref[2] - time_step * third
    last_layers(h_out, out_x, out_y, out_z)


def electric_curl(h_ref, face_x, face_y, face_z):
    lane = lane_index(ROWS)
    start = row_in_brick() == 0
    hx, hy, hz = h_ref[0], h_ref[1], h_ref[2]
    first = (hz - behind_y(hz, face_y[1], start)) - (hy - behind_z(hy, face_z[1], lane))
    second = (hx - behind_z(hx, face_z[0], lane)) - (hz - behind_x(hz, face_x[1]))
    third = (hy - behind_x(hy, face_x[0])) - (hx - behind_y(hx, face_y[0], start))
    return first, second, third


def row_hits(offsets, width):
    return (row_index(ROWS, width) == (offsets >> 7)).astype(F32).astype(BF16)


def lane_hits(offsets, width):
    return row_index(CZ, width) == (offsets & (CZ - 1))


def scatter_kernel(count_ref, owner_ref, offsets_ref, fields_ref, dense, placed, total):
    count = count_ref[0]
    for slot in range(SLOTS):
        line = offsets_ref[slot : slot + 1]
        placed[pl.ds(owner_ref[slot], 1)] = jnp.where(slot < count, line, -1)
    total[...] = jnp.zeros_like(total)

    def pair(index, carry):
        lines = placed[pl.ds(2 * index, 2)]
        offsets = jnp.concatenate([lines[0:1], lines[1:2]], axis=1)
        rows = row_hits(offsets, 2 * CZ)
        lanes = lane_hits(offsets, 2 * CZ)
        values = jnp.concatenate([fields_ref[2 * index], fields_ref[2 * index + 1]], axis=1)
        for part in split_parts(values):
            part = part.astype(F32)
            spots = jnp.concatenate(
                [
                    jnp.where(lanes, part[field : field + 1], 0.0).astype(BF16)
                    for field in range(8)
                ],
                axis=0,
            )
            total[...] += lax.dot_general(
                rows, spots, (((1,), (1,)), ((), ())), preferred_element_type=F32
            )
        return carry

    lax.fori_loop(0, SLOTS // 2, pair, 0)
    for field in range(8):
        dense[field] = total[:, field * CZ : (field + 1) * CZ]


def electric_kernel(
    e_ref, h_ref, face_x, face_y, face_z, eps_ref, dense, e_out, out_x, out_y, out_z, source_out
):
    curls = electric_curl(h_ref, face_x, face_y, face_z)
    scaled = time_step * eps_ref[...]
    inversion = dense[6]
    power = jnp.zeros_like(inversion)
    rates = []
    for comp in range(3):
        field = e_ref[comp]
        rate = dense[comp] + gain_push * inversion * field
        power = power + field * rate
        rates.append(rate)
        e_out[comp] = field + scaled * (curls[comp] - rate)
    later = dense[7] + (2.0 * time_step * cross_rate) * power
    for comp in range(3):
        polar = dense[3 + comp] + time_step * rates[comp]
        free = keep_rate * rates[comp] - spring * polar
        source_out[comp] = free + gain_push * later * e_out[comp]
    first_layers(e_out, out_x, out_y, out_z)


def gather_lines(high, low, offsets, width, fields):
    rows = row_hits(offsets, width)
    lanes = lane_hits(offsets, width)
    picked = jnp.dot(high, rows, preferred_element_type=F32)
    picked = picked + jnp.dot(low, rows, preferred_element_type=F32)
    return [
        jnp.sum(jnp.where(lanes, picked[field * CZ : (field + 1) * CZ], 0.0), axis=0, keepdims=True)
        for field in range(fields)
    ]


def turned(fields):
    return split_parts(jnp.concatenate([jnp.transpose(field) for field in fields], axis=0))


def drive_kernel(e_old, e_new, h_new, placed, surf_ref, drives, sampled):
    high, low = turned([e_old[c] for c in range(3)] + [e_new[c] for c in range(3)])
    drives[...] = jnp.zeros_like(drives)

    def pair(index, carry):
        lines = placed[pl.ds(2 * index, 2)]
        offsets = jnp.concatenate([lines[0:1], lines[1:2]], axis=1)
        got = gather_lines(high, low, offsets, 2 * CZ, 6)
        for field in range(6):
            drives[2 * index, field : field + 1] = got[field][:, :CZ]
            drives[2 * index + 1, field : field + 1] = got[field][:, CZ:]
        return carry

    lax.fori_loop(0, SLOTS // 2, pair, 0)
    sample_rows(e_new, h_new, surf_ref, sampled)


def sample_rows(e_ref, h_ref, surf_ref, sampled):
    high, low = turned([e_ref[c] for c in range(3)] + [h_ref[c] for c in range(3)])
    got = gather_lines(high, low, surf_ref[...], CZ, 6)
    sampled[...] = jnp.zeros_like(sampled)
    for field in range(6):
        sampled[field : field + 1] = got[field]


def table_kernel(surf_ref, units_ref, table):
    cells = surf_ref[...]
    rows = cells >> 7
    layer = (rows * 2731) >> 16
    cell_x = lax.axis_index("gx") * CX + layer
    cell_y = lax.axis_index("gy") * CY + (rows - CY * layer)
    cell_z = lax.axis_index("gz") * CZ + (cells & (CZ - 1))
    along = jnp.zeros((CZ, DIRS), F32)
    for axis, (cell, size) in enumerate(((cell_x, 128), (cell_y, 192), (cell_z, 256))):
        place = cell.astype(F32) - 0.5 * (size - 1)
        column = jnp.transpose(jnp.broadcast_to(place, (CZ, CZ)))
        along = along + column * units_ref[axis : axis + 1]
    tall = 32
    for block in range(CZ // tall):
        part = along[block * tall : (block + 1) * tall]
        turn_re = jnp.cos(freq_pitch * part)
        turn_im = jnp.sin(freq_pitch * part)
        now_re = jnp.cos(freq_low * part)
        now_im = jnp.sin(freq_low * part)

        def step(freq, now, block=block, turn_re=turn_re, turn_im=turn_im):
            now_re, now_im = now
            for place, value in ((0, now_re), (1, now_im)):
                high, low = split_parts(value)
                across = pl.ds(place * DIRS, DIRS)
                table[freq, pl.ds(block * tall, tall), across] = high
                table[freq, pl.ds(CZ + block * tall, tall), across] = low
            return (
                now_re * turn_re - now_im * turn_im,
                now_im * turn_re + now_re * turn_im,
            )

        lax.fori_loop(0, FREQ, step, (now_re, now_im))


def final_kernel(
    e_ref,
    h_ref,
    face_x,
    face_y,
    face_z,
    eps_ref,
    source,
    surf_ref,
    early_ref,
    table,
    e_out,
    keep_out,
    send_out,
    late,
):
    curls = electric_curl(h_ref, face_x, face_y, face_z)
    scaled = time_step * eps_ref[...]
    for comp in range(3):
        e_out[comp] = e_ref[comp] + scaled * (curls[comp] - source[comp])
    sample_rows(e_out, h_ref, surf_ref, late)
    high, low = split_parts(jnp.concatenate([early_ref[...], late[...]], axis=0))
    left = jnp.concatenate(
        [
            jnp.concatenate([high, high], axis=1),
            jnp.concatenate([low, jnp.zeros_like(low)], axis=1),
        ],
        axis=0,
    )
    own = lax.axis_index("gz")
    scale = 1.0 / math.sqrt(STEPS * CZ * 256)
    for freq in range(FREQ // 2):
        for side, out in ((0, keep_out), (1, send_out)):
            target = lax.rem(own + side, 2)
            omega = freq_low + freq_pitch * (target * (FREQ // 2) + freq).astype(F32)
            both = jnp.dot(
                left, table[target * (FREQ // 2) + freq], preferred_element_type=F32
            )
            both = both[0:16] + both[16:32]
            real = jnp.zeros((8, DIRS), F32)
            imag = jnp.zeros((8, DIRS), F32)
            for step in range(STEPS):
                moment = jnp.full((8, DIRS), (step + 1) * time_step, F32) * omega
                cosine = jnp.cos(moment)
                sine = jnp.sin(moment)
                upper = both[8 * step : 8 * step + 8, 0:DIRS]
                under = both[8 * step : 8 * step + 8, DIRS:]
                real = real + cosine * upper + sine * under
                imag = imag + cosine * under - sine * upper
            out[freq, 0:8] = scale * real
            out[freq, 8:16] = scale * imag


def atoms_kernel(state_ref, pump_ref, drives, out):
    polar = [state_ref[:, c] for c in range(3)]
    rate = [state_ref[:, 3 + c] for c in range(3)]
    ground, lower, lasing, upper = [state_ref[:, 6 + level] for level in range(4)]
    pump = pump_ref[...]
    for step in range(STEPS):
        drive = [drives[:, 3 * step + c] for c in range(3)]
        inversion = lasing - lower
        power = jnp.zeros_like(pump)
        for c in range(3):
            rate[c] = (
                (1.0 - half) * rate[c]
                + time_step
                * (coupling * inversion * drive[c] - omega_rest * omega_rest * polar[c])
            ) / (1.0 + half)
            polar[c] = polar[c] + time_step * rate[c]
            power = power + drive[c] * rate[c]
        upper_new = upper + time_step * (pump * ground - upper / upper_life)
        lasing_new = lasing + time_step * (
            upper / upper_life - lasing / lasing_life + cross_rate * power
        )
        lower_new = lower + time_step * (
            lasing / lasing_life - lower / lower_life - cross_rate * power
        )
        ground = ground + time_step * (lower / lower_life - pump * ground)
        lower, lasing, upper = lower_new, lasing_new, upper_new
    for place, value in enumerate(polar + rate + [ground, lower, lasing, upper]):
        out[:, place] = value


def directions(count):
    index = np.arange(count, dtype=np.float32)
    cosine = np.float32(1.0) - np.float32(2.0) * (index + np.float32(0.5)) / np.float32(count)
    sine = np.sqrt(np.float32(1.0) - cosine * cosine)
    azimuth = (np.float32(golden) * index).astype(np.float64)
    rows = np.zeros((8, count), np.float32)
    rows[0] = sine * np.cos(azimuth).astype(np.float32)
    rows[1] = sine * np.sin(azimuth).astype(np.float32)
    rows[2] = cosine
    return rows


def all_reduce(value, axis, peers):
    one, two, three = [lax.ppermute(value, axis, peers(k)) for k in (1, 2, 3)]
    return (value + one) + (two + three)


def local(
    efield,
    hfield,
    inv_eps,
    gain_state,
    pump,
    gain_offsets,
    gain_count,
    block_owner,
    surf_offsets,
    far_acc,
):
    e_old = efield.reshape(3, ROWS, CZ)
    h_old = hfield.reshape(3, ROWS, CZ)
    eps = inv_eps.reshape(ROWS, CZ)
    state = gain_state.reshape(SLOTS, 10, CZ)
    surf = surf_offsets.reshape(1, CZ)
    faces = (shape(2, CY, CZ), shape(2, CX, CZ), shape(2, ROWS, CZ))
    dense = shape(3, ROWS, CZ)
    down = [[(i + 1, i) for i in range(n - 1)] for n in (16, 8, 2)]
    up = [[(i, i + 1) for i in range(n - 1)] for n in (16, 8, 2)]

    def shifted(parts, perms):
        return [
            lax.ppermute(part, axis, perm)
            for part, axis, perm in zip(parts, ("gx", "gy", "gz"), perms)
        ]

    def whole(count):
        return [pl.BlockSpec(memory_space=pltpu.VMEM)] * count

    scalars = [pl.BlockSpec(memory_space=pltpu.SMEM)]

    *near, packed = call(
        prepare_kernel, faces + (shape(SLOTS, 8, CZ),), (e_old, state), name="prepare"
    )
    near = shifted(near, down)
    fields = lax.all_to_all(packed, "gx", 0, 0, tiled=True)
    h_one, *edge = call(magnetic_kernel, (dense,) + faces, (e_old, h_old, *near), name="magnetic")
    edge = shifted(edge, up)
    spread_fields, placed = call(
        scatter_kernel,
        (shape(8, ROWS, CZ), shape(SLOTS, CZ, dtype=jnp.int32)),
        (
            gain_count.reshape(1),
            block_owner.reshape(SLOTS),
            gain_offsets.reshape(SLOTS, CZ),
            fields,
        ),
        in_specs=scalars * 2 + whole(2),
        scratch=[pltpu.VMEM((ROWS, 8 * CZ), F32)],
        flops=4 * 10**9,
        name="scatter",
    )
    e_one, *near_rest = call(
        electric_kernel,
        (dense,) + faces + (dense,),
        (e_old, h_one, *edge, eps, spread_fields),
        name="electric",
    )
    *near, source = near_rest
    near = shifted(near, down)
    drives, early = call(
        drive_kernel,
        (shape(SLOTS, 8, CZ), shape(8, CZ)),
        (e_old, e_one, h_one, placed, surf),
        flops=4 * 10**9,
        name="drive",
    )
    h_two, *edge = call(magnetic_kernel, (dense,) + faces, (e_one, h_one, *near), name="magnetic2")
    edge = shifted(edge, up)
    table = call(
        table_kernel,
        shape(FREQ, 2 * CZ, 2 * DIRS, dtype=BF16),
        (surf, jnp.asarray(directions(DIRS))),
        flops=4 * 10**9,
        vmem=24,
        moved=8 * MIB,
        name="table",
    )
    part = shape(FREQ // 2, 16, DIRS)
    e_two, keep, send = call(
        final_kernel,
        (dense, part, part),
        (e_one, h_two, *edge, eps, source, surf, early, table),
        scratch=[pltpu.VMEM((8, CZ), F32)],
        vmem=28,
        flops=4 * 10**9,
        moved=10 * MIB,
        name="final",
    )
    back = lax.all_to_all(drives, "gx", 0, 0, tiled=True)
    state_out = call(
        atoms_kernel, shape(SLOTS, 10, CZ), (state, pump.reshape(SLOTS, CZ), back), name="atoms"
    )
    chip = keep + lax.ppermute(send, "gz", [(0, 1), (1, 0)])
    pieces = lax.all_to_all(chip.reshape(8, 4, 16, DIRS), "gy", 0, 0, tiled=True)
    total = jnp.sum(pieces, axis=0)
    total = all_reduce(
        total, "gx", lambda k: [(a * 4 + z, (a ^ k) * 4 + z) for a in range(4) for z in range(4)]
    )
    total = all_reduce(
        total, "gx", lambda k: [(a * 4 + z, a * 4 + (z ^ k)) for a in range(4) for z in range(4)]
    )
    gathered = lax.all_to_all(
        jnp.broadcast_to(total[None], (8, 4, 16, DIRS)), "gy", 0, 0, tiled=True
    ).reshape(FREQ // 2, 16, DIRS)
    far_out = far_acc + jnp.concatenate([gathered[:, 0:6], gathered[:, 8:14]], axis=1)
    return (
        e_two.reshape(efield.shape),
        h_two.reshape(hfield.shape),
        state_out.reshape(gain_state.shape),
        far_out,
    )


def solution(mesh):
    placed = (
        P(None, "gx", "gy", "gz"),
        P(None, "gx", "gy", "gz"),
        P("gx", "gy", "gz"),
        P("gx", "gy", "gz", None, None, None),
        P("gx", "gy", "gz", None, None),
        P("gx", "gy", "gz", None, None),
        P("gx", "gy", "gz"),
        P("gx", "gy", "gz", None),
        P("gx", "gy", "gz", None),
        P("gz", None, None),
    )
    return jax.shard_map(
        local,
        mesh=mesh,
        in_specs=placed,
        out_specs=(
            P(None, "gx", "gy", "gz"),
            P(None, "gx", "gy", "gz"),
            P("gx", "gy", "gz", None, None, None),
            P("gz", None, None),
        ),
        check_vma=False,
    )
```

```python
import math

import jax
import jax.numpy as jnp
import numpy as np
from jax import lax
from jax.experimental import pallas as pl
from jax.experimental.pallas import tpu as pltpu
from jax.sharding import PartitionSpec as P

FREQ = 64
STEPS = 2
CX = 8
CY = 24
CZ = 128
ROWS = CX * CY
SLOTS = 32
DIRS = 128

time_step = 0.5
damping = 0.1
omega_rest = 1.0
coupling = 0.5
cross_rate = 0.3
upper_life = 2.0
lasing_life = 20.0
lower_life = 2.0
freq_low = 0.3
freq_pitch = 0.01
golden = 2.399963229728653

half = 0.5 * damping * time_step
keep_rate = (1.0 - half) / (1.0 + half)
spring = time_step * omega_rest * omega_rest / (1.0 + half)
gain_push = time_step * coupling / (1.0 + half)

F32 = jnp.float32
BF16 = jnp.bfloat16
MIB = 1 << 20


def shape(*dims, dtype=F32):
    return jax.ShapeDtypeStruct(dims, dtype)


def call(kernel, outs, args, in_specs=None, scratch=(), vmem=16, flops=0, moved=2 * MIB, name=None):
    return pl.pallas_call(
        kernel,
        out_shape=outs,
        in_specs=in_specs or [pl.BlockSpec(memory_space=pltpu.VMEM)] * len(args),
        scratch_shapes=scratch,
        compiler_params=pltpu.CompilerParams(vmem_limit_bytes=vmem * MIB),
        cost_estimate=pl.CostEstimate(flops=flops, bytes_accessed=moved, transcendentals=0),
        name=name,
    )(*args)


def stay(*values):
    return [pltpu.with_memory_space_constraint(value, pltpu.HBM) for value in values]


def split_parts(value):
    high = value.astype(BF16)
    low = (value - high.astype(F32)).astype(BF16)
    return high, low


def row_index(count, width):
    return lax.broadcasted_iota(jnp.int32, (count, width), 0)


def lane_index(count):
    return lax.broadcasted_iota(jnp.int32, (count, CZ), 1)


def ahead_x(field, face):
    return jnp.concatenate([field[CY:], face], axis=0)


def behind_x(field, face):
    return jnp.concatenate([face, field[:-CY]], axis=0)


def spread(face):
    return jnp.broadcast_to(face[:, None, :], (CX, CY, CZ)).reshape(ROWS, CZ)


def ahead_y(field, face, last):
    return jnp.where(last, spread(face), pltpu.roll(field, ROWS - 1, 0))


def behind_y(field, face, first):
    return jnp.where(first, spread(face), pltpu.roll(field, 1, 0))


def ahead_z(field, other, lane):
    return pltpu.roll(jnp.where(lane == 0, other, field), CZ - 1, 1)


def behind_z(field, other, lane):
    return pltpu.roll(jnp.where(lane == CZ - 1, other, field), 1, 1)


def row_in_brick():
    rows = row_index(ROWS, CZ)
    return rows - CY * ((rows * 2731) >> 16)


def first_layers(field_ref, out_x, out_y, out_z):
    out_x[0] = field_ref[1, 0:CY]
    out_x[1] = field_ref[2, 0:CY]
    for place, comp in ((0, 0), (1, 2)):
        for layer in range(CX):
            out_y[place, layer : layer + 1] = field_ref[comp, layer * CY : layer * CY + 1]
    out_z[0] = field_ref[0]
    out_z[1] = field_ref[1]


def last_layers(field_ref, out_x, out_y, out_z):
    out_x[0] = field_ref[1, ROWS - CY : ROWS]
    out_x[1] = field_ref[2, ROWS - CY : ROWS]
    for place, comp in ((0, 0), (1, 2)):
        for layer in range(CX):
            row = layer * CY + CY - 1
            out_y[place, layer : layer + 1] = field_ref[comp, row : row + 1]
    out_z[0] = field_ref[0]
    out_z[1] = field_ref[1]


def inside(faces, ahead):
    kept = []
    for face, axis in zip(faces, ("gx", "gy", "gz")):
        index = lax.axis_index(axis)
        real = index < lax.axis_size(axis) - 1 if ahead else index > 0
        kept.append([jnp.where(real, face[place], 0.0) for place in range(2)])
    return kept


def prepare_kernel(
    e_hbm, state_hbm, h_hbm, eps_hbm, out_x, out_y, out_z, packed, e_out, h_out, eps_out, state, sems
):
    copies = [
        pltpu.make_async_copy(source, target, sems.at[place])
        for place, (source, target) in enumerate(
            ((e_hbm, e_out), (state_hbm, state), (h_hbm, h_out), (eps_hbm, eps_out))
        )
    ]
    for copy in copies:
        copy.start()
    copies[0].wait()
    first_layers(e_out, out_x, out_y, out_z)
    copies[1].wait()
    lower, lasing, upper = state[7], state[8], state[9]
    for comp in range(3):
        polar = state[comp]
        packed[:, comp] = keep_rate * state[3 + comp] - spring * polar
        packed[:, 3 + comp] = polar
    packed[:, 6] = lasing - lower
    lasing_free = lasing + time_step * (upper / upper_life - lasing / lasing_life)
    lower_free = lower + time_step * (lasing / lasing_life - lower / lower_life)
    packed[:, 7] = lasing_free - lower_free
    copies[2].wait()
    copies[3].wait()


def magnetic_kernel(e_ref, h_ref, face_x, face_y, face_z, h_out, out_x, out_y, out_z):
    lane = lane_index(ROWS)
    last = row_in_brick() == CY - 1
    face_x, face_y, face_z = inside((face_x, face_y, face_z), True)
    ex, ey, ez = e_ref[0], e_ref[1], e_ref[2]
    first = (ahead_y(ez, face_y[1], last) - ez) - (ahead_z(ey, face_z[1], lane) - ey)
    second = (ahead_z(ex, face_z[0], lane) - ex) - (ahead_x(ez, face_x[1]) - ez)
    third = (ahead_x(ey, face_x[0]) - ey) - (ahead_y(ex, face_y[0], last) - ex)
    h_out[0] = h_ref[0] - time_step * first
    h_out[1] = h_ref[1] - time_step * second
    h_out[2] = h_ref[2] - time_step * third
    last_layers(h_out, out_x, out_y, out_z)


def electric_curl(h_ref, face_x, face_y, face_z):
    lane = lane_index(ROWS)
    start = row_in_brick() == 0
    face_x, face_y, face_z = inside((face_x, face_y, face_z), False)
    hx, hy, hz = h_ref[0], h_ref[1], h_ref[2]
    first = (hz - behind_y(hz, face_y[1], start)) - (hy - behind_z(hy, face_z[1], lane))
    second = (hx - behind_z(hx, face_z[0], lane)) - (hz - behind_x(hz, face_x[1]))
    third = (hy - behind_x(hy, face_x[0])) - (hx - behind_y(hx, face_y[0], start))
    return first, second, third


def row_hits(offsets, width):
    return row_index(ROWS, width) == (offsets >> 7)


def lane_hits(offsets, width):
    hits = row_index(CZ, width) == (offsets & (CZ - 1))
    return hits.astype(F32).astype(BF16)


GROUP = 4


def scatter_kernel(placed, fields_ref, dense, total, spots, rows):
    total[...] = jnp.zeros_like(total)

    def group(index, carry):
        lines = placed[pl.ds(GROUP * index, GROUP)]
        for slot in range(GROUP):
            line = lines[slot : slot + 1]
            hits = row_hits(line, CZ).astype(F32).astype(BF16)
            lanes = lane_hits(line, CZ).reshape(8, 16, CZ)
            for place, part in enumerate(split_parts(fields_ref[GROUP * index + slot])):
                across = (place * GROUP + slot) * CZ
                rows[:, across : across + CZ] = hits
                part = part.astype(F32)
                for field in range(8):
                    line = jnp.broadcast_to(part[field : field + 1], (16, CZ)).astype(BF16)
                    spots[field * CZ : (field + 1) * CZ, across : across + CZ] = (
                        lanes * line[None]
                    ).reshape(CZ, CZ)
        total[...] += lax.dot_general(
            spots[...], rows[...], (((1,), (1,)), ((), ())), preferred_element_type=F32
        )
        return carry

    lax.fori_loop(0, SLOTS // GROUP, group, 0)
    for field in range(8):
        dense[field] = jnp.transpose(total[field * CZ : (field + 1) * CZ])


def electric_kernel(
    e_ref, h_ref, face_x, face_y, face_z, eps_ref, dense, e_out, out_x, out_y, out_z, source_out
):
    curls = electric_curl(h_ref, face_x, face_y, face_z)
    scaled = time_step * eps_ref[...]
    inversion = dense[6]
    power = jnp.zeros_like(inversion)
    rates = []
    for comp in range(3):
        field = e_ref[comp]
        rate = dense[comp] + gain_push * inversion * field
        power = power + field * rate
        rates.append(rate)
        e_out[comp] = field + scaled * (curls[comp] - rate)
    later = dense[7] + (2.0 * time_step * cross_rate) * power
    for comp in range(3):
        polar = dense[3 + comp] + time_step * rates[comp]
        free = keep_rate * rates[comp] - spring * polar
        source_out[comp] = free + gain_push * later * e_out[comp]
    first_layers(e_out, out_x, out_y, out_z)


def stacked(fields):
    high, low = split_parts(jnp.concatenate(fields, axis=0))
    return jnp.concatenate([high, low], axis=1)


def gather_lines(values, offsets, width):
    lanes = lane_hits(offsets, width)
    rows = row_hits(offsets, width)
    picked = jnp.dot(
        values, jnp.concatenate([lanes, lanes], axis=0), preferred_element_type=F32
    )
    return [
        jnp.sum(
            jnp.where(rows, picked[field * ROWS : (field + 1) * ROWS], 0.0), axis=0, keepdims=True
        )
        for field in range(6)
    ]


def drive_kernel(e_old, e_new, h_new, placed, surf_ref, drives, sampled, values):
    values[...] = stacked([e_old[c] for c in range(3)] + [e_new[c] for c in range(3)])
    drives[...] = jnp.zeros_like(drives)

    def pair(index, carry):
        lines = placed[pl.ds(2 * index, 2)]
        offsets = jnp.concatenate([lines[0:1], lines[1:2]], axis=1)
        got = gather_lines(values[...], offsets, 2 * CZ)
        for field in range(6):
            drives[2 * index, field : field + 1] = got[field][:, :CZ]
            drives[2 * index + 1, field : field + 1] = got[field][:, CZ:]
        return carry

    lax.fori_loop(0, SLOTS // 2, pair, 0)
    sample_rows(e_new, h_new, surf_ref, sampled)


def sample_rows(e_ref, h_ref, surf_ref, sampled):
    values = stacked([e_ref[c] for c in range(3)] + [h_ref[c] for c in range(3)])
    got = gather_lines(values, surf_ref[...], CZ)
    sampled[...] = jnp.zeros_like(sampled)
    for field in range(6):
        sampled[field : field + 1] = got[field]


def table_kernel(
    count_ref,
    owner_hbm,
    offsets_ref,
    surf_ref,
    units_ref,
    table,
    factors,
    placed,
    surf_out,
    owner_ref,
    sem,
):
    copy = pltpu.make_async_copy(owner_hbm, owner_ref, sem)
    copy.start()
    copy.wait()
    count = count_ref[0]
    for slot in range(SLOTS):
        line = offsets_ref[slot : slot + 1]
        placed[pl.ds(owner_ref[0, slot], 1)] = jnp.where(slot < count, line, -1)
    omega = freq_low + freq_pitch * row_index(FREQ, DIRS).astype(F32)
    for step in range(STEPS):
        moment = omega * ((step + 1) * time_step)
        factors[2 * step] = jnp.cos(moment)
        factors[2 * step + 1] = jnp.sin(moment)
    cells = surf_ref[...]
    surf_out[...] = cells
    rows = cells >> 7
    layer = (rows * 2731) >> 16
    cell_x = lax.axis_index("gx") * CX + layer
    cell_y = lax.axis_index("gy") * CY + (rows - CY * layer)
    cell_z = lax.axis_index("gz") * CZ + (cells & (CZ - 1))
    along = jnp.zeros((CZ, DIRS), F32)
    for axis, (cell, size) in enumerate(((cell_x, 128), (cell_y, 192), (cell_z, 256))):
        place = cell.astype(F32) - 0.5 * (size - 1)
        column = jnp.transpose(jnp.broadcast_to(place, (CZ, CZ)))
        along = along + column * units_ref[axis : axis + 1]
    tall = 32
    for block in range(CZ // tall):
        part = along[block * tall : (block + 1) * tall]
        turn_re = jnp.cos(freq_pitch * part)
        turn_im = jnp.sin(freq_pitch * part)
        now_re = jnp.cos(freq_low * part)
        now_im = jnp.sin(freq_low * part)

        def step(freq, now, block=block, turn_re=turn_re, turn_im=turn_im):
            now_re, now_im = now
            for place, value in ((0, now_re), (1, now_im)):
                high, low = split_parts(value)
                across = pl.ds(place * DIRS, DIRS)
                table[freq, pl.ds(block * tall, tall), across] = high
                table[freq, pl.ds(CZ + block * tall, tall), across] = low
            return (
                now_re * turn_re - now_im * turn_im,
                now_im * turn_re + now_re * turn_im,
            )

        lax.fori_loop(0, FREQ, step, (now_re, now_im))


def final_kernel(
    e_ref,
    h_ref,
    face_x,
    face_y,
    face_z,
    eps_ref,
    source,
    surf_ref,
    early_ref,
    table,
    factors,
    e_out,
    keep_out,
    send_out,
    late,
):
    curls = electric_curl(h_ref, face_x, face_y, face_z)
    scaled = time_step * eps_ref[...]
    for comp in range(3):
        e_out[comp] = e_ref[comp] + scaled * (curls[comp] - source[comp])
    sample_rows(e_out, h_ref, surf_ref, late)
    scale = 1.0 / math.sqrt(STEPS * CZ * 256)
    high, low = split_parts(scale * jnp.concatenate([early_ref[...], late[...]], axis=0))
    left = jnp.concatenate(
        [
            jnp.concatenate([high, high], axis=1),
            jnp.concatenate([low, jnp.zeros_like(low)], axis=1),
        ],
        axis=0,
    )
    own = lax.axis_index("gz")
    for side, out in ((1, send_out), (0, keep_out)):
        base = lax.rem(own + side, 2) * (FREQ // 2)
        for freq in range(FREQ // 2):
            both = jnp.dot(left, table[base + freq], preferred_element_type=F32)
            both = both[0:16] + both[16:32]
            real = jnp.zeros((8, DIRS), F32)
            imag = jnp.zeros((8, DIRS), F32)
            for step in range(STEPS):
                cosine = factors[2 * step, pl.ds(base + freq, 1)]
                sine = factors[2 * step + 1, pl.ds(base + freq, 1)]
                upper = both[8 * step : 8 * step + 8, 0:DIRS]
                under = both[8 * step : 8 * step + 8, DIRS:]
                real = real + (cosine * upper + sine * under)
                imag = imag + (cosine * under - sine * upper)
            for comp in range(6):
                row = comp * (FREQ // 2) + freq
                out[row : row + 1] = real[comp : comp + 1]
                row = (comp + 6) * (FREQ // 2) + freq
                out[row : row + 1] = imag[comp : comp + 1]


def atoms_kernel(state_ref, pump_ref, drives, e_ref, h_ref, out, e_out, h_out):
    polar = [state_ref[c] for c in range(3)]
    rate = [state_ref[3 + c] for c in range(3)]
    ground, lower, lasing, upper = [state_ref[6 + level] for level in range(4)]
    pump = pump_ref[...]
    for step in range(STEPS):
        drive = [drives[:, 3 * step + c] for c in range(3)]
        inversion = lasing - lower
        power = jnp.zeros_like(pump)
        for c in range(3):
            rate[c] = (
                (1.0 - half) * rate[c]
                + time_step
                * (coupling * inversion * drive[c] - omega_rest * omega_rest * polar[c])
            ) / (1.0 + half)
            polar[c] = polar[c] + time_step * rate[c]
            power = power + drive[c] * rate[c]
        upper_new = upper + time_step * (pump * ground - upper / upper_life)
        lasing_new = lasing + time_step * (
            upper / upper_life - lasing / lasing_life + cross_rate * power
        )
        lower_new = lower + time_step * (
            lasing / lasing_life - lower / lower_life - cross_rate * power
        )
        ground = ground + time_step * (lower / lower_life - pump * ground)
        lower, lasing, upper = lower_new, lasing_new, upper_new
    for place, value in enumerate(polar + rate + [ground, lower, lasing, upper]):
        out[place] = value
    e_out[...] = e_ref[...]
    h_out[...] = h_ref[...]


def directions(count):
    index = np.arange(count, dtype=np.float32)
    cosine = np.float32(1.0) - np.float32(2.0) * (index + np.float32(0.5)) / np.float32(count)
    sine = np.sqrt(np.float32(1.0) - cosine * cosine)
    azimuth = (np.float32(golden) * index).astype(np.float64)
    rows = np.zeros((8, count), np.float32)
    rows[0] = sine * np.cos(azimuth).astype(np.float32)
    rows[1] = sine * np.sin(azimuth).astype(np.float32)
    rows[2] = cosine
    return rows


def all_reduce(value, axis, peers):
    one, two, three = [lax.ppermute(value, axis, peers(k)) for k in (1, 2, 3)]
    return (value + one) + (two + three)


def local(
    efield,
    hfield,
    inv_eps,
    gain_state,
    pump,
    gain_offsets,
    gain_count,
    block_owner,
    surf_offsets,
    far_acc,
):
    state = jnp.transpose(gain_state.reshape(SLOTS, 10, CZ), (1, 0, 2))
    dense = shape(3, ROWS, CZ)
    faces = (shape(2, CY, CZ), shape(2, CX, CZ), shape(2, ROWS, CZ))
    down = [[((i + 1) % n, i) for i in range(n)] for n in (16, 8, 2)]
    up = [[(i, (i + 1) % n) for i in range(n)] for n in (16, 8, 2)]
    vmem = pl.BlockSpec(memory_space=pltpu.VMEM)

    hbm = pl.BlockSpec(memory_space=pltpu.HBM)

    def shifted(parts, perms):
        return [
            lax.ppermute(part, axis, perm)
            for part, axis, perm in zip(parts, ("gx", "gy", "gz"), perms)
        ]

    *near, packed, e_old, h_old, eps = call(
        prepare_kernel,
        faces + (shape(SLOTS, 8, CZ), dense, dense, shape(ROWS, CZ)),
        stay(
            efield.reshape(3, ROWS, CZ),
            state,
            hfield.reshape(3, ROWS, CZ),
            inv_eps.reshape(ROWS, CZ),
        ),
        in_specs=[hbm] * 4,
        scratch=[pltpu.VMEM((10, SLOTS, CZ), F32), pltpu.SemaphoreType.DMA((4,))],
        name="prepare",
    )
    near = shifted(near, down)
    fields = lax.all_to_all(packed, "gx", 0, 0, tiled=True)
    table, factors, placed, surf = call(
        table_kernel,
        (
            shape(FREQ, 2 * CZ, 2 * DIRS, dtype=BF16),
            shape(2 * STEPS, FREQ, DIRS),
            shape(SLOTS, CZ, dtype=jnp.int32),
            shape(1, CZ, dtype=jnp.int32),
        ),
        [gain_count.reshape(1)]
        + stay(
            block_owner.reshape(1, SLOTS),
            gain_offsets.reshape(SLOTS, CZ),
            surf_offsets.reshape(1, CZ),
            jnp.asarray(directions(DIRS)),
        ),
        in_specs=[pl.BlockSpec(memory_space=pltpu.SMEM), hbm, vmem, vmem, vmem],
        scratch=[pltpu.SMEM((1, SLOTS), jnp.int32), pltpu.SemaphoreType.DMA],
        vmem=24,
        moved=8 * MIB,
        name="table",
    )
    *near, placed = lax.optimization_barrier((*near, placed))
    h_one, *edge = call(magnetic_kernel, (dense,) + faces, (e_old, h_old, *near), name="magnetic")
    edge = shifted(edge, up)
    spread_fields = call(
        scatter_kernel,
        shape(8, ROWS, CZ),
        (placed, fields),
        scratch=[
            pltpu.VMEM((8 * CZ, ROWS), F32),
            pltpu.VMEM((8 * CZ, 2 * GROUP * CZ), BF16),
            pltpu.VMEM((ROWS, 2 * GROUP * CZ), BF16),
        ],
        name="scatter",
    )
    e_one, *near, source = call(
        electric_kernel,
        (dense,) + faces + (dense,),
        (e_old, h_one, *edge, eps, spread_fields),
        name="electric",
    )
    near = shifted(near, down)
    drives, early = call(
        drive_kernel,
        (shape(SLOTS, 8, CZ), shape(8, CZ)),
        (e_old, e_one, h_one, placed, surf),
        scratch=[pltpu.VMEM((6 * ROWS, 2 * CZ), BF16)],
        name="drive",
    )
    *near, early = lax.optimization_barrier((*near, early))
    h_two, *edge = call(magnetic_kernel, (dense,) + faces, (e_one, h_one, *near), name="magnetic2")
    edge = shifted(edge, up)
    back = lax.all_to_all(drives, "gx", 0, 0, tiled=True)
    part = shape(12 * FREQ // 2, DIRS)
    e_two, keep, send = call(
        final_kernel,
        (dense, part, part),
        (e_one, h_two, *edge, eps, source, surf, early, table, factors),
        scratch=[pltpu.VMEM((8, CZ), F32)],
        vmem=24,
        moved=8 * MIB,
        name="final",
    )
    chip = keep + lax.ppermute(send, "gz", down[2])
    chip, back = lax.optimization_barrier((chip, back))
    pieces = lax.all_to_all(chip.reshape(8, 48, DIRS), "gy", 0, 0, tiled=True)
    total = jnp.sum(pieces, axis=0)
    total = all_reduce(
        total, "gx", lambda k: [(a * 4 + z, (a ^ k) * 4 + z) for a in range(4) for z in range(4)]
    )
    total = all_reduce(
        total, "gx", lambda k: [(a * 4 + z, a * 4 + (z ^ k)) for a in range(4) for z in range(4)]
    )
    gathered = lax.all_to_all(
        jnp.broadcast_to(total[None], (8, 48, DIRS)), "gy", 0, 0, tiled=True
    )
    far_out = far_acc + jnp.transpose(gathered.reshape(12, FREQ // 2, DIRS), (1, 0, 2))
    state_out, e_out, h_out = call(
        atoms_kernel,
        (shape(10, SLOTS, CZ), dense, dense),
        (state, pump.reshape(SLOTS, CZ), back, e_two, h_two),
        name="atoms",
    )
    return (
        e_out.reshape(efield.shape),
        h_out.reshape(hfield.shape),
        jnp.transpose(state_out, (1, 0, 2)).reshape(gain_state.shape),
        far_out,
    )


def solution(mesh):
    placed = (
        P(None, "gx", "gy", "gz"),
        P(None, "gx", "gy", "gz"),
        P("gx", "gy", "gz"),
        P("gx", "gy", "gz", None, None, None),
        P("gx", "gy", "gz", None, None),
        P("gx", "gy", "gz", None, None),
        P("gx", "gy", "gz"),
        P("gx", "gy", "gz", None),
        P("gx", "gy", "gz", None),
        P("gz", None, None),
    )
    return jax.shard_map(
        local,
        mesh=mesh,
        in_specs=placed,
        out_specs=(
            P(None, "gx", "gy", "gz"),
            P(None, "gx", "gy", "gz"),
            P("gx", "gy", "gz", None, None, None),
            P("gz", None, None),
        ),
        check_vma=False,
    )
```

```python
import functools
import math

import jax
import jax.numpy as jnp
import numpy as np
from jax import lax
from jax.experimental import pallas as pl
from jax.experimental.pallas import tpu as pltpu
from jax.sharding import PartitionSpec as P

FREQ = 64
STEPS = 2
CX = 8
CY = 24
CZ = 128
ROWS = CX * CY
SLOTS = 32
DIRS = 128

time_step = 0.5
damping = 0.1
omega_rest = 1.0
coupling = 0.5
cross_rate = 0.3
upper_life = 2.0
lasing_life = 20.0
lower_life = 2.0
freq_low = 0.3
freq_pitch = 0.01
golden = 2.399963229728653

half = 0.5 * damping * time_step
keep_rate = (1.0 - half) / (1.0 + half)
spring = time_step * omega_rest * omega_rest / (1.0 + half)
gain_push = time_step * coupling / (1.0 + half)

F32 = jnp.float32
BF16 = jnp.bfloat16
MIB = 1 << 20


def shape(*dims, dtype=F32):
    return jax.ShapeDtypeStruct(dims, dtype)


def call(kernel, outs, args, in_specs=None, scratch=(), vmem=16, flops=0, moved=2 * MIB, name=None):
    return pl.pallas_call(
        kernel,
        out_shape=outs,
        in_specs=in_specs or [pl.BlockSpec(memory_space=pltpu.VMEM)] * len(args),
        scratch_shapes=scratch,
        compiler_params=pltpu.CompilerParams(vmem_limit_bytes=vmem * MIB),
        cost_estimate=pl.CostEstimate(flops=flops, bytes_accessed=moved, transcendentals=0),
        name=name,
    )(*args)


def stay(*values):
    return [pltpu.with_memory_space_constraint(value, pltpu.HBM) for value in values]


def split_parts(value):
    high = value.astype(BF16)
    low = (value - high.astype(F32)).astype(BF16)
    return high, low


def row_index(count, width):
    return lax.broadcasted_iota(jnp.int32, (count, width), 0)


def lane_index(count):
    return lax.broadcasted_iota(jnp.int32, (count, CZ), 1)


def ahead_x(field, face):
    return jnp.concatenate([field[CY:], face], axis=0)


def behind_x(field, face):
    return jnp.concatenate([face, field[:-CY]], axis=0)


def spread(face):
    return jnp.broadcast_to(face[:, None, :], (CX, CY, CZ)).reshape(ROWS, CZ)


def ahead_y(field, face, last):
    return jnp.where(last, spread(face), pltpu.roll(field, ROWS - 1, 0))


def behind_y(field, face, first):
    return jnp.where(first, spread(face), pltpu.roll(field, 1, 0))


def ahead_z(field, other, lane):
    return pltpu.roll(jnp.where(lane == 0, other, field), CZ - 1, 1)


def behind_z(field, other, lane):
    return pltpu.roll(jnp.where(lane == CZ - 1, other, field), 1, 1)


def row_in_brick():
    rows = row_index(ROWS, CZ)
    return rows - CY * ((rows * 2731) >> 16)


def first_layers(field_ref, out_x, out_y, out_z):
    out_x[0] = field_ref[1, 0:CY]
    out_x[1] = field_ref[2, 0:CY]
    for place, comp in ((0, 0), (1, 2)):
        for layer in range(CX):
            out_y[place, layer : layer + 1] = field_ref[comp, layer * CY : layer * CY + 1]
    out_z[0] = field_ref[0]
    out_z[1] = field_ref[1]


def last_layers(field_ref, out_x, out_y, out_z):
    out_x[0] = field_ref[1, ROWS - CY : ROWS]
    out_x[1] = field_ref[2, ROWS - CY : ROWS]
    for place, comp in ((0, 0), (1, 2)):
        for layer in range(CX):
            row = layer * CY + CY - 1
            out_y[place, layer : layer + 1] = field_ref[comp, row : row + 1]
    out_z[0] = field_ref[0]
    out_z[1] = field_ref[1]


def inside(faces, ahead):
    kept = []
    for face, axis in zip(faces, ("gx", "gy", "gz")):
        index = lax.axis_index(axis)
        real = index < lax.axis_size(axis) - 1 if ahead else index > 0
        kept.append([jnp.where(real, face[place], 0.0) for place in range(2)])
    return kept


def prepare_kernel(
    e_hbm, state_hbm, h_hbm, eps_hbm, out_x, out_y, out_z, packed, e_out, h_out, eps_out, state, sems
):
    copies = [
        pltpu.make_async_copy(source, target, sems.at[place])
        for place, (source, target) in enumerate(
            ((e_hbm, e_out), (state_hbm, state), (h_hbm, h_out), (eps_hbm, eps_out))
        )
    ]
    for copy in copies:
        copy.start()
    copies[0].wait()
    first_layers(e_out, out_x, out_y, out_z)
    copies[1].wait()
    lower, lasing, upper = state[7], state[8], state[9]
    lasing_free = lasing + time_step * (upper / upper_life - lasing / lasing_life)
    lower_free = lower + time_step * (lasing / lasing_life - lower / lower_life)
    polar = [state[comp] for comp in range(3)]
    free = [keep_rate * state[3 + comp] - spring * polar[comp] for comp in range(3)]
    for field, value in enumerate(free + [lasing - lower] + polar + [lasing_free - lower_free]):
        for owner in range(SLOTS // 2):
            packed[owner, 2 * field : 2 * field + 2] = value[2 * owner : 2 * owner + 2]
    copies[2].wait()
    copies[3].wait()


def magnetic_kernel(e_ref, h_ref, face_x, face_y, face_z, h_out, out_x, out_y, out_z):
    lane = lane_index(ROWS)
    last = row_in_brick() == CY - 1
    face_x, face_y, face_z = inside((face_x, face_y, face_z), True)
    ex, ey, ez = e_ref[0], e_ref[1], e_ref[2]
    first = (ahead_y(ez, face_y[1], last) - ez) - (ahead_z(ey, face_z[1], lane) - ey)
    second = (ahead_z(ex, face_z[0], lane) - ex) - (ahead_x(ez, face_x[1]) - ez)
    third = (ahead_x(ey, face_x[0]) - ey) - (ahead_y(ex, face_y[0], last) - ex)
    h_out[0] = h_ref[0] - time_step * first
    h_out[1] = h_ref[1] - time_step * second
    h_out[2] = h_ref[2] - time_step * third
    last_layers(h_out, out_x, out_y, out_z)


def electric_curl(h_ref, face_x, face_y, face_z):
    lane = lane_index(ROWS)
    start = row_in_brick() == 0
    face_x, face_y, face_z = inside((face_x, face_y, face_z), False)
    hx, hy, hz = h_ref[0], h_ref[1], h_ref[2]
    first = (hz - behind_y(hz, face_y[1], start)) - (hy - behind_z(hy, face_z[1], lane))
    second = (hx - behind_z(hx, face_z[0], lane)) - (hz - behind_x(hz, face_x[1]))
    third = (hy - behind_x(hy, face_x[0])) - (hx - behind_y(hx, face_y[0], start))
    return first, second, third


HALF = ROWS // 2
WIDE = 2 * CZ


def wide_hits(offsets, width):
    hits = row_index(WIDE, width) == (offsets & (WIDE - 1))
    return hits.astype(F32).astype(BF16)


def tall_hits(offsets, width):
    return row_index(HALF, width) == (offsets >> 8)


GROUP = 8


def scatter_kernel(first, placed, fields_ref, dense, total, spots, columns):
    def group(index, carry):
        lines = placed[pl.ds(GROUP * index, GROUP)]
        for slot in range(GROUP):
            line = lines[slot : slot + 1]
            hits = wide_hits(line, CZ)
            tall = tall_hits(line, CZ).astype(F32).astype(BF16).reshape(6, 16, CZ)
            values = fields_ref[
                (GROUP // 2) * index + slot // 2, pl.ds(2 * first + slot % 2, 4, 2), :
            ]
            for place, part in enumerate(split_parts(values)):
                across = (place * GROUP + slot) * CZ
                columns[:, across : across + CZ] = hits
                part = part.astype(F32)
                for field in range(4):
                    row = jnp.broadcast_to(part[field : field + 1], (16, CZ)).astype(BF16)
                    spots[field * HALF : (field + 1) * HALF, across : across + CZ] = (
                        tall * row[None]
                    ).reshape(HALF, CZ)
        got = lax.dot_general(
            spots[...], columns[...], (((1,), (1,)), ((), ())), preferred_element_type=F32
        )

        @pl.when(index == 0)
        def _():
            total[...] = got

        @pl.when(index > 0)
        def _():
            total[...] += got

        return carry

    lax.fori_loop(0, SLOTS // GROUP, group, 0)
    for field in range(4):
        got = total[field * HALF : (field + 1) * HALF]
        dense[field, pl.ds(0, HALF, 2), :] = got[:, :CZ]
        dense[field, pl.ds(1, HALF, 2), :] = got[:, CZ:]


def scattered(first, placed, fields, name):
    return call(
        functools.partial(scatter_kernel, first),
        shape(4, ROWS, CZ),
        (placed, fields),
        scratch=[
            pltpu.VMEM((4 * HALF, WIDE), F32),
            pltpu.VMEM((4 * HALF, 2 * GROUP * CZ), BF16),
            pltpu.VMEM((WIDE, 2 * GROUP * CZ), BF16),
        ],
        name=name,
    )


def electric_kernel(
    e_ref, h_ref, face_x, face_y, face_z, eps_ref, dense, e_out, out_x, out_y, out_z, rates
):
    curls = electric_curl(h_ref, face_x, face_y, face_z)
    scaled = time_step * eps_ref[...]
    inversion = dense[3]
    power = jnp.zeros_like(inversion)
    for comp in range(3):
        field = e_ref[comp]
        rate = dense[comp] + gain_push * inversion * field
        power = power + field * rate
        rates[comp] = rate
        e_out[comp] = field + scaled * (curls[comp] - rate)
    rates[3] = power
    first_layers(e_out, out_x, out_y, out_z)


def paired(ref, comp):
    return jnp.concatenate(
        [ref[comp, pl.ds(0, HALF, 2), :], ref[comp, pl.ds(1, HALF, 2), :]], axis=1
    )


def stacked(fields):
    return split_parts(jnp.concatenate([paired(ref, comp) for ref, comp in fields], axis=0))


def gather_lines(high, low, offsets, width):
    hits = wide_hits(offsets, width)
    tall = tall_hits(offsets, width)
    picked = jnp.dot(high, hits, preferred_element_type=F32)
    picked = picked + jnp.dot(low, hits, preferred_element_type=F32)
    return [
        jnp.sum(
            jnp.where(tall, picked[field * HALF : (field + 1) * HALF], 0.0), axis=0, keepdims=True
        )
        for field in range(picked.shape[0] // HALF)
    ]


TAKE = 4


def gather_drive(field_ref, placed, drives, first, high, low):
    high[...], low[...] = stacked([(field_ref, comp) for comp in range(3)])

    def group(index, carry):
        lines = placed[pl.ds(TAKE * index, TAKE)]
        offsets = jnp.concatenate([lines[slot : slot + 1] for slot in range(TAKE)], axis=1)
        got = gather_lines(high[...], low[...], offsets, TAKE * CZ)
        for comp in range(3):
            for slot in range(TAKE):
                drives[TAKE * index + slot, first + comp : first + comp + 1] = got[comp][
                    :, slot * CZ : (slot + 1) * CZ
                ]
        return carry

    lax.fori_loop(0, SLOTS // TAKE, group, 0)


def sample_rows(e_ref, h_ref, surf_ref, sampled):
    high, low = stacked([(ref, comp) for ref in (e_ref, h_ref) for comp in range(3)])
    got = gather_lines(high, low, surf_ref[...], CZ)
    sampled[...] = jnp.zeros_like(sampled)
    for field in range(6):
        sampled[field : field + 1] = got[field]


def drive_kernel(e_ref, h_ref, placed, surf_ref, before, drives, sampled, high, low):
    drives[...] = before[...]
    gather_drive(e_ref, placed, drives, 3, high, low)
    sample_rows(e_ref, h_ref, surf_ref, sampled)


def times(left, right):
    return (left[0] * right[0] - left[1] * right[1], left[1] * right[0] + left[0] * right[1])


def early_kernel(
    count_ref,
    owner_hbm,
    offsets_ref,
    surf_ref,
    units_ref,
    e_ref,
    placed,
    drives,
    surf_out,
    starts,
    turn,
    factors,
    owner_ref,
    sem,
    high,
    low,
):
    copy = pltpu.make_async_copy(owner_hbm, owner_ref, sem)
    copy.start()
    lanes = lax.broadcasted_iota(jnp.int32, (8, DIRS), 1)
    omega = freq_low + freq_pitch * (lanes & (FREQ - 1)).astype(F32)
    moment = omega * jnp.where(lanes < FREQ, time_step, 2.0 * time_step)
    for place, value in enumerate((jnp.cos(moment), jnp.sin(moment))):
        factors[place] = jnp.transpose(jnp.broadcast_to(value[0:1], (DIRS, DIRS)))
    cells = surf_ref[...]
    surf_out[...] = cells
    rows = cells >> 7
    layer = (rows * 2731) >> 16
    cell_x = lax.axis_index("gx") * CX + layer
    cell_y = lax.axis_index("gy") * CY + (rows - CY * layer)
    cell_z = lax.axis_index("gz") * CZ + (cells & (CZ - 1))
    along = jnp.zeros((CZ, DIRS), F32)
    for axis, (cell, size) in enumerate(((cell_x, 128), (cell_y, 192), (cell_z, 256))):
        place = cell.astype(F32) - 0.5 * (size - 1)
        column = jnp.transpose(jnp.broadcast_to(place, (CZ, CZ)))
        along = along + column * units_ref[axis : axis + 1]
    angle = (0.25 * freq_pitch) * along
    square = angle * angle
    cosine = 1.0 + square * (
        -1 / 2 + square * (1 / 24 + square * (-1 / 720 + square * (1 / 40320)))
    )
    sine = angle * (
        1.0 + square * (-1 / 6 + square * (1 / 120 + square * (-1 / 5040 + square * (1 / 362880))))
    )
    two = times((cosine, sine), (cosine, sine))
    powers = {1: times(two, two)}
    for power in (2, 4, 8, 16, 32):
        powers[power] = times(powers[power // 2], powers[power // 2])
    low_start = times(times(powers[16], powers[8]), times(powers[4], powers[2]))
    high_start = times(low_start, powers[32])
    turn[0], turn[1] = powers[1]
    starts[0], starts[1] = low_start
    starts[2], starts[3] = high_start
    copy.wait()
    count = count_ref[0]
    for slot in range(SLOTS):
        line = offsets_ref[slot : slot + 1]
        placed[pl.ds(owner_ref[0, slot], 1)] = jnp.where(slot < count, line, -1)
    drives[...] = jnp.zeros_like(drives)
    gather_drive(e_ref, placed, drives, 0, high, low)


def final_kernel(
    e_ref,
    h_ref,
    face_x,
    face_y,
    face_z,
    eps_ref,
    rates,
    dense,
    surf_ref,
    early_ref,
    starts,
    turn,
    factors,
    e_out,
    keep_out,
    send_out,
    late,
    now,
):
    curls = electric_curl(h_ref, face_x, face_y, face_z)
    scaled = time_step * eps_ref[...]
    later = dense[3] + (2.0 * time_step * cross_rate) * rates[3]
    for comp in range(3):
        field = e_ref[comp]
        polar = dense[comp] + time_step * rates[comp]
        rate = keep_rate * rates[comp] - spring * polar + gain_push * later * field
        e_out[comp] = field + scaled * (curls[comp] - rate)
    sample_rows(e_out, h_ref, surf_ref, late)
    scale = 1.0 / math.sqrt(STEPS * CZ * 256)
    high, low = split_parts(scale * jnp.concatenate([early_ref[...], late[...]], axis=0))
    left = jnp.concatenate(
        [
            jnp.concatenate([high, high], axis=1),
            jnp.concatenate([low, jnp.zeros_like(low)], axis=1),
        ],
        axis=0,
    )
    own = lax.axis_index("gz")
    for side, out in ((1, send_out), (0, keep_out)):
        target = lax.rem(own + side, 2)
        now[0] = starts[2 * target]
        now[1] = starts[2 * target + 1]
        for freq in range(FREQ // 2):
            here = (now[0], now[1])
            re_high, re_low = split_parts(here[0])
            im_high, im_low = split_parts(here[1])
            right = jnp.concatenate(
                [
                    jnp.concatenate([re_high, im_high], axis=1),
                    jnp.concatenate([re_low, im_low], axis=1),
                ],
                axis=0,
            )
            now[0], now[1] = times(here, (turn[0], turn[1]))
            both = jnp.dot(left, right, preferred_element_type=F32)
            both = both[0:16] + both[16:32]
            real = jnp.zeros((8, DIRS), F32)
            imag = jnp.zeros((8, DIRS), F32)
            for step in range(STEPS):
                row = pl.ds(step * FREQ + target * (FREQ // 2) + freq, 1)
                cosine = factors[0, row]
                sine = factors[1, row]
                upper = both[8 * step : 8 * step + 8, 0:DIRS]
                under = both[8 * step : 8 * step + 8, DIRS:]
                real = real + (cosine * upper + sine * under)
                imag = imag + (cosine * under - sine * upper)
            for comp in range(6):
                row = comp * (FREQ // 2) + freq
                out[row : row + 1] = real[comp : comp + 1]
                row = (comp + 6) * (FREQ // 2) + freq
                out[row : row + 1] = imag[comp : comp + 1]


def atoms_kernel(state_ref, pump_ref, drives, e_ref, h_ref, out, e_out, h_out):
    polar = [state_ref[c] for c in range(3)]
    rate = [state_ref[3 + c] for c in range(3)]
    ground, lower, lasing, upper = [state_ref[6 + level] for level in range(4)]
    pump = pump_ref[...]
    for step in range(STEPS):
        drive = [drives[:, 3 * step + c] for c in range(3)]
        inversion = lasing - lower
        power = jnp.zeros_like(pump)
        for c in range(3):
            rate[c] = (
                (1.0 - half) * rate[c]
                + time_step
                * (coupling * inversion * drive[c] - omega_rest * omega_rest * polar[c])
            ) / (1.0 + half)
            polar[c] = polar[c] + time_step * rate[c]
            power = power + drive[c] * rate[c]
        upper_new = upper + time_step * (pump * ground - upper / upper_life)
        lasing_new = lasing + time_step * (
            upper / upper_life - lasing / lasing_life + cross_rate * power
        )
        lower_new = lower + time_step * (
            lasing / lasing_life - lower / lower_life - cross_rate * power
        )
        ground = ground + time_step * (lower / lower_life - pump * ground)
        lower, lasing, upper = lower_new, lasing_new, upper_new
    for place, value in enumerate(polar + rate + [ground, lower, lasing, upper]):
        out[place] = value
    e_out[...] = e_ref[...]
    h_out[...] = h_ref[...]


def directions(count):
    index = np.arange(count, dtype=np.float32)
    cosine = np.float32(1.0) - np.float32(2.0) * (index + np.float32(0.5)) / np.float32(count)
    sine = np.sqrt(np.float32(1.0) - cosine * cosine)
    azimuth = (np.float32(golden) * index).astype(np.float64)
    rows = np.zeros((8, count), np.float32)
    rows[0] = sine * np.cos(azimuth).astype(np.float32)
    rows[1] = sine * np.sin(azimuth).astype(np.float32)
    rows[2] = cosine
    return rows


def all_reduce(value, axis, peers):
    one, two, three = [lax.ppermute(value, axis, peers(k)) for k in (1, 2, 3)]
    return (value + one) + (two + three)


def local(
    efield,
    hfield,
    inv_eps,
    gain_state,
    pump,
    gain_offsets,
    gain_count,
    block_owner,
    surf_offsets,
    far_acc,
):
    state = jnp.transpose(gain_state.reshape(SLOTS, 10, CZ), (1, 0, 2))
    dense = shape(3, ROWS, CZ)
    faces = (shape(2, CY, CZ), shape(2, CX, CZ), shape(2, ROWS, CZ))
    down = [[((i + 1) % n, i) for i in range(n)] for n in (16, 8, 2)]
    up = [[(i, (i + 1) % n) for i in range(n)] for n in (16, 8, 2)]
    vmem = pl.BlockSpec(memory_space=pltpu.VMEM)

    hbm = pl.BlockSpec(memory_space=pltpu.HBM)

    def shifted(parts, perms):
        return [
            lax.ppermute(part, axis, perm)
            for part, axis, perm in zip(parts, ("gx", "gy", "gz"), perms)
        ]

    *near, packed, e_old, h_old, eps = call(
        prepare_kernel,
        faces + (shape(SLOTS // 2, 16, CZ), dense, dense, shape(ROWS, CZ)),
        stay(
            efield.reshape(3, ROWS, CZ),
            state,
            hfield.reshape(3, ROWS, CZ),
            inv_eps.reshape(ROWS, CZ),
        ),
        in_specs=[hbm] * 4,
        scratch=[pltpu.VMEM((10, SLOTS, CZ), F32), pltpu.SemaphoreType.DMA((4,))],
        name="prepare",
    )
    near = shifted(near, down)
    fields = lax.all_to_all(packed, "gx", 0, 0, tiled=True)
    halves = [pltpu.VMEM((3 * HALF, WIDE), BF16)] * 2
    placed, before, surf, starts, turn, factors = call(
        early_kernel,
        (
            shape(SLOTS, CZ, dtype=jnp.int32),
            shape(SLOTS, 8, CZ),
            shape(1, CZ, dtype=jnp.int32),
            shape(4, CZ, DIRS),
            shape(2, CZ, DIRS),
            shape(2, STEPS * FREQ, DIRS),
        ),
        [gain_count.reshape(1)]
        + stay(
            block_owner.reshape(1, SLOTS),
            gain_offsets.reshape(SLOTS, CZ),
            surf_offsets.reshape(1, CZ),
            jnp.asarray(directions(DIRS)),
        )
        + [e_old],
        in_specs=[pl.BlockSpec(memory_space=pltpu.SMEM), hbm, vmem, vmem, vmem, vmem],
        scratch=[pltpu.SMEM((1, SLOTS), jnp.int32), pltpu.SemaphoreType.DMA] + halves,
        name="early",
    )
    *near, placed = lax.optimization_barrier((*near, placed))
    h_one, *edge = call(magnetic_kernel, (dense,) + faces, (e_old, h_old, *near), name="magnetic")
    edge = shifted(edge, up)
    spread_now = scattered(0, placed, fields, "scatter")
    e_one, *near, rates = call(
        electric_kernel,
        (dense,) + faces + (shape(4, ROWS, CZ),),
        (e_old, h_one, *edge, eps, spread_now),
        name="electric",
    )
    near = shifted(near, down)
    drives, early = call(
        drive_kernel,
        (shape(SLOTS, 8, CZ), shape(8, CZ)),
        (e_one, h_one, placed, surf, before),
        scratch=halves,
        name="drive",
    )
    *near, early = lax.optimization_barrier((*near, early))
    h_two, *edge = call(magnetic_kernel, (dense,) + faces, (e_one, h_one, *near), name="magnetic2")
    edge = shifted(edge, up)
    back = lax.all_to_all(drives, "gx", 0, 0, tiled=True)
    placed, fields, early = lax.optimization_barrier((placed, fields, early))
    spread_next = scattered(4, placed, fields, "scatter2")
    part = shape(12 * FREQ // 2, DIRS)
    e_two, keep, send = call(
        final_kernel,
        (dense, part, part),
        (e_one, h_two, *edge, eps, rates, spread_next, surf, early, starts, turn, factors),
        scratch=[pltpu.VMEM((8, CZ), F32), pltpu.VMEM((2, CZ, DIRS), F32)],
        name="final",
    )
    chip = keep + lax.ppermute(send, "gz", down[2])
    chip, back = lax.optimization_barrier((chip, back))
    pieces = lax.all_to_all(chip.reshape(8, 48, DIRS), "gy", 0, 0, tiled=True)
    total = jnp.sum(pieces, axis=0)
    total = all_reduce(
        total, "gx", lambda k: [(a * 4 + z, (a ^ k) * 4 + z) for a in range(4) for z in range(4)]
    )
    total = all_reduce(
        total, "gx", lambda k: [(a * 4 + z, a * 4 + (z ^ k)) for a in range(4) for z in range(4)]
    )
    results = call(
        atoms_kernel,
        (shape(10, SLOTS, CZ), dense, dense),
        (state, pump.reshape(SLOTS, CZ), back, e_two, h_two),
        name="atoms",
    )
    total, state_out, e_out, h_out = lax.optimization_barrier((total, *results))
    gathered = lax.all_to_all(
        jnp.broadcast_to(total[None], (8, 48, DIRS)), "gy", 0, 0, tiled=True
    )
    far_out = far_acc + jnp.transpose(gathered.reshape(12, FREQ // 2, DIRS), (1, 0, 2))
    return (
        e_out.reshape(efield.shape),
        h_out.reshape(hfield.shape),
        jnp.transpose(state_out, (1, 0, 2)).reshape(gain_state.shape),
        far_out,
    )


def solution(mesh):
    placed = (
        P(None, "gx", "gy", "gz"),
        P(None, "gx", "gy", "gz"),
        P("gx", "gy", "gz"),
        P("gx", "gy", "gz", None, None, None),
        P("gx", "gy", "gz", None, None),
        P("gx", "gy", "gz", None, None),
        P("gx", "gy", "gz"),
        P("gx", "gy", "gz", None),
        P("gx", "gy", "gz", None),
        P("gz", None, None),
    )
    return jax.shard_map(
        local,
        mesh=mesh,
        in_specs=placed,
        out_specs=(
            P(None, "gx", "gy", "gz"),
            P(None, "gx", "gy", "gz"),
            P("gx", "gy", "gz", None, None, None),
            P("gz", None, None),
        ),
        check_vma=False,
    )
```

```python
import functools
import math

import jax
import jax.numpy as jnp
import numpy as np
from jax import lax
from jax.experimental import pallas as pl
from jax.experimental.pallas import tpu as pltpu
from jax.sharding import PartitionSpec as P

FREQ = 64
STEPS = 2
CX = 8
CY = 24
CZ = 128
ROWS = CX * CY
SLOTS = 32
DIRS = 128

time_step = 0.5
damping = 0.1
omega_rest = 1.0
coupling = 0.5
cross_rate = 0.3
upper_life = 2.0
lasing_life = 20.0
lower_life = 2.0
freq_low = 0.3
freq_pitch = 0.01
golden = 2.399963229728653

half = 0.5 * damping * time_step
keep_rate = (1.0 - half) / (1.0 + half)
spring = time_step * omega_rest * omega_rest / (1.0 + half)
gain_push = time_step * coupling / (1.0 + half)

F32 = jnp.float32
BF16 = jnp.bfloat16
MIB = 1 << 20


def shape(*dims, dtype=F32):
    return jax.ShapeDtypeStruct(dims, dtype)


def call(kernel, outs, args, in_specs=None, scratch=(), vmem=16, flops=0, moved=2 * MIB, name=None):
    return pl.pallas_call(
        kernel,
        out_shape=outs,
        in_specs=in_specs or [pl.BlockSpec(memory_space=pltpu.VMEM)] * len(args),
        scratch_shapes=scratch,
        compiler_params=pltpu.CompilerParams(vmem_limit_bytes=vmem * MIB),
        cost_estimate=pl.CostEstimate(flops=flops, bytes_accessed=moved, transcendentals=0),
        name=name,
    )(*args)


def stay(*values):
    return [pltpu.with_memory_space_constraint(value, pltpu.HBM) for value in values]


def split_parts(value):
    high = value.astype(BF16)
    low = (value - high.astype(F32)).astype(BF16)
    return high, low


def row_index(count, width):
    return lax.broadcasted_iota(jnp.int32, (count, width), 0)


def lane_index(count):
    return lax.broadcasted_iota(jnp.int32, (count, CZ), 1)


def ahead_x(field, face):
    return jnp.concatenate([field[CY:], face], axis=0)


def behind_x(field, face):
    return jnp.concatenate([face, field[:-CY]], axis=0)


def spread(face):
    return jnp.broadcast_to(face[:, None, :], (CX, CY, CZ)).reshape(ROWS, CZ)


def ahead_y(field, face, last):
    return jnp.where(last, spread(face), pltpu.roll(field, ROWS - 1, 0))


def behind_y(field, face, first):
    return jnp.where(first, spread(face), pltpu.roll(field, 1, 0))


def ahead_z(field, other, lane):
    return pltpu.roll(jnp.where(lane == 0, other, field), CZ - 1, 1)


def behind_z(field, other, lane):
    return pltpu.roll(jnp.where(lane == CZ - 1, other, field), 1, 1)


def row_in_brick():
    rows = row_index(ROWS, CZ)
    return rows - CY * ((rows * 2731) >> 16)


def first_layers(field_ref, out_x, out_y, out_z):
    out_x[0] = field_ref[1, 0:CY]
    out_x[1] = field_ref[2, 0:CY]
    for place, comp in ((0, 0), (1, 2)):
        for layer in range(CX):
            out_y[place, layer : layer + 1] = field_ref[comp, layer * CY : layer * CY + 1]
    out_z[0] = field_ref[0]
    out_z[1] = field_ref[1]


def last_layers(field_ref, out_x, out_y, out_z):
    out_x[0] = field_ref[1, ROWS - CY : ROWS]
    out_x[1] = field_ref[2, ROWS - CY : ROWS]
    for place, comp in ((0, 0), (1, 2)):
        for layer in range(CX):
            row = layer * CY + CY - 1
            out_y[place, layer : layer + 1] = field_ref[comp, row : row + 1]
    out_z[0] = field_ref[0]
    out_z[1] = field_ref[1]


def inside(faces, ahead):
    kept = []
    for face, axis in zip(faces, ("gx", "gy", "gz")):
        index = lax.axis_index(axis)
        real = index < lax.axis_size(axis) - 1 if ahead else index > 0
        kept.append([jnp.where(real, face[place], 0.0) for place in range(2)])
    return kept


def prepare_kernel(
    e_hbm, state_hbm, h_hbm, eps_hbm, out_x, out_y, out_z, packed, e_out, h_out, eps_out, state, sems
):
    copies = [
        pltpu.make_async_copy(source, target, sems.at[place])
        for place, (source, target) in enumerate(
            ((e_hbm, e_out), (state_hbm, state), (h_hbm, h_out), (eps_hbm, eps_out))
        )
    ]
    for copy in copies:
        copy.start()
    copies[0].wait()
    first_layers(e_out, out_x, out_y, out_z)
    copies[1].wait()
    lower, lasing, upper = state[7], state[8], state[9]
    lasing_free = lasing + time_step * (upper / upper_life - lasing / lasing_life)
    lower_free = lower + time_step * (lasing / lasing_life - lower / lower_life)
    polar = [state[comp] for comp in range(3)]
    free = [keep_rate * state[3 + comp] - spring * polar[comp] for comp in range(3)]
    for field, value in enumerate(free + [lasing - lower] + polar + [lasing_free - lower_free]):
        for owner in range(SLOTS // 2):
            packed[owner, 2 * field : 2 * field + 2] = value[2 * owner : 2 * owner + 2]
    copies[2].wait()
    copies[3].wait()


def magnetic_kernel(e_ref, h_ref, face_x, face_y, face_z, h_out, out_x, out_y, out_z):
    lane = lane_index(ROWS)
    last = row_in_brick() == CY - 1
    face_x, face_y, face_z = inside((face_x, face_y, face_z), True)
    ex, ey, ez = e_ref[0], e_ref[1], e_ref[2]
    first = (ahead_y(ez, face_y[1], last) - ez) - (ahead_z(ey, face_z[1], lane) - ey)
    second = (ahead_z(ex, face_z[0], lane) - ex) - (ahead_x(ez, face_x[1]) - ez)
    third = (ahead_x(ey, face_x[0]) - ey) - (ahead_y(ex, face_y[0], last) - ex)
    h_out[0] = h_ref[0] - time_step * first
    h_out[1] = h_ref[1] - time_step * second
    h_out[2] = h_ref[2] - time_step * third
    last_layers(h_out, out_x, out_y, out_z)


def electric_curl(h_ref, face_x, face_y, face_z):
    lane = lane_index(ROWS)
    start = row_in_brick() == 0
    face_x, face_y, face_z = inside((face_x, face_y, face_z), False)
    hx, hy, hz = h_ref[0], h_ref[1], h_ref[2]
    first = (hz - behind_y(hz, face_y[1], start)) - (hy - behind_z(hy, face_z[1], lane))
    second = (hx - behind_z(hx, face_z[0], lane)) - (hz - behind_x(hz, face_x[1]))
    third = (hy - behind_x(hy, face_x[0])) - (hx - behind_y(hx, face_y[0], start))
    return first, second, third


HALF = ROWS // 2
WIDE = 2 * CZ


def wide_hits(offsets, width):
    hits = row_index(WIDE, width) == (offsets & (WIDE - 1))
    return hits.astype(F32).astype(BF16)


def tall_hits(offsets, width):
    return row_index(HALF, width) == (offsets >> 8)


GROUP = 8


def scatter_kernel(first, placed, fields_ref, dense, total, spots, columns):
    def group(index, carry):
        lines = placed[pl.ds(GROUP * index, GROUP)]
        for slot in range(GROUP):
            line = lines[slot : slot + 1]
            hits = wide_hits(line, CZ)
            tall = tall_hits(line, CZ).astype(F32).astype(BF16).reshape(6, 16, CZ)
            values = fields_ref[
                (GROUP // 2) * index + slot // 2, pl.ds(2 * first + slot % 2, 4, 2), :
            ]
            for place, part in enumerate(split_parts(values)):
                across = (place * GROUP + slot) * CZ
                columns[:, across : across + CZ] = hits
                part = part.astype(F32)
                for field in range(4):
                    row = jnp.broadcast_to(part[field : field + 1], (16, CZ)).astype(BF16)
                    spots[field * HALF : (field + 1) * HALF, across : across + CZ] = (
                        tall * row[None]
                    ).reshape(HALF, CZ)
        got = lax.dot_general(
            spots[...], columns[...], (((1,), (1,)), ((), ())), preferred_element_type=F32
        )

        @pl.when(index == 0)
        def _():
            total[...] = got

        @pl.when(index > 0)
        def _():
            total[...] += got

        return carry

    lax.fori_loop(0, SLOTS // GROUP, group, 0)
    for field in range(4):
        got = total[field * HALF : (field + 1) * HALF]
        dense[field, pl.ds(0, HALF, 2), :] = got[:, :CZ]
        dense[field, pl.ds(1, HALF, 2), :] = got[:, CZ:]


def scattered(first, placed, fields, name):
    return call(
        functools.partial(scatter_kernel, first),
        shape(4, ROWS, CZ),
        (placed, fields),
        scratch=[
            pltpu.VMEM((4 * HALF, WIDE), F32),
            pltpu.VMEM((4 * HALF, 2 * GROUP * CZ), BF16),
            pltpu.VMEM((WIDE, 2 * GROUP * CZ), BF16),
        ],
        name=name,
    )


def electric_kernel(
    e_ref, h_ref, face_x, face_y, face_z, eps_ref, dense, e_out, out_x, out_y, out_z, rates
):
    curls = electric_curl(h_ref, face_x, face_y, face_z)
    scaled = time_step * eps_ref[...]
    inversion = dense[3]
    power = jnp.zeros_like(inversion)
    for comp in range(3):
        field = e_ref[comp]
        rate = dense[comp] + gain_push * inversion * field
        power = power + field * rate
        rates[comp] = rate
        e_out[comp] = field + scaled * (curls[comp] - rate)
    rates[3] = power
    first_layers(e_out, out_x, out_y, out_z)


def paired(ref, comp):
    return jnp.concatenate(
        [ref[comp, pl.ds(0, HALF, 2), :], ref[comp, pl.ds(1, HALF, 2), :]], axis=1
    )


def stacked(fields):
    return split_parts(jnp.concatenate([paired(ref, comp) for ref, comp in fields], axis=0))


def gather_lines(high, low, offsets, width):
    hits = wide_hits(offsets, width)
    tall = tall_hits(offsets, width)
    picked = jnp.dot(high, hits, preferred_element_type=F32)
    picked = picked + jnp.dot(low, hits, preferred_element_type=F32)
    return [
        jnp.sum(
            jnp.where(tall, picked[field * HALF : (field + 1) * HALF], 0.0), axis=0, keepdims=True
        )
        for field in range(picked.shape[0] // HALF)
    ]


TAKE = 4


def gather_drive(field_ref, placed, drives, first, high, low):
    high[...], low[...] = stacked([(field_ref, comp) for comp in range(3)])

    def group(index, carry):
        lines = placed[pl.ds(TAKE * index, TAKE)]
        offsets = jnp.concatenate([lines[slot : slot + 1] for slot in range(TAKE)], axis=1)
        got = gather_lines(high[...], low[...], offsets, TAKE * CZ)
        for comp in range(3):
            for slot in range(TAKE):
                drives[TAKE * index + slot, first + comp : first + comp + 1] = got[comp][
                    :, slot * CZ : (slot + 1) * CZ
                ]
        return carry

    lax.fori_loop(0, SLOTS // TAKE, group, 0)


def sample_rows(e_ref, h_ref, surf_ref, sampled):
    high, low = stacked([(ref, comp) for ref in (e_ref, h_ref) for comp in range(3)])
    got = gather_lines(high, low, surf_ref[...], CZ)
    sampled[...] = jnp.zeros_like(sampled)
    for field in range(6):
        sampled[field : field + 1] = got[field]


def drive_kernel(e_ref, h_ref, placed, surf_ref, before, drives, sampled, high, low):
    drives[...] = before[...]
    gather_drive(e_ref, placed, drives, 3, high, low)
    sample_rows(e_ref, h_ref, surf_ref, sampled)


def times(left, right):
    return (left[0] * right[0] - left[1] * right[1], left[1] * right[0] + left[0] * right[1])


def early_kernel(
    count_ref, owner_hbm, offsets_ref, e_ref, placed, drives, owner_ref, sem, high, low
):
    copy = pltpu.make_async_copy(owner_hbm, owner_ref, sem)
    copy.start()
    drives[...] = jnp.zeros_like(drives)
    copy.wait()
    count = count_ref[0]
    for slot in range(SLOTS):
        line = offsets_ref[slot : slot + 1]
        placed[pl.ds(owner_ref[0, slot], 1)] = jnp.where(slot < count, line, -1)
    gather_drive(e_ref, placed, drives, 0, high, low)


def phase_kernel(surf_ref, units_ref, surf_out, starts, turn, factors):
    lanes = lax.broadcasted_iota(jnp.int32, (8, DIRS), 1)
    omega = freq_low + freq_pitch * (lanes & (FREQ - 1)).astype(F32)
    moment = omega * jnp.where(lanes < FREQ, time_step, 2.0 * time_step)
    for place, value in enumerate((jnp.cos(moment), jnp.sin(moment))):
        factors[place] = jnp.transpose(jnp.broadcast_to(value[0:1], (DIRS, DIRS)))
    cells = surf_ref[...]
    surf_out[...] = cells
    rows = cells >> 7
    layer = (rows * 2731) >> 16
    cell_x = lax.axis_index("gx") * CX + layer
    cell_y = lax.axis_index("gy") * CY + (rows - CY * layer)
    cell_z = lax.axis_index("gz") * CZ + (cells & (CZ - 1))
    along = jnp.zeros((CZ, DIRS), F32)
    for axis, (cell, size) in enumerate(((cell_x, 128), (cell_y, 192), (cell_z, 256))):
        place = cell.astype(F32) - 0.5 * (size - 1)
        column = jnp.transpose(jnp.broadcast_to(place, (CZ, CZ)))
        along = along + column * units_ref[axis : axis + 1]
    angle = (0.25 * freq_pitch) * along
    square = angle * angle
    cosine = 1.0 + square * (
        -1 / 2 + square * (1 / 24 + square * (-1 / 720 + square * (1 / 40320)))
    )
    sine = angle * (
        1.0 + square * (-1 / 6 + square * (1 / 120 + square * (-1 / 5040 + square * (1 / 362880))))
    )
    two = times((cosine, sine), (cosine, sine))
    powers = {1: times(two, two)}
    for power in (2, 4, 8, 16, 32):
        powers[power] = times(powers[power // 2], powers[power // 2])
    low_start = times(times(powers[16], powers[8]), times(powers[4], powers[2]))
    high_start = times(low_start, powers[32])
    turn[0], turn[1] = powers[1]
    starts[0], starts[1] = low_start
    starts[2], starts[3] = high_start


FAR = 48
LOAD = 64
CELL = 16


def partner(step):
    index = lax.axis_index("gx")
    return (index >> 2) ^ step, (index & 3) ^ step


def fold_kernel(pieces, drives, total, *loads):
    total[...] = jnp.sum(pieces[...], axis=0)
    for step in (1, 2, 3):
        load = loads[step - 1]
        load[0:FAR] = total[...]
        load[FAR:] = drives[pl.ds(partner(step)[0], 1)][0]


def relay_kernel(total_in, drives, one, two, three, total, kept, *loads):
    arrived = (one, two, three)
    total[...] = (total_in[...] + one[0:FAR]) + (two[0:FAR] + three[0:FAR])
    own = partner(0)[0]
    for step in range(4):
        target = partner(step)[1]
        out, first = (kept, 0) if step == 0 else (loads[step - 1], FAR)
        if step:
            out[0:FAR] = total[...]
        spot = pl.multiple_of(target * CELL, CELL)
        for source in range(4):
            if source == 0:
                piece = drives[pl.ds(own, 1), pl.ds(spot, CELL)][0]
            else:
                piece = arrived[source - 1][pl.ds(FAR + spot, CELL)]
            out[first + source * CELL : first + (source + 1) * CELL] = piece


def finish_kernel(total_in, kept, one, two, three, spread_out, back):
    total = (total_in[...] + one[0:FAR]) + (two[0:FAR] + three[0:FAR])
    for peer in range(8):
        spread_out[peer] = total
    for step, arrived in enumerate((kept, one, two, three)):
        first = FAR if step else 0
        for source in range(4):
            brick = partner(source)[0] * 4 + partner(step)[1]
            start = first + source * CELL
            back[pl.ds(brick, 1)] = arrived[start : start + CELL][None]


def final_kernel(
    e_ref,
    h_ref,
    face_x,
    face_y,
    face_z,
    eps_ref,
    rates,
    dense,
    surf_ref,
    early_ref,
    starts,
    turn,
    factors,
    e_out,
    keep_out,
    send_out,
    late,
    now,
):
    curls = electric_curl(h_ref, face_x, face_y, face_z)
    scaled = time_step * eps_ref[...]
    later = dense[3] + (2.0 * time_step * cross_rate) * rates[3]
    for comp in range(3):
        field = e_ref[comp]
        polar = dense[comp] + time_step * rates[comp]
        rate = keep_rate * rates[comp] - spring * polar + gain_push * later * field
        e_out[comp] = field + scaled * (curls[comp] - rate)
    sample_rows(e_out, h_ref, surf_ref, late)
    scale = 1.0 / math.sqrt(STEPS * CZ * 256)
    high, low = split_parts(scale * jnp.concatenate([early_ref[...], late[...]], axis=0))
    left = jnp.concatenate(
        [
            jnp.concatenate([high, high], axis=1),
            jnp.concatenate([low, jnp.zeros_like(low)], axis=1),
        ],
        axis=0,
    )
    own = lax.axis_index("gz")
    for side, out in ((1, send_out), (0, keep_out)):
        target = lax.rem(own + side, 2)
        now[0] = starts[2 * target]
        now[1] = starts[2 * target + 1]
        for freq in range(FREQ // 2):
            here = (now[0], now[1])
            re_high, re_low = split_parts(here[0])
            im_high, im_low = split_parts(here[1])
            right = jnp.concatenate(
                [
                    jnp.concatenate([re_high, im_high], axis=1),
                    jnp.concatenate([re_low, im_low], axis=1),
                ],
                axis=0,
            )
            now[0], now[1] = times(here, (turn[0], turn[1]))
            both = jnp.dot(left, right, preferred_element_type=F32)
            both = both[0:16] + both[16:32]
            real = jnp.zeros((8, DIRS), F32)
            imag = jnp.zeros((8, DIRS), F32)
            for step in range(STEPS):
                row = pl.ds(step * FREQ + target * (FREQ // 2) + freq, 1)
                cosine = factors[0, row]
                sine = factors[1, row]
                upper = both[8 * step : 8 * step + 8, 0:DIRS]
                under = both[8 * step : 8 * step + 8, DIRS:]
                real = real + (cosine * upper + sine * under)
                imag = imag + (cosine * under - sine * upper)
            for comp in range(6):
                row = comp * (FREQ // 2) + freq
                out[row : row + 1] = real[comp : comp + 1]
                row = (comp + 6) * (FREQ // 2) + freq
                out[row : row + 1] = imag[comp : comp + 1]


def atoms_kernel(state_ref, pump_ref, drives, out):
    polar = [state_ref[c] for c in range(3)]
    rate = [state_ref[3 + c] for c in range(3)]
    ground, lower, lasing, upper = [state_ref[6 + level] for level in range(4)]
    pump = pump_ref[...]
    for step in range(STEPS):
        drive = [drives[:, 3 * step + c] for c in range(3)]
        inversion = lasing - lower
        power = jnp.zeros_like(pump)
        for c in range(3):
            rate[c] = (
                (1.0 - half) * rate[c]
                + time_step
                * (coupling * inversion * drive[c] - omega_rest * omega_rest * polar[c])
            ) / (1.0 + half)
            polar[c] = polar[c] + time_step * rate[c]
            power = power + drive[c] * rate[c]
        upper_new = upper + time_step * (pump * ground - upper / upper_life)
        lasing_new = lasing + time_step * (
            upper / upper_life - lasing / lasing_life + cross_rate * power
        )
        lower_new = lower + time_step * (
            lasing / lasing_life - lower / lower_life - cross_rate * power
        )
        ground = ground + time_step * (lower / lower_life - pump * ground)
        lower, lasing, upper = lower_new, lasing_new, upper_new
    for place, value in enumerate(polar + rate + [ground, lower, lasing, upper]):
        out[place] = value


def store_kernel(e_ref, h_ref, e_out, h_out):
    e_out[...] = e_ref[...]
    h_out[...] = h_ref[...]


def directions(count):
    index = np.arange(count, dtype=np.float32)
    cosine = np.float32(1.0) - np.float32(2.0) * (index + np.float32(0.5)) / np.float32(count)
    sine = np.sqrt(np.float32(1.0) - cosine * cosine)
    azimuth = (np.float32(golden) * index).astype(np.float64)
    rows = np.zeros((8, count), np.float32)
    rows[0] = sine * np.cos(azimuth).astype(np.float32)
    rows[1] = sine * np.sin(azimuth).astype(np.float32)
    rows[2] = cosine
    return rows


def local(
    efield,
    hfield,
    inv_eps,
    gain_state,
    pump,
    gain_offsets,
    gain_count,
    block_owner,
    surf_offsets,
    far_acc,
):
    state = jnp.transpose(gain_state.reshape(SLOTS, 10, CZ), (1, 0, 2))
    dense = shape(3, ROWS, CZ)
    faces = (shape(2, CY, CZ), shape(2, CX, CZ), shape(2, ROWS, CZ))
    down = [[((i + 1) % n, i) for i in range(n)] for n in (16, 8, 2)]
    up = [[(i, (i + 1) % n) for i in range(n)] for n in (16, 8, 2)]
    vmem = pl.BlockSpec(memory_space=pltpu.VMEM)

    hbm = pl.BlockSpec(memory_space=pltpu.HBM)

    def shifted(parts, perms):
        return [
            lax.ppermute(part, axis, perm)
            for part, axis, perm in zip(parts, ("gx", "gy", "gz"), perms)
        ]

    *near, packed, e_old, h_old, eps = call(
        prepare_kernel,
        faces + (shape(SLOTS // 2, 16, CZ), dense, dense, shape(ROWS, CZ)),
        stay(
            efield.reshape(3, ROWS, CZ),
            state,
            hfield.reshape(3, ROWS, CZ),
            inv_eps.reshape(ROWS, CZ),
        ),
        in_specs=[hbm] * 4,
        scratch=[pltpu.VMEM((10, SLOTS, CZ), F32), pltpu.SemaphoreType.DMA((4,))],
        name="prepare",
    )
    near = shifted(near, down)
    fields = lax.all_to_all(packed, "gx", 0, 0, tiled=True)
    halves = [pltpu.VMEM((3 * HALF, WIDE), BF16)] * 2
    placed, before = call(
        early_kernel,
        (shape(SLOTS, CZ, dtype=jnp.int32), shape(SLOTS, 8, CZ)),
        [gain_count.reshape(1)]
        + stay(block_owner.reshape(1, SLOTS), gain_offsets.reshape(SLOTS, CZ))
        + [e_old],
        in_specs=[pl.BlockSpec(memory_space=pltpu.SMEM), hbm, vmem, vmem],
        scratch=[pltpu.SMEM((1, SLOTS), jnp.int32), pltpu.SemaphoreType.DMA] + halves,
        name="early",
    )
    *near, placed = lax.optimization_barrier((*near, placed))
    h_one, *edge = call(magnetic_kernel, (dense,) + faces, (e_old, h_old, *near), name="magnetic")
    edge = shifted(edge, up)
    spread_now = scattered(0, placed, fields, "scatter")
    surf, starts, turn, factors = call(
        phase_kernel,
        (
            shape(1, CZ, dtype=jnp.int32),
            shape(4, CZ, DIRS),
            shape(2, CZ, DIRS),
            shape(2, STEPS * FREQ, DIRS),
        ),
        stay(surf_offsets.reshape(1, CZ), jnp.asarray(directions(DIRS))),
        name="phase",
    )
    *edge, surf = lax.optimization_barrier((*edge, surf))
    e_one, *near, rates = call(
        electric_kernel,
        (dense,) + faces + (shape(4, ROWS, CZ),),
        (e_old, h_one, *edge, eps, spread_now),
        name="electric",
    )
    near = shifted(near, down)
    drives, early = call(
        drive_kernel,
        (shape(SLOTS, 8, CZ), shape(8, CZ)),
        (e_one, h_one, placed, surf, before),
        scratch=halves,
        name="drive",
    )
    *near, early = lax.optimization_barrier((*near, early))
    h_two, *edge = call(magnetic_kernel, (dense,) + faces, (e_one, h_one, *near), name="magnetic2")
    edge = shifted(edge, up)
    placed, fields, early = lax.optimization_barrier((placed, fields, early))
    spread_next = scattered(4, placed, fields, "scatter2")
    part = shape(12 * FREQ // 2, DIRS)
    e_two, keep, send = call(
        final_kernel,
        (dense, part, part),
        (e_one, h_two, *edge, eps, rates, spread_next, surf, early, starts, turn, factors),
        scratch=[pltpu.VMEM((8, CZ), F32), pltpu.VMEM((2, CZ, DIRS), F32)],
        name="final",
    )
    chip = keep + lax.ppermute(send, "gz", down[2])
    pieces = lax.all_to_all(chip.reshape(8, FAR, DIRS), "gy", 0, 0, tiled=True)
    drives = drives.reshape(4, LOAD, CZ)
    load = shape(FAR + LOAD, CZ)
    total, *loads = call(
        fold_kernel, (shape(FAR, DIRS),) + (load,) * 3, (pieces, drives), name="fold"
    )
    loads = [
        lax.ppermute(
            value, "gx", [(a * 4 + z, (a ^ k) * 4 + z) for a in range(4) for z in range(4)]
        )
        for k, value in enumerate(loads, 1)
    ]
    total, kept, *loads = call(
        relay_kernel,
        (shape(FAR, DIRS), shape(LOAD, CZ)) + (load,) * 3,
        (total, drives, *loads),
        name="relay",
    )
    loads = [
        lax.ppermute(
            value, "gx", [(a * 4 + z, a * 4 + (z ^ k)) for a in range(4) for z in range(4)]
        )
        for k, value in enumerate(loads, 1)
    ]
    e_out, h_out = call(store_kernel, (dense, dense), (e_two, h_two), name="store")
    copies, back = call(
        finish_kernel,
        (shape(8, FAR, DIRS), shape(SLOTS // 2, CELL, CZ)),
        (total, kept, *loads),
        name="finish",
    )
    state_out = call(
        atoms_kernel,
        shape(10, SLOTS, CZ),
        (state, pump.reshape(SLOTS, CZ), back.reshape(SLOTS, 8, CZ)),
        name="atoms",
    )
    copies, state_out, e_out, h_out = lax.optimization_barrier((copies, state_out, e_out, h_out))
    gathered = lax.all_to_all(copies, "gy", 0, 0, tiled=True)
    far_out = far_acc + jnp.transpose(gathered.reshape(12, FREQ // 2, DIRS), (1, 0, 2))
    return (
        e_out.reshape(efield.shape),
        h_out.reshape(hfield.shape),
        jnp.transpose(state_out, (1, 0, 2)).reshape(gain_state.shape),
        far_out,
    )


def solution(mesh):
    placed = (
        P(None, "gx", "gy", "gz"),
        P(None, "gx", "gy", "gz"),
        P("gx", "gy", "gz"),
        P("gx", "gy", "gz", None, None, None),
        P("gx", "gy", "gz", None, None),
        P("gx", "gy", "gz", None, None),
        P("gx", "gy", "gz"),
        P("gx", "gy", "gz", None),
        P("gx", "gy", "gz", None),
        P("gz", None, None),
    )
    return jax.shard_map(
        local,
        mesh=mesh,
        in_specs=placed,
        out_specs=(
            P(None, "gx", "gy", "gz"),
            P(None, "gx", "gy", "gz"),
            P("gx", "gy", "gz", None, None, None),
            P("gz", None, None),
        ),
        check_vma=False,
    )
```

```python
import functools
import math

import jax
import jax.numpy as jnp
import numpy as np
from jax import lax
from jax.experimental import pallas as pl
from jax.experimental.pallas import tpu as pltpu
from jax.sharding import PartitionSpec as P

FREQ = 64
STEPS = 2
CX = 8
CY = 24
CZ = 128
ROWS = CX * CY
SLOTS = 32
DIRS = 128

time_step = 0.5
damping = 0.1
omega_rest = 1.0
coupling = 0.5
cross_rate = 0.3
upper_life = 2.0
lasing_life = 20.0
lower_life = 2.0
freq_low = 0.3
freq_pitch = 0.01
golden = 2.399963229728653

half = 0.5 * damping * time_step
keep_rate = (1.0 - half) / (1.0 + half)
spring = time_step * omega_rest * omega_rest / (1.0 + half)
gain_push = time_step * coupling / (1.0 + half)

F32 = jnp.float32
BF16 = jnp.bfloat16
MIB = 1 << 20


def shape(*dims, dtype=F32):
    return jax.ShapeDtypeStruct(dims, dtype)


def call(kernel, outs, args, in_specs=None, scratch=(), vmem=16, flops=0, moved=2 * MIB, name=None):
    return pl.pallas_call(
        kernel,
        out_shape=outs,
        in_specs=in_specs or [pl.BlockSpec(memory_space=pltpu.VMEM)] * len(args),
        scratch_shapes=scratch,
        compiler_params=pltpu.CompilerParams(vmem_limit_bytes=vmem * MIB),
        cost_estimate=pl.CostEstimate(flops=flops, bytes_accessed=moved, transcendentals=0),
        name=name,
    )(*args)


def stay(*values):
    return [pltpu.with_memory_space_constraint(value, pltpu.HBM) for value in values]


def split_parts(value):
    high = value.astype(BF16)
    low = (value - high.astype(F32)).astype(BF16)
    return high, low


def row_index(count, width):
    return lax.broadcasted_iota(jnp.int32, (count, width), 0)


def lane_index(count):
    return lax.broadcasted_iota(jnp.int32, (count, CZ), 1)


def ahead_x(field, face):
    return jnp.concatenate([field[CY:], face], axis=0)


def behind_x(field, face):
    return jnp.concatenate([face, field[:-CY]], axis=0)


def spread(face):
    return jnp.broadcast_to(face[:, None, :], (CX, CY, CZ)).reshape(ROWS, CZ)


def ahead_y(field, face, last):
    return jnp.where(last, spread(face), pltpu.roll(field, ROWS - 1, 0))


def behind_y(field, face, first):
    return jnp.where(first, spread(face), pltpu.roll(field, 1, 0))


def ahead_z(field, other, lane):
    return pltpu.roll(jnp.where(lane == 0, other, field), CZ - 1, 1)


def behind_z(field, other, lane):
    return pltpu.roll(jnp.where(lane == CZ - 1, other, field), 1, 1)


def row_in_brick():
    rows = row_index(ROWS, CZ)
    return rows - CY * ((rows * 2731) >> 16)


def first_layers(field_ref, out_x, out_y, out_z):
    out_x[0] = field_ref[1, 0:CY]
    out_x[1] = field_ref[2, 0:CY]
    for place, comp in ((0, 0), (1, 2)):
        for layer in range(CX):
            out_y[place, layer : layer + 1] = field_ref[comp, layer * CY : layer * CY + 1]
    out_z[0] = field_ref[0]
    out_z[1] = field_ref[1]


def last_layers(field_ref, out_x, out_y, out_z):
    out_x[0] = field_ref[1, ROWS - CY : ROWS]
    out_x[1] = field_ref[2, ROWS - CY : ROWS]
    for place, comp in ((0, 0), (1, 2)):
        for layer in range(CX):
            row = layer * CY + CY - 1
            out_y[place, layer : layer + 1] = field_ref[comp, row : row + 1]
    out_z[0] = field_ref[0]
    out_z[1] = field_ref[1]


def inside(faces, ahead):
    kept = []
    for face, axis in zip(faces, ("gx", "gy", "gz")):
        index = lax.axis_index(axis)
        real = index < lax.axis_size(axis) - 1 if ahead else index > 0
        kept.append([jnp.where(real, face[place], 0.0) for place in range(2)])
    return kept


def prepare_kernel(
    e_hbm,
    state_hbm,
    h_hbm,
    eps_hbm,
    pump_hbm,
    out_x,
    out_y,
    out_z,
    packed,
    e_out,
    state,
    h_out,
    eps_out,
    pump_out,
    sems,
):
    copies = [
        pltpu.make_async_copy(source, target, sems.at[place])
        for place, (source, target) in enumerate(
            (
                (e_hbm, e_out),
                (state_hbm, state),
                (h_hbm, h_out),
                (eps_hbm, eps_out),
                (pump_hbm, pump_out),
            )
        )
    ]
    for copy in copies:
        copy.start()
    copies[0].wait()
    first_layers(e_out, out_x, out_y, out_z)
    copies[1].wait()
    lower, lasing, upper = state[7], state[8], state[9]
    lasing_free = lasing + time_step * (upper / upper_life - lasing / lasing_life)
    lower_free = lower + time_step * (lasing / lasing_life - lower / lower_life)
    polar = [state[comp] for comp in range(3)]
    free = [keep_rate * state[3 + comp] - spring * polar[comp] for comp in range(3)]
    for field, value in enumerate(free + [lasing - lower] + polar + [lasing_free - lower_free]):
        for owner in range(SLOTS // 2):
            packed[owner, 2 * field : 2 * field + 2] = value[2 * owner : 2 * owner + 2]
    for copy in copies[2:]:
        copy.wait()


def magnetic_kernel(e_ref, h_ref, face_x, face_y, face_z, h_out, out_x, out_y, out_z):
    lane = lane_index(ROWS)
    last = row_in_brick() == CY - 1
    face_x, face_y, face_z = inside((face_x, face_y, face_z), True)
    ex, ey, ez = e_ref[0], e_ref[1], e_ref[2]
    first = (ahead_y(ez, face_y[1], last) - ez) - (ahead_z(ey, face_z[1], lane) - ey)
    second = (ahead_z(ex, face_z[0], lane) - ex) - (ahead_x(ez, face_x[1]) - ez)
    third = (ahead_x(ey, face_x[0]) - ey) - (ahead_y(ex, face_y[0], last) - ex)
    h_out[0] = h_ref[0] - time_step * first
    h_out[1] = h_ref[1] - time_step * second
    h_out[2] = h_ref[2] - time_step * third
    last_layers(h_out, out_x, out_y, out_z)


def electric_curl(h_ref, face_x, face_y, face_z):
    lane = lane_index(ROWS)
    start = row_in_brick() == 0
    face_x, face_y, face_z = inside((face_x, face_y, face_z), False)
    hx, hy, hz = h_ref[0], h_ref[1], h_ref[2]
    first = (hz - behind_y(hz, face_y[1], start)) - (hy - behind_z(hy, face_z[1], lane))
    second = (hx - behind_z(hx, face_z[0], lane)) - (hz - behind_x(hz, face_x[1]))
    third = (hy - behind_x(hy, face_x[0])) - (hx - behind_y(hx, face_y[0], start))
    return first, second, third


HALF = ROWS // 2
WIDE = 2 * CZ


def wide_hits(offsets, width):
    hits = row_index(WIDE, width) == (offsets & (WIDE - 1))
    return hits.astype(F32).astype(BF16)


def tall_hits(offsets, width):
    return row_index(HALF, width) == (offsets >> 8)


GROUP = 16


def scatter_kernel(first, placed, fields_ref, dense, total, spots, columns):
    def group(index, carry):
        lines = placed[pl.ds(GROUP * index, GROUP)]
        for slot in range(GROUP):
            line = lines[slot : slot + 1]
            hits = wide_hits(line, CZ)
            tall = tall_hits(line, CZ).astype(F32).astype(BF16).reshape(6, 16, CZ)
            values = fields_ref[
                (GROUP // 2) * index + slot // 2, pl.ds(2 * first + slot % 2, 4, 2), :
            ]
            for place, part in enumerate(split_parts(values)):
                across = (place * GROUP + slot) * CZ
                columns[:, across : across + CZ] = hits
                part = part.astype(F32)
                for field in range(4):
                    row = jnp.broadcast_to(part[field : field + 1], (16, CZ)).astype(BF16)
                    spots[field * HALF : (field + 1) * HALF, across : across + CZ] = (
                        tall * row[None]
                    ).reshape(HALF, CZ)
        got = lax.dot_general(
            spots[...], columns[...], (((1,), (1,)), ((), ())), preferred_element_type=F32
        )

        @pl.when(index == 0)
        def _():
            total[...] = got

        @pl.when(index > 0)
        def _():
            total[...] += got

        return carry

    lax.fori_loop(0, SLOTS // GROUP, group, 0)
    for field in range(4):
        got = total[field * HALF : (field + 1) * HALF]
        dense[field, pl.ds(0, HALF, 2), :] = got[:, :CZ]
        dense[field, pl.ds(1, HALF, 2), :] = got[:, CZ:]


def scattered(first, placed, fields, name):
    return call(
        functools.partial(scatter_kernel, first),
        shape(4, ROWS, CZ),
        (placed, fields),
        scratch=[
            pltpu.VMEM((4 * HALF, WIDE), F32),
            pltpu.VMEM((4 * HALF, 2 * GROUP * CZ), BF16),
            pltpu.VMEM((WIDE, 2 * GROUP * CZ), BF16),
        ],
        name=name,
    )


def electric_kernel(
    e_ref, h_ref, face_x, face_y, face_z, eps_ref, dense, e_out, out_x, out_y, out_z, rates
):
    curls = electric_curl(h_ref, face_x, face_y, face_z)
    scaled = time_step * eps_ref[...]
    inversion = dense[3]
    power = jnp.zeros_like(inversion)
    for comp in range(3):
        field = e_ref[comp]
        rate = dense[comp] + gain_push * inversion * field
        power = power + field * rate
        rates[comp] = rate
        e_out[comp] = field + scaled * (curls[comp] - rate)
    rates[3] = power
    first_layers(e_out, out_x, out_y, out_z)


def paired(ref, comp):
    return jnp.concatenate(
        [ref[comp, pl.ds(0, HALF, 2), :], ref[comp, pl.ds(1, HALF, 2), :]], axis=1
    )


def stacked(fields):
    return split_parts(jnp.concatenate([paired(ref, comp) for ref, comp in fields], axis=0))


def gather_lines(high, low, offsets, width):
    hits = wide_hits(offsets, width)
    tall = tall_hits(offsets, width)
    picked = jnp.dot(high, hits, preferred_element_type=F32)
    picked = picked + jnp.dot(low, hits, preferred_element_type=F32)
    return [
        jnp.sum(
            jnp.where(tall, picked[field * HALF : (field + 1) * HALF], 0.0), axis=0, keepdims=True
        )
        for field in range(picked.shape[0] // HALF)
    ]


TAKE = 8


def drive_kernel(e_old, e_new, placed, drives, high, low):
    high[...], low[...] = stacked([(ref, comp) for ref in (e_old, e_new) for comp in range(3)])
    drives[...] = jnp.zeros_like(drives)

    def group(index, carry):
        lines = placed[pl.ds(TAKE * index, TAKE)]
        offsets = jnp.concatenate([lines[slot : slot + 1] for slot in range(TAKE)], axis=1)
        got = gather_lines(high[...], low[...], offsets, TAKE * CZ)
        for field in range(6):
            for slot in range(TAKE):
                drives[TAKE * index + slot, field : field + 1] = got[field][
                    :, slot * CZ : (slot + 1) * CZ
                ]
        return carry

    lax.fori_loop(0, SLOTS // TAKE, group, 0)


def sample_rows(e_ref, h_ref, surf_ref, sampled):
    high, low = stacked([(ref, comp) for ref in (e_ref, h_ref) for comp in range(3)])
    got = gather_lines(high, low, surf_ref[...], CZ)
    sampled[...] = jnp.zeros_like(sampled)
    for field in range(6):
        sampled[field : field + 1] = got[field]


def times(left, right):
    return (left[0] * right[0] - left[1] * right[1], left[1] * right[0] + left[0] * right[1])


def phase_kernel(
    count_ref,
    owner_hbm,
    offsets_ref,
    surf_ref,
    units_ref,
    placed,
    surf_out,
    starts,
    turn,
    factors,
    owner_ref,
    sem,
):
    copy = pltpu.make_async_copy(owner_hbm, owner_ref, sem)
    copy.start()
    lanes = lax.broadcasted_iota(jnp.int32, (8, DIRS), 1)
    omega = freq_low + freq_pitch * (lanes & (FREQ - 1)).astype(F32)
    moment = omega * jnp.where(lanes < FREQ, time_step, 2.0 * time_step)
    for place, value in enumerate((jnp.cos(moment), jnp.sin(moment))):
        factors[place] = jnp.transpose(jnp.broadcast_to(value[0:1], (DIRS, DIRS)))
    cells = surf_ref[...]
    surf_out[...] = cells
    rows = cells >> 7
    layer = (rows * 2731) >> 16
    cell_x = lax.axis_index("gx") * CX + layer
    cell_y = lax.axis_index("gy") * CY + (rows - CY * layer)
    cell_z = lax.axis_index("gz") * CZ + (cells & (CZ - 1))
    along = jnp.zeros((CZ, DIRS), F32)
    for axis, (cell, size) in enumerate(((cell_x, 128), (cell_y, 192), (cell_z, 256))):
        place = cell.astype(F32) - 0.5 * (size - 1)
        column = jnp.transpose(jnp.broadcast_to(place, (CZ, CZ)))
        along = along + column * units_ref[axis : axis + 1]
    angle = (0.25 * freq_pitch) * along
    square = angle * angle
    cosine = 1.0 + square * (
        -1 / 2 + square * (1 / 24 + square * (-1 / 720 + square * (1 / 40320)))
    )
    sine = angle * (
        1.0 + square * (-1 / 6 + square * (1 / 120 + square * (-1 / 5040 + square * (1 / 362880))))
    )
    two = times((cosine, sine), (cosine, sine))
    powers = {1: times(two, two)}
    for power in (2, 4, 8, 16, 32):
        powers[power] = times(powers[power // 2], powers[power // 2])
    low_start = times(times(powers[16], powers[8]), times(powers[4], powers[2]))
    high_start = times(low_start, powers[32])
    turn[0], turn[1] = powers[1]
    starts[0], starts[1] = low_start
    starts[2], starts[3] = high_start
    copy.wait()
    count = count_ref[0]
    for slot in range(SLOTS):
        line = offsets_ref[slot : slot + 1]
        placed[pl.ds(owner_ref[0, slot], 1)] = jnp.where(slot < count, line, -1)


FAR = 48
LOAD = 64
CELL = 16


def partner(step):
    index = lax.axis_index("gx")
    return (index >> 2) ^ step, (index & 3) ^ step


def fold_kernel(pieces, drives, total, *loads):
    total[...] = jnp.sum(pieces[...], axis=0)
    for step in (1, 2, 3):
        load = loads[step - 1]
        load[0:FAR] = total[...]
        load[FAR:] = drives[pl.ds(partner(step)[0], 1)][0]


def relay_kernel(total_in, drives, one, two, three, total, kept, *loads):
    arrived = (one, two, three)
    total[...] = (total_in[...] + one[0:FAR]) + (two[0:FAR] + three[0:FAR])
    own = partner(0)[0]
    for step in range(4):
        target = partner(step)[1]
        out, first = (kept, 0) if step == 0 else (loads[step - 1], FAR)
        if step:
            out[0:FAR] = total[...]
        spot = pl.multiple_of(target * CELL, CELL)
        for source in range(4):
            if source == 0:
                piece = drives[pl.ds(own, 1), pl.ds(spot, CELL)][0]
            else:
                piece = arrived[source - 1][pl.ds(FAR + spot, CELL)]
            out[first + source * CELL : first + (source + 1) * CELL] = piece


def finish_kernel(total_in, kept, one, two, three, spread_out, back):
    total = (total_in[...] + one[0:FAR]) + (two[0:FAR] + three[0:FAR])
    for peer in range(8):
        spread_out[peer] = total
    for step, arrived in enumerate((kept, one, two, three)):
        first = FAR if step else 0
        for source in range(4):
            brick = partner(source)[0] * 4 + partner(step)[1]
            start = first + source * CELL
            back[pl.ds(brick, 1)] = arrived[start : start + CELL][None]


def final_kernel(
    e_ref,
    h_ref,
    face_x,
    face_y,
    face_z,
    eps_ref,
    rates,
    dense,
    surf_ref,
    early_ref,
    starts,
    turn,
    factors,
    e_out,
    keep_out,
    send_out,
    late,
    now,
):
    curls = electric_curl(h_ref, face_x, face_y, face_z)
    scaled = time_step * eps_ref[...]
    later = dense[3] + (2.0 * time_step * cross_rate) * rates[3]
    for comp in range(3):
        field = e_ref[comp]
        polar = dense[comp] + time_step * rates[comp]
        rate = keep_rate * rates[comp] - spring * polar + gain_push * later * field
        e_out[comp] = field + scaled * (curls[comp] - rate)
    sample_rows(e_out, h_ref, surf_ref, late)
    scale = 1.0 / math.sqrt(STEPS * CZ * 256)
    high, low = split_parts(scale * jnp.concatenate([early_ref[...], late[...]], axis=0))
    left = jnp.concatenate(
        [
            jnp.concatenate([high, high], axis=1),
            jnp.concatenate([low, jnp.zeros_like(low)], axis=1),
        ],
        axis=0,
    )
    own = lax.axis_index("gz")
    for side, out in ((1, send_out), (0, keep_out)):
        target = lax.rem(own + side, 2)
        now[0] = starts[2 * target]
        now[1] = starts[2 * target + 1]
        for freq in range(FREQ // 2):
            here = (now[0], now[1])
            re_high, re_low = split_parts(here[0])
            im_high, im_low = split_parts(here[1])
            right = jnp.concatenate(
                [
                    jnp.concatenate([re_high, im_high], axis=1),
                    jnp.concatenate([re_low, im_low], axis=1),
                ],
                axis=0,
            )
            now[0], now[1] = times(here, (turn[0], turn[1]))
            both = jnp.dot(left, right, preferred_element_type=F32)
            both = both[0:16] + both[16:32]
            real = jnp.zeros((8, DIRS), F32)
            imag = jnp.zeros((8, DIRS), F32)
            for step in range(STEPS):
                row = pl.ds(step * FREQ + target * (FREQ // 2) + freq, 1)
                cosine = factors[0, row]
                sine = factors[1, row]
                upper = both[8 * step : 8 * step + 8, 0:DIRS]
                under = both[8 * step : 8 * step + 8, DIRS:]
                real = real + (cosine * upper + sine * under)
                imag = imag + (cosine * under - sine * upper)
            for comp in range(6):
                row = comp * (FREQ // 2) + freq
                out[row : row + 1] = real[comp : comp + 1]
                row = (comp + 6) * (FREQ // 2) + freq
                out[row : row + 1] = imag[comp : comp + 1]


def atoms_kernel(state_ref, pump_ref, drives, out):
    polar = [state_ref[c] for c in range(3)]
    rate = [state_ref[3 + c] for c in range(3)]
    ground, lower, lasing, upper = [state_ref[6 + level] for level in range(4)]
    pump = pump_ref[...]
    for step in range(STEPS):
        drive = [drives[:, 3 * step + c] for c in range(3)]
        inversion = lasing - lower
        power = jnp.zeros_like(pump)
        for c in range(3):
            rate[c] = (
                (1.0 - half) * rate[c]
                + time_step
                * (coupling * inversion * drive[c] - omega_rest * omega_rest * polar[c])
            ) / (1.0 + half)
            polar[c] = polar[c] + time_step * rate[c]
            power = power + drive[c] * rate[c]
        upper_new = upper + time_step * (pump * ground - upper / upper_life)
        lasing_new = lasing + time_step * (
            upper / upper_life - lasing / lasing_life + cross_rate * power
        )
        lower_new = lower + time_step * (
            lasing / lasing_life - lower / lower_life - cross_rate * power
        )
        ground = ground + time_step * (lower / lower_life - pump * ground)
        lower, lasing, upper = lower_new, lasing_new, upper_new
    for place, value in enumerate(polar + rate + [ground, lower, lasing, upper]):
        out[place] = value


def store_kernel(e_ref, h_ref, e_out, h_out):
    e_out[...] = e_ref[...]
    h_out[...] = h_ref[...]


def directions(count):
    index = np.arange(count, dtype=np.float32)
    cosine = np.float32(1.0) - np.float32(2.0) * (index + np.float32(0.5)) / np.float32(count)
    sine = np.sqrt(np.float32(1.0) - cosine * cosine)
    azimuth = (np.float32(golden) * index).astype(np.float64)
    rows = np.zeros((8, count), np.float32)
    rows[0] = sine * np.cos(azimuth).astype(np.float32)
    rows[1] = sine * np.sin(azimuth).astype(np.float32)
    rows[2] = cosine
    return rows


def local(
    efield,
    hfield,
    inv_eps,
    gain_state,
    pump,
    gain_offsets,
    gain_count,
    block_owner,
    surf_offsets,
    far_acc,
):
    dense = shape(3, ROWS, CZ)
    faces = (shape(2, CY, CZ), shape(2, CX, CZ), shape(2, ROWS, CZ))
    down = [[((i + 1) % n, i) for i in range(n)] for n in (16, 8, 2)]
    up = [[(i, (i + 1) % n) for i in range(n)] for n in (16, 8, 2)]
    vmem = pl.BlockSpec(memory_space=pltpu.VMEM)

    hbm = pl.BlockSpec(memory_space=pltpu.HBM)

    def shifted(parts, perms):
        return [
            lax.ppermute(part, axis, perm)
            for part, axis, perm in zip(parts, ("gx", "gy", "gz"), perms)
        ]

    *near, packed, e_old, state, h_old, eps, pumps = call(
        prepare_kernel,
        faces
        + (
            shape(SLOTS // 2, 16, CZ),
            dense,
            shape(10, SLOTS, CZ),
            dense,
            shape(ROWS, CZ),
            shape(SLOTS, CZ),
        ),
        stay(
            efield.reshape(3, ROWS, CZ),
            jnp.transpose(gain_state.reshape(SLOTS, 10, CZ), (1, 0, 2)),
            hfield.reshape(3, ROWS, CZ),
            inv_eps.reshape(ROWS, CZ),
            pump.reshape(SLOTS, CZ),
        ),
        in_specs=[hbm] * 5,
        scratch=[pltpu.SemaphoreType.DMA((5,))],
        name="prepare",
    )
    near = shifted(near, down)
    fields = lax.all_to_all(packed, "gx", 0, 0, tiled=True)
    placed, surf, starts, turn, factors = call(
        phase_kernel,
        (
            shape(SLOTS, CZ, dtype=jnp.int32),
            shape(1, CZ, dtype=jnp.int32),
            shape(4, CZ, DIRS),
            shape(2, CZ, DIRS),
            shape(2, STEPS * FREQ, DIRS),
        ),
        [gain_count.reshape(1)]
        + stay(
            block_owner.reshape(1, SLOTS),
            gain_offsets.reshape(SLOTS, CZ),
            surf_offsets.reshape(1, CZ),
            jnp.asarray(directions(DIRS)),
        ),
        in_specs=[pl.BlockSpec(memory_space=pltpu.SMEM), hbm, vmem, vmem, vmem],
        scratch=[pltpu.SMEM((1, SLOTS), jnp.int32), pltpu.SemaphoreType.DMA],
        name="phase",
    )
    *near, placed = lax.optimization_barrier((*near, placed))
    h_one, *edge = call(magnetic_kernel, (dense,) + faces, (e_old, h_old, *near), name="magnetic")
    edge = shifted(edge, up)
    spread_now = scattered(0, placed, fields, "scatter")
    e_one, *near, rates = call(
        electric_kernel,
        (dense,) + faces + (shape(4, ROWS, CZ),),
        (e_old, h_one, *edge, eps, spread_now),
        name="electric",
    )
    near = shifted(near, down)
    spread_next = scattered(4, placed, fields, "scatter2")
    *near, spread_next = lax.optimization_barrier((*near, spread_next))
    h_two, *edge = call(magnetic_kernel, (dense,) + faces, (e_one, h_one, *near), name="magnetic2")
    edge = shifted(edge, up)
    e_seen, h_seen, h_two = lax.optimization_barrier((e_one, h_one, h_two))
    early = call(sample_rows, shape(8, CZ), (e_seen, h_seen, surf), name="sample")
    part = shape(12 * FREQ // 2, DIRS)
    e_two, keep, send = call(
        final_kernel,
        (dense, part, part),
        (e_one, h_two, *edge, eps, rates, spread_next, surf, early, starts, turn, factors),
        scratch=[pltpu.VMEM((8, CZ), F32), pltpu.VMEM((2, CZ, DIRS), F32)],
        name="final",
    )
    chip = keep + lax.ppermute(send, "gz", down[2])
    chip, e_seen = lax.optimization_barrier((chip, e_one))
    pieces = lax.all_to_all(chip.reshape(8, FAR, DIRS), "gy", 0, 0, tiled=True)
    drives = call(
        drive_kernel,
        shape(SLOTS, 8, CZ),
        (e_old, e_seen, placed),
        scratch=[pltpu.VMEM((6 * HALF, WIDE), BF16)] * 2,
        name="drive",
    ).reshape(4, LOAD, CZ)
    load = shape(FAR + LOAD, CZ)
    total, *loads = call(
        fold_kernel, (shape(FAR, DIRS),) + (load,) * 3, (pieces, drives), name="fold"
    )
    loads = [
        lax.ppermute(
            value, "gx", [(a * 4 + z, (a ^ k) * 4 + z) for a in range(4) for z in range(4)]
        )
        for k, value in enumerate(loads, 1)
    ]
    total, kept, *loads = call(
        relay_kernel,
        (shape(FAR, DIRS), shape(LOAD, CZ)) + (load,) * 3,
        (total, drives, *loads),
        name="relay",
    )
    loads = [
        lax.ppermute(
            value, "gx", [(a * 4 + z, a * 4 + (z ^ k)) for a in range(4) for z in range(4)]
        )
        for k, value in enumerate(loads, 1)
    ]
    e_out, h_out = call(store_kernel, (dense, dense), (e_two, h_two), name="store")
    copies, back = call(
        finish_kernel,
        (shape(8, FAR, DIRS), shape(SLOTS // 2, CELL, CZ)),
        (total, kept, *loads),
        name="finish",
    )
    state_out = call(
        atoms_kernel,
        shape(10, SLOTS, CZ),
        (state, pumps, back.reshape(SLOTS, 8, CZ)),
        name="atoms",
    )
    copies, state_out, e_out, h_out = lax.optimization_barrier((copies, state_out, e_out, h_out))
    gathered = lax.all_to_all(copies, "gy", 0, 0, tiled=True)
    far_out = far_acc + jnp.transpose(gathered.reshape(12, FREQ // 2, DIRS), (1, 0, 2))
    return (
        e_out.reshape(efield.shape),
        h_out.reshape(hfield.shape),
        jnp.transpose(state_out, (1, 0, 2)).reshape(gain_state.shape),
        far_out,
    )


def solution(mesh):
    placed = (
        P(None, "gx", "gy", "gz"),
        P(None, "gx", "gy", "gz"),
        P("gx", "gy", "gz"),
        P("gx", "gy", "gz", None, None, None),
        P("gx", "gy", "gz", None, None),
        P("gx", "gy", "gz", None, None),
        P("gx", "gy", "gz"),
        P("gx", "gy", "gz", None),
        P("gx", "gy", "gz", None),
        P("gz", None, None),
    )
    return jax.shard_map(
        local,
        mesh=mesh,
        in_specs=placed,
        out_specs=(
            P(None, "gx", "gy", "gz"),
            P(None, "gx", "gy", "gz"),
            P("gx", "gy", "gz", None, None, None),
            P("gz", None, None),
        ),
        check_vma=False,
    )
```

```python
import functools
import math

import jax
import jax.numpy as jnp
import numpy as np
from jax import lax
from jax.experimental import pallas as pl
from jax.experimental.pallas import tpu as pltpu
from jax.sharding import PartitionSpec as P

FREQ = 64
STEPS = 2
CX = 8
CY = 24
CZ = 128
ROWS = CX * CY
SLOTS = 32
DIRS = 128

time_step = 0.5
damping = 0.1
omega_rest = 1.0
coupling = 0.5
cross_rate = 0.3
upper_life = 2.0
lasing_life = 20.0
lower_life = 2.0
freq_low = 0.3
freq_pitch = 0.01
golden = 2.399963229728653

half = 0.5 * damping * time_step
keep_rate = (1.0 - half) / (1.0 + half)
spring = time_step * omega_rest * omega_rest / (1.0 + half)
gain_push = time_step * coupling / (1.0 + half)

F32 = jnp.float32
BF16 = jnp.bfloat16
MIB = 1 << 20


def shape(*dims, dtype=F32):
    return jax.ShapeDtypeStruct(dims, dtype)


def call(kernel, outs, args, in_specs=None, scratch=(), vmem=16, flops=0, moved=2 * MIB, name=None):
    return pl.pallas_call(
        kernel,
        out_shape=outs,
        in_specs=in_specs or [pl.BlockSpec(memory_space=pltpu.VMEM)] * len(args),
        scratch_shapes=scratch,
        compiler_params=pltpu.CompilerParams(vmem_limit_bytes=vmem * MIB),
        cost_estimate=pl.CostEstimate(flops=flops, bytes_accessed=moved, transcendentals=0),
        name=name,
    )(*args)


def stay(*values):
    return [pltpu.with_memory_space_constraint(value, pltpu.HBM) for value in values]


def split_parts(value):
    high = value.astype(BF16)
    low = (value - high.astype(F32)).astype(BF16)
    return high, low


def row_index(count, width):
    return lax.broadcasted_iota(jnp.int32, (count, width), 0)


def lane_index(count):
    return lax.broadcasted_iota(jnp.int32, (count, CZ), 1)


def ahead_x(field, face):
    return jnp.concatenate([field[CY:], face], axis=0)


def behind_x(field, face):
    return jnp.concatenate([face, field[:-CY]], axis=0)


def spread(face):
    return jnp.broadcast_to(face[:, None, :], (CX, CY, CZ)).reshape(ROWS, CZ)


def ahead_y(field, face, last):
    return jnp.where(last, spread(face), pltpu.roll(field, ROWS - 1, 0))


def behind_y(field, face, first):
    return jnp.where(first, spread(face), pltpu.roll(field, 1, 0))


def ahead_z(field, other, lane):
    return pltpu.roll(jnp.where(lane == 0, other, field), CZ - 1, 1)


def behind_z(field, other, lane):
    return pltpu.roll(jnp.where(lane == CZ - 1, other, field), 1, 1)


def row_in_brick():
    rows = row_index(ROWS, CZ)
    return rows - CY * ((rows * 2731) >> 16)


def first_layers(field_ref, out_x, out_y, out_z):
    out_x[0] = field_ref[1, 0:CY]
    out_x[1] = field_ref[2, 0:CY]
    for place, comp in ((0, 0), (1, 2)):
        for layer in range(CX):
            out_y[place, layer : layer + 1] = field_ref[comp, layer * CY : layer * CY + 1]
    out_z[0] = field_ref[0]
    out_z[1] = field_ref[1]


def last_layers(field_ref, out_x, out_y, out_z):
    out_x[0] = field_ref[1, ROWS - CY : ROWS]
    out_x[1] = field_ref[2, ROWS - CY : ROWS]
    for place, comp in ((0, 0), (1, 2)):
        for layer in range(CX):
            row = layer * CY + CY - 1
            out_y[place, layer : layer + 1] = field_ref[comp, row : row + 1]
    out_z[0] = field_ref[0]
    out_z[1] = field_ref[1]


def inside(faces, ahead):
    kept = []
    for face, axis in zip(faces, ("gx", "gy", "gz")):
        index = lax.axis_index(axis)
        real = index < lax.axis_size(axis) - 1 if ahead else index > 0
        kept.append([jnp.where(real, face[place], 0.0) for place in range(2)])
    return kept


def prepare_kernel(
    e_hbm,
    state_hbm,
    h_hbm,
    eps_hbm,
    pump_hbm,
    out_x,
    out_y,
    out_z,
    packed,
    e_out,
    state,
    h_out,
    eps_out,
    pump_out,
    sems,
):
    copies = [
        pltpu.make_async_copy(source, target, sems.at[place])
        for place, (source, target) in enumerate(
            (
                (e_hbm, e_out),
                (state_hbm, state),
                (h_hbm, h_out),
                (eps_hbm, eps_out),
                (pump_hbm, pump_out),
            )
        )
    ]
    for copy in copies:
        copy.start()
    copies[0].wait()
    first_layers(e_out, out_x, out_y, out_z)
    copies[1].wait()
    lower, lasing, upper = state[7], state[8], state[9]
    lasing_free = lasing + time_step * (upper / upper_life - lasing / lasing_life)
    lower_free = lower + time_step * (lasing / lasing_life - lower / lower_life)
    polar = [state[comp] for comp in range(3)]
    free = [keep_rate * state[3 + comp] - spring * polar[comp] for comp in range(3)]
    for field, value in enumerate(free + [lasing - lower] + polar + [lasing_free - lower_free]):
        for owner in range(SLOTS // 2):
            packed[owner, 2 * field : 2 * field + 2] = value[2 * owner : 2 * owner + 2]
    for copy in copies[2:]:
        copy.wait()


def magnetic_kernel(e_ref, h_ref, face_x, face_y, face_z, h_out, out_x, out_y, out_z):
    lane = lane_index(ROWS)
    last = row_in_brick() == CY - 1
    face_x, face_y, face_z = inside((face_x, face_y, face_z), True)
    ex, ey, ez = e_ref[0], e_ref[1], e_ref[2]
    first = (ahead_y(ez, face_y[1], last) - ez) - (ahead_z(ey, face_z[1], lane) - ey)
    second = (ahead_z(ex, face_z[0], lane) - ex) - (ahead_x(ez, face_x[1]) - ez)
    third = (ahead_x(ey, face_x[0]) - ey) - (ahead_y(ex, face_y[0], last) - ex)
    h_out[0] = h_ref[0] - time_step * first
    h_out[1] = h_ref[1] - time_step * second
    h_out[2] = h_ref[2] - time_step * third
    last_layers(h_out, out_x, out_y, out_z)


def electric_curl(h_ref, face_x, face_y, face_z):
    lane = lane_index(ROWS)
    start = row_in_brick() == 0
    face_x, face_y, face_z = inside((face_x, face_y, face_z), False)
    hx, hy, hz = h_ref[0], h_ref[1], h_ref[2]
    first = (hz - behind_y(hz, face_y[1], start)) - (hy - behind_z(hy, face_z[1], lane))
    second = (hx - behind_z(hx, face_z[0], lane)) - (hz - behind_x(hz, face_x[1]))
    third = (hy - behind_x(hy, face_x[0])) - (hx - behind_y(hx, face_y[0], start))
    return first, second, third


HALF = ROWS // 2
WIDE = 2 * CZ


def wide_hits(offsets, width):
    hits = row_index(WIDE, width) == (offsets & (WIDE - 1))
    return hits.astype(F32).astype(BF16)


def tall_hits(offsets, width):
    return row_index(HALF, width) == (offsets >> 8)


GROUP = 16


def scatter_kernel(first, placed, fields_ref, dense, total, spots, columns):
    def group(index, carry):
        lines = placed[pl.ds(GROUP * index, GROUP)]
        for slot in range(GROUP):
            line = lines[slot : slot + 1]
            hits = wide_hits(line, CZ)
            tall = tall_hits(line, CZ).astype(F32).astype(BF16).reshape(6, 16, CZ)
            values = fields_ref[
                (GROUP // 2) * index + slot // 2, pl.ds(2 * first + slot % 2, 4, 2), :
            ]
            for place, part in enumerate(split_parts(values)):
                across = (place * GROUP + slot) * CZ
                columns[:, across : across + CZ] = hits
                part = part.astype(F32)
                for field in range(4):
                    row = jnp.broadcast_to(part[field : field + 1], (16, CZ)).astype(BF16)
                    spots[field * HALF : (field + 1) * HALF, across : across + CZ] = (
                        tall * row[None]
                    ).reshape(HALF, CZ)
        got = lax.dot_general(
            spots[...], columns[...], (((1,), (1,)), ((), ())), preferred_element_type=F32
        )

        @pl.when(index == 0)
        def _():
            total[...] = got

        @pl.when(index > 0)
        def _():
            total[...] += got

        return carry

    lax.fori_loop(0, SLOTS // GROUP, group, 0)
    for field in range(4):
        got = total[field * HALF : (field + 1) * HALF]
        dense[field, pl.ds(0, HALF, 2), :] = got[:, :CZ]
        dense[field, pl.ds(1, HALF, 2), :] = got[:, CZ:]


def scattered(first, placed, fields, name):
    return call(
        functools.partial(scatter_kernel, first),
        shape(4, ROWS, CZ),
        (placed, fields),
        scratch=[
            pltpu.VMEM((4 * HALF, WIDE), F32),
            pltpu.VMEM((4 * HALF, 2 * GROUP * CZ), BF16),
            pltpu.VMEM((WIDE, 2 * GROUP * CZ), BF16),
        ],
        name=name,
    )


def electric_kernel(
    e_ref, h_ref, face_x, face_y, face_z, eps_ref, dense, e_out, out_x, out_y, out_z, rates
):
    curls = electric_curl(h_ref, face_x, face_y, face_z)
    scaled = time_step * eps_ref[...]
    inversion = dense[3]
    power = jnp.zeros_like(inversion)
    for comp in range(3):
        field = e_ref[comp]
        rate = dense[comp] + gain_push * inversion * field
        power = power + field * rate
        rates[comp] = rate
        e_out[comp] = field + scaled * (curls[comp] - rate)
    rates[3] = power
    first_layers(e_out, out_x, out_y, out_z)


def paired(ref, comp):
    return jnp.concatenate(
        [ref[comp, pl.ds(0, HALF, 2), :], ref[comp, pl.ds(1, HALF, 2), :]], axis=1
    )


def stacked(fields):
    return split_parts(jnp.concatenate([paired(ref, comp) for ref, comp in fields], axis=0))


def gather_lines(high, low, offsets, width):
    hits = wide_hits(offsets, width)
    tall = tall_hits(offsets, width)
    picked = jnp.dot(high, hits, preferred_element_type=F32)
    picked = picked + jnp.dot(low, hits, preferred_element_type=F32)
    return [
        jnp.sum(
            jnp.where(tall, picked[field * HALF : (field + 1) * HALF], 0.0), axis=0, keepdims=True
        )
        for field in range(picked.shape[0] // HALF)
    ]


TAKE = 8


def gather_drive(field_ref, placed, drives, first, high, low):
    high[...], low[...] = stacked([(field_ref, comp) for comp in range(3)])

    def group(index, carry):
        lines = placed[pl.ds(TAKE * index, TAKE)]
        offsets = jnp.concatenate([lines[slot : slot + 1] for slot in range(TAKE)], axis=1)
        got = gather_lines(high[...], low[...], offsets, TAKE * CZ)
        for comp in range(3):
            for slot in range(TAKE):
                drives[first + comp, pl.ds(TAKE * index + slot, 1)] = got[comp][
                    :, slot * CZ : (slot + 1) * CZ
                ]
        return carry

    lax.fori_loop(0, SLOTS // TAKE, group, 0)


def first_drive_kernel(e_ref, placed, e_seen, h_seen, surf_ref, drives, sampled, high, low):
    gather_drive(e_ref, placed, drives, 0, high, low)
    sample_rows(e_seen, h_seen, surf_ref, sampled)


def second_drive_kernel(e_ref, placed, before, drives, high, low):
    drives[0:3] = before[...]
    gather_drive(e_ref, placed, drives, 3, high, low)


def sample_rows(e_ref, h_ref, surf_ref, sampled):
    high, low = stacked([(ref, comp) for ref in (e_ref, h_ref) for comp in range(3)])
    got = gather_lines(high, low, surf_ref[...], CZ)
    sampled[...] = jnp.zeros_like(sampled)
    for field in range(6):
        sampled[field : field + 1] = got[field]


def times(left, right):
    return (left[0] * right[0] - left[1] * right[1], left[1] * right[0] + left[0] * right[1])


def phase_kernel(
    count_ref,
    owner_hbm,
    offsets_ref,
    surf_ref,
    units_ref,
    placed,
    surf_out,
    starts,
    turn,
    factors,
    owner_ref,
    sem,
):
    copy = pltpu.make_async_copy(owner_hbm, owner_ref, sem)
    copy.start()
    lanes = lax.broadcasted_iota(jnp.int32, (8, DIRS), 1)
    omega = freq_low + freq_pitch * (lanes & (FREQ - 1)).astype(F32)
    moment = omega * jnp.where(lanes < FREQ, time_step, 2.0 * time_step)
    for place, value in enumerate((jnp.cos(moment), jnp.sin(moment))):
        factors[place] = jnp.transpose(jnp.broadcast_to(value[0:1], (DIRS, DIRS)))
    cells = surf_ref[...]
    surf_out[...] = cells
    rows = cells >> 7
    layer = (rows * 2731) >> 16
    cell_x = lax.axis_index("gx") * CX + layer
    cell_y = lax.axis_index("gy") * CY + (rows - CY * layer)
    cell_z = lax.axis_index("gz") * CZ + (cells & (CZ - 1))
    along = jnp.zeros((CZ, DIRS), F32)
    for axis, (cell, size) in enumerate(((cell_x, 128), (cell_y, 192), (cell_z, 256))):
        place = cell.astype(F32) - 0.5 * (size - 1)
        column = jnp.transpose(jnp.broadcast_to(place, (CZ, CZ)))
        along = along + column * units_ref[axis : axis + 1]
    angle = (0.25 * freq_pitch) * along
    square = angle * angle
    cosine = 1.0 + square * (
        -1 / 2 + square * (1 / 24 + square * (-1 / 720 + square * (1 / 40320)))
    )
    sine = angle * (
        1.0 + square * (-1 / 6 + square * (1 / 120 + square * (-1 / 5040 + square * (1 / 362880))))
    )
    two = times((cosine, sine), (cosine, sine))
    powers = {1: times(two, two)}
    for power in (2, 4, 8, 16, 32):
        powers[power] = times(powers[power // 2], powers[power // 2])
    low_start = times(times(powers[16], powers[8]), times(powers[4], powers[2]))
    high_start = times(low_start, powers[32])
    turn[0], turn[1] = powers[1]
    starts[0], starts[1] = low_start
    starts[2], starts[3] = high_start
    copy.wait()
    count = count_ref[0]
    for slot in range(SLOTS):
        line = offsets_ref[slot : slot + 1]
        placed[pl.ds(owner_ref[0, slot], 1)] = jnp.where(slot < count, line, -1)


FAR = 48
LOAD = 48


def partner(step):
    index = lax.axis_index("gx")
    return (index >> 2) ^ step, (index & 3) ^ step


def chunk(drives, owner_x):
    return drives[:, pl.ds(pl.multiple_of(8 * owner_x, 8), 8)]


def pick(tiles, pairs):
    rows = row_index(8, CZ) >> 1
    result = jnp.zeros((8, CZ), F32)
    for tile, (taken, put) in zip(tiles, pairs):
        moved = pltpu.roll(tile, (2 * put - 2 * taken + 8) & 7, 0)
        result = jnp.where(rows == put, moved, result)
    return result


def fold_kernel(pieces, drives, total, *loads):
    total[...] = jnp.sum(pieces[...], axis=0)
    for step in (1, 2, 3):
        load = loads[step - 1]
        load[0:FAR] = total[...]
        load[FAR:] = chunk(drives, partner(step)[0]).reshape(LOAD, CZ)


def relay_kernel(total_in, drives, one, two, three, total, kept, *loads):
    total[...] = (total_in[...] + one[0:FAR]) + (two[0:FAR] + three[0:FAR])
    held = [chunk(drives, partner(0)[0]).reshape(LOAD, CZ)]
    held += [arrived[FAR:] for arrived in (one, two, three)]
    for step in range(4):
        target = partner(step)[1]
        out, first = (loads[step - 1], FAR) if step else (kept, 0)
        if step:
            out[0:FAR] = total[...]
        for field in range(6):
            tiles = [value[8 * field : 8 * field + 8] for value in held]
            start = first + 8 * field
            out[start : start + 8] = pick(tiles, [(target, source) for source in range(4)])


def finish_kernel(total_in, kept, one, two, three, spread_out, back):
    total = (total_in[...] + one[0:FAR]) + (two[0:FAR] + three[0:FAR])
    for peer in range(8):
        spread_out[peer] = total
    held = [kept[...]] + [arrived[FAR:] for arrived in (one, two, three)]
    for source in range(4):
        rows = pl.ds(pl.multiple_of(8 * partner(source)[0], 8), 8)
        for field in range(6):
            tiles = [value[8 * field : 8 * field + 8] for value in held]
            back[field, rows] = pick(tiles, [(source, partner(step)[1]) for step in range(4)])


def final_kernel(
    e_ref,
    h_ref,
    face_x,
    face_y,
    face_z,
    eps_ref,
    rates,
    dense,
    surf_ref,
    early_ref,
    starts,
    turn,
    factors,
    e_out,
    keep_out,
    send_out,
    late,
    now,
):
    curls = electric_curl(h_ref, face_x, face_y, face_z)
    scaled = time_step * eps_ref[...]
    later = dense[3] + (2.0 * time_step * cross_rate) * rates[3]
    for comp in range(3):
        field = e_ref[comp]
        polar = dense[comp] + time_step * rates[comp]
        rate = keep_rate * rates[comp] - spring * polar + gain_push * later * field
        e_out[comp] = field + scaled * (curls[comp] - rate)
    sample_rows(e_out, h_ref, surf_ref, late)
    scale = 1.0 / math.sqrt(STEPS * CZ * 256)
    high, low = split_parts(scale * jnp.concatenate([early_ref[...], late[...]], axis=0))
    left = jnp.concatenate(
        [
            jnp.concatenate([high, high], axis=1),
            jnp.concatenate([low, jnp.zeros_like(low)], axis=1),
        ],
        axis=0,
    )
    own = lax.axis_index("gz")
    for side, out in ((1, send_out), (0, keep_out)):
        target = lax.rem(own + side, 2)
        now[0] = starts[2 * target]
        now[1] = starts[2 * target + 1]
        for freq in range(FREQ // 2):
            here = (now[0], now[1])
            re_high, re_low = split_parts(here[0])
            im_high, im_low = split_parts(here[1])
            right = jnp.concatenate(
                [
                    jnp.concatenate([re_high, im_high], axis=1),
                    jnp.concatenate([re_low, im_low], axis=1),
                ],
                axis=0,
            )
            now[0], now[1] = times(here, (turn[0], turn[1]))
            both = jnp.dot(left, right, preferred_element_type=F32)
            both = both[0:16] + both[16:32]
            real = jnp.zeros((8, DIRS), F32)
            imag = jnp.zeros((8, DIRS), F32)
            for step in range(STEPS):
                row = pl.ds(step * FREQ + target * (FREQ // 2) + freq, 1)
                cosine = factors[0, row]
                sine = factors[1, row]
                upper = both[8 * step : 8 * step + 8, 0:DIRS]
                under = both[8 * step : 8 * step + 8, DIRS:]
                real = real + (cosine * upper + sine * under)
                imag = imag + (cosine * under - sine * upper)
            for comp in range(6):
                row = comp * (FREQ // 2) + freq
                out[row : row + 1] = real[comp : comp + 1]
                row = (comp + 6) * (FREQ // 2) + freq
                out[row : row + 1] = imag[comp : comp + 1]


def atoms_kernel(state_ref, pump_ref, drives, out):
    polar = [state_ref[c] for c in range(3)]
    rate = [state_ref[3 + c] for c in range(3)]
    ground, lower, lasing, upper = [state_ref[6 + level] for level in range(4)]
    pump = pump_ref[...]
    for step in range(STEPS):
        drive = [drives[3 * step + c] for c in range(3)]
        inversion = lasing - lower
        power = jnp.zeros_like(pump)
        for c in range(3):
            rate[c] = (
                (1.0 - half) * rate[c]
                + time_step
                * (coupling * inversion * drive[c] - omega_rest * omega_rest * polar[c])
            ) / (1.0 + half)
            polar[c] = polar[c] + time_step * rate[c]
            power = power + drive[c] * rate[c]
        upper_new = upper + time_step * (pump * ground - upper / upper_life)
        lasing_new = lasing + time_step * (
            upper / upper_life - lasing / lasing_life + cross_rate * power
        )
        lower_new = lower + time_step * (
            lasing / lasing_life - lower / lower_life - cross_rate * power
        )
        ground = ground + time_step * (lower / lower_life - pump * ground)
        lower, lasing, upper = lower_new, lasing_new, upper_new
    for place, value in enumerate(polar + rate + [ground, lower, lasing, upper]):
        out[place] = value


def store_kernel(e_ref, h_ref, e_out, h_out):
    e_out[...] = e_ref[...]
    h_out[...] = h_ref[...]


def directions(count):
    index = np.arange(count, dtype=np.float32)
    cosine = np.float32(1.0) - np.float32(2.0) * (index + np.float32(0.5)) / np.float32(count)
    sine = np.sqrt(np.float32(1.0) - cosine * cosine)
    azimuth = (np.float32(golden) * index).astype(np.float64)
    rows = np.zeros((8, count), np.float32)
    rows[0] = sine * np.cos(azimuth).astype(np.float32)
    rows[1] = sine * np.sin(azimuth).astype(np.float32)
    rows[2] = cosine
    return rows


def local(
    efield,
    hfield,
    inv_eps,
    gain_state,
    pump,
    gain_offsets,
    gain_count,
    block_owner,
    surf_offsets,
    far_acc,
):
    dense = shape(3, ROWS, CZ)
    faces = (shape(2, CY, CZ), shape(2, CX, CZ), shape(2, ROWS, CZ))
    down = [[((i + 1) % n, i) for i in range(n)] for n in (16, 8, 2)]
    up = [[(i, (i + 1) % n) for i in range(n)] for n in (16, 8, 2)]
    vmem = pl.BlockSpec(memory_space=pltpu.VMEM)

    hbm = pl.BlockSpec(memory_space=pltpu.HBM)

    def shifted(parts, perms):
        return [
            lax.ppermute(part, axis, perm)
            for part, axis, perm in zip(parts, ("gx", "gy", "gz"), perms)
        ]

    *near, packed, e_old, state, h_old, eps, pumps = call(
        prepare_kernel,
        faces
        + (
            shape(SLOTS // 2, 16, CZ),
            dense,
            shape(10, SLOTS, CZ),
            dense,
            shape(ROWS, CZ),
            shape(SLOTS, CZ),
        ),
        stay(
            efield.reshape(3, ROWS, CZ),
            jnp.transpose(gain_state.reshape(SLOTS, 10, CZ), (1, 0, 2)),
            hfield.reshape(3, ROWS, CZ),
            inv_eps.reshape(ROWS, CZ),
            pump.reshape(SLOTS, CZ),
        ),
        in_specs=[hbm] * 5,
        scratch=[pltpu.SemaphoreType.DMA((5,))],
        name="prepare",
    )
    near = shifted(near, down)
    fields = lax.all_to_all(packed, "gx", 0, 0, tiled=True)
    placed, surf, starts, turn, factors = call(
        phase_kernel,
        (
            shape(SLOTS, CZ, dtype=jnp.int32),
            shape(1, CZ, dtype=jnp.int32),
            shape(4, CZ, DIRS),
            shape(2, CZ, DIRS),
            shape(2, STEPS * FREQ, DIRS),
        ),
        [gain_count.reshape(1)]
        + stay(
            block_owner.reshape(1, SLOTS),
            gain_offsets.reshape(SLOTS, CZ),
            surf_offsets.reshape(1, CZ),
            jnp.asarray(directions(DIRS)),
        ),
        in_specs=[pl.BlockSpec(memory_space=pltpu.SMEM), hbm, vmem, vmem, vmem],
        scratch=[pltpu.SMEM((1, SLOTS), jnp.int32), pltpu.SemaphoreType.DMA],
        moved=MIB // 4,
        name="phase",
    )
    *near, placed = lax.optimization_barrier((*near, placed))
    h_one, *edge = call(
        magnetic_kernel,
        (dense,) + faces,
        (e_old, h_old, *near),
        flops=10**11,
        moved=100 * MIB,
        name="magnetic",
    )
    edge = shifted(edge, up)
    spread_now = scattered(0, placed, fields, "scatter")
    e_one, *near, rates = call(
        electric_kernel,
        (dense,) + faces + (shape(4, ROWS, CZ),),
        (e_old, h_one, *edge, eps, spread_now),
        name="electric",
    )
    near = shifted(near, down)
    spread_next = scattered(4, placed, fields, "scatter2")
    *near, spread_next = lax.optimization_barrier((*near, spread_next))
    h_two, *edge = call(magnetic_kernel, (dense,) + faces, (e_one, h_one, *near), name="magnetic2")
    edge = shifted(edge, up)
    e_seen, h_seen, h_two = lax.optimization_barrier((e_one, h_one, h_two))
    halves = [pltpu.VMEM((3 * HALF, WIDE), BF16)] * 2
    before, early = call(
        first_drive_kernel,
        (shape(3, SLOTS, CZ), shape(8, CZ)),
        (e_old, placed, e_seen, h_seen, surf),
        scratch=halves,
        name="drive",
    )
    part = shape(12 * FREQ // 2, DIRS)
    e_two, keep, send = call(
        final_kernel,
        (dense, part, part),
        (e_one, h_two, *edge, eps, rates, spread_next, surf, early, starts, turn, factors),
        scratch=[pltpu.VMEM((8, CZ), F32), pltpu.VMEM((2, CZ, DIRS), F32)],
        name="final",
    )
    chip = keep + lax.ppermute(send, "gz", down[2])
    chip, e_seen = lax.optimization_barrier((chip, e_one))
    pieces = lax.all_to_all(chip.reshape(8, FAR, DIRS), "gy", 0, 0, tiled=True)
    drives = call(
        second_drive_kernel,
        shape(6, SLOTS, CZ),
        (e_seen, placed, before),
        scratch=halves,
        name="drive2",
    )
    load = shape(FAR + LOAD, CZ)
    total, *loads = call(
        fold_kernel, (shape(FAR, DIRS),) + (load,) * 3, (pieces, drives), name="fold"
    )
    loads = [
        lax.ppermute(
            value, "gx", [(a * 4 + z, (a ^ k) * 4 + z) for a in range(4) for z in range(4)]
        )
        for k, value in enumerate(loads, 1)
    ]
    total, kept, *loads = call(
        relay_kernel,
        (shape(FAR, DIRS), shape(LOAD, CZ)) + (load,) * 3,
        (total, drives, *loads),
        name="relay",
    )
    loads = [
        lax.ppermute(
            value, "gx", [(a * 4 + z, a * 4 + (z ^ k)) for a in range(4) for z in range(4)]
        )
        for k, value in enumerate(loads, 1)
    ]
    e_out, h_out = call(store_kernel, (dense, dense), (e_two, h_two), name="store")
    copies, back = call(
        finish_kernel,
        (shape(8, FAR, DIRS), shape(6, SLOTS, CZ)),
        (total, kept, *loads),
        name="finish",
    )
    state_out = call(
        atoms_kernel,
        shape(10, SLOTS, CZ),
        (state, pumps, back),
        name="atoms",
    )
    copies, state_out, e_out, h_out = lax.optimization_barrier((copies, state_out, e_out, h_out))
    gathered = lax.all_to_all(copies, "gy", 0, 0, tiled=True)
    far_out = far_acc + jnp.transpose(gathered.reshape(12, FREQ // 2, DIRS), (1, 0, 2))
    return (
        e_out.reshape(efield.shape),
        h_out.reshape(hfield.shape),
        jnp.transpose(state_out, (1, 0, 2)).reshape(gain_state.shape),
        far_out,
    )


def solution(mesh):
    placed = (
        P(None, "gx", "gy", "gz"),
        P(None, "gx", "gy", "gz"),
        P("gx", "gy", "gz"),
        P("gx", "gy", "gz", None, None, None),
        P("gx", "gy", "gz", None, None),
        P("gx", "gy", "gz", None, None),
        P("gx", "gy", "gz"),
        P("gx", "gy", "gz", None),
        P("gx", "gy", "gz", None),
        P("gz", None, None),
    )
    return jax.shard_map(
        local,
        mesh=mesh,
        in_specs=placed,
        out_specs=(
            P(None, "gx", "gy", "gz"),
            P(None, "gx", "gy", "gz"),
            P("gx", "gy", "gz", None, None, None),
            P("gz", None, None),
        ),
        check_vma=False,
    )
```

```python
import functools
import math

import jax
import jax.numpy as jnp
import numpy as np
from jax import lax
from jax.experimental import pallas as pl
from jax.experimental.pallas import tpu as pltpu
from jax.sharding import PartitionSpec as P

FREQ = 64
STEPS = 2
CX = 8
CY = 24
CZ = 128
ROWS = CX * CY
SLOTS = 32
DIRS = 128

time_step = 0.5
damping = 0.1
omega_rest = 1.0
coupling = 0.5
cross_rate = 0.3
upper_life = 2.0
lasing_life = 20.0
lower_life = 2.0
freq_low = 0.3
freq_pitch = 0.01
golden = 2.399963229728653

half = 0.5 * damping * time_step
keep_rate = (1.0 - half) / (1.0 + half)
spring = time_step * omega_rest * omega_rest / (1.0 + half)
gain_push = time_step * coupling / (1.0 + half)

F32 = jnp.float32
BF16 = jnp.bfloat16
MIB = 1 << 20


def shape(*dims, dtype=F32):
    return jax.ShapeDtypeStruct(dims, dtype)


def call(kernel, outs, args, in_specs=None, scratch=(), vmem=16, flops=0, moved=2 * MIB, name=None):
    return pl.pallas_call(
        kernel,
        out_shape=outs,
        in_specs=in_specs or [pl.BlockSpec(memory_space=pltpu.VMEM)] * len(args),
        scratch_shapes=scratch,
        compiler_params=pltpu.CompilerParams(vmem_limit_bytes=vmem * MIB),
        cost_estimate=pl.CostEstimate(flops=flops, bytes_accessed=moved, transcendentals=0),
        name=name,
    )(*args)


def stay(*values):
    return [pltpu.with_memory_space_constraint(value, pltpu.HBM) for value in values]


def split_parts(value):
    high = value.astype(BF16)
    low = (value - high.astype(F32)).astype(BF16)
    return high, low


def row_index(count, width):
    return lax.broadcasted_iota(jnp.int32, (count, width), 0)


def lane_index(count):
    return lax.broadcasted_iota(jnp.int32, (count, CZ), 1)


def ahead_x(field, face):
    return jnp.concatenate([field[CY:], face], axis=0)


def behind_x(field, face):
    return jnp.concatenate([face, field[:-CY]], axis=0)


def spread(face):
    return jnp.broadcast_to(face[:, None, :], (CX, CY, CZ)).reshape(ROWS, CZ)


def ahead_y(field, face, last):
    return jnp.where(last, spread(face), pltpu.roll(field, ROWS - 1, 0))


def behind_y(field, face, first):
    return jnp.where(first, spread(face), pltpu.roll(field, 1, 0))


def ahead_z(field, other, lane):
    return pltpu.roll(jnp.where(lane == 0, other, field), CZ - 1, 1)


def behind_z(field, other, lane):
    return pltpu.roll(jnp.where(lane == CZ - 1, other, field), 1, 1)


def row_in_brick():
    rows = row_index(ROWS, CZ)
    return rows - CY * ((rows * 2731) >> 16)


def first_layers(field_ref, out_x, out_y, out_z):
    out_x[0] = field_ref[1, 0:CY]
    out_x[1] = field_ref[2, 0:CY]
    for place, comp in ((0, 0), (1, 2)):
        for layer in range(CX):
            out_y[place, layer : layer + 1] = field_ref[comp, layer * CY : layer * CY + 1]
    out_z[0] = field_ref[0]
    out_z[1] = field_ref[1]


def last_layers(field_ref, out_x, out_y, out_z):
    out_x[0] = field_ref[1, ROWS - CY : ROWS]
    out_x[1] = field_ref[2, ROWS - CY : ROWS]
    for place, comp in ((0, 0), (1, 2)):
        for layer in range(CX):
            row = layer * CY + CY - 1
            out_y[place, layer : layer + 1] = field_ref[comp, row : row + 1]
    out_z[0] = field_ref[0]
    out_z[1] = field_ref[1]


def inside(faces, ahead):
    kept = []
    for face, axis in zip(faces, ("gx", "gy", "gz")):
        index = lax.axis_index(axis)
        real = index < lax.axis_size(axis) - 1 if ahead else index > 0
        kept.append([jnp.where(real, face[place], 0.0) for place in range(2)])
    return kept


def prepare_kernel(e_hbm, state_hbm, out_x, out_y, out_z, packed, e_out, state, sems):
    copies = [
        pltpu.make_async_copy(e_hbm, e_out, sems.at[0]),
        pltpu.make_async_copy(state_hbm, state, sems.at[1]),
    ]
    for copy in copies:
        copy.start()
    copies[0].wait()
    first_layers(e_out, out_x, out_y, out_z)
    copies[1].wait()
    lower, lasing, upper = state[7], state[8], state[9]
    lasing_free = lasing + time_step * (upper / upper_life - lasing / lasing_life)
    lower_free = lower + time_step * (lasing / lasing_life - lower / lower_life)
    polar = [state[comp] for comp in range(3)]
    free = [keep_rate * state[3 + comp] - spring * polar[comp] for comp in range(3)]
    for field, value in enumerate(free + [lasing - lower] + polar + [lasing_free - lower_free]):
        for owner in range(SLOTS // 2):
            packed[owner, 2 * field : 2 * field + 2] = value[2 * owner : 2 * owner + 2]


def magnetic_kernel(e_ref, h_ref, face_x, face_y, face_z, h_out, out_x, out_y, out_z):
    lane = lane_index(ROWS)
    last = row_in_brick() == CY - 1
    face_x, face_y, face_z = inside((face_x, face_y, face_z), True)
    ex, ey, ez = e_ref[0], e_ref[1], e_ref[2]
    first = (ahead_y(ez, face_y[1], last) - ez) - (ahead_z(ey, face_z[1], lane) - ey)
    second = (ahead_z(ex, face_z[0], lane) - ex) - (ahead_x(ez, face_x[1]) - ez)
    third = (ahead_x(ey, face_x[0]) - ey) - (ahead_y(ex, face_y[0], last) - ex)
    h_out[0] = h_ref[0] - time_step * first
    h_out[1] = h_ref[1] - time_step * second
    h_out[2] = h_ref[2] - time_step * third
    last_layers(h_out, out_x, out_y, out_z)


def electric_curl(h_ref, face_x, face_y, face_z):
    lane = lane_index(ROWS)
    start = row_in_brick() == 0
    face_x, face_y, face_z = inside((face_x, face_y, face_z), False)
    hx, hy, hz = h_ref[0], h_ref[1], h_ref[2]
    first = (hz - behind_y(hz, face_y[1], start)) - (hy - behind_z(hy, face_z[1], lane))
    second = (hx - behind_z(hx, face_z[0], lane)) - (hz - behind_x(hz, face_x[1]))
    third = (hy - behind_x(hy, face_x[0])) - (hx - behind_y(hx, face_y[0], start))
    return first, second, third


HALF = ROWS // 2
WIDE = 2 * CZ


def wide_hits(offsets, width):
    hits = row_index(WIDE, width) == (offsets & (WIDE - 1))
    return hits.astype(F32).astype(BF16)


def tall_hits(offsets, width):
    return row_index(HALF, width) == (offsets >> 8)


def scatter_kernel(first, placed, fields_ref, dense, spots, columns):
    for slot in range(SLOTS):
        line = placed[slot : slot + 1]
        across = slice(slot * CZ, (slot + 1) * CZ)
        columns[:, across] = wide_hits(line, CZ)
        tall = tall_hits(line, CZ).astype(F32).astype(BF16).reshape(6, 16, CZ)
        values = fields_ref[slot // 2, pl.ds(2 * first + slot % 2, 4, 2), :]
        for place, part in enumerate(split_parts(values)):
            part = part.astype(F32)
            for field in range(4):
                row = jnp.broadcast_to(part[field : field + 1], (16, CZ)).astype(BF16)
                top = (4 * place + field) * HALF
                spots[top : top + HALF, across] = (tall * row[None]).reshape(HALF, CZ)
    total = lax.dot_general(
        spots[...], columns[...], (((1,), (1,)), ((), ())), preferred_element_type=F32
    )
    total = total[: 4 * HALF] + total[4 * HALF :]
    for field in range(4):
        got = total[field * HALF : (field + 1) * HALF]
        dense[field, pl.ds(0, HALF, 2), :] = got[:, :CZ]
        dense[field, pl.ds(1, HALF, 2), :] = got[:, CZ:]


SCATTER = [pltpu.VMEM((8 * HALF, SLOTS * CZ), BF16), pltpu.VMEM((WIDE, SLOTS * CZ), BF16)]


def scatter_sample_kernel(
    placed, fields_ref, e_ref, h_ref, surf_ref, dense, sampled, spots, columns
):
    scatter_kernel(4, placed, fields_ref, dense, spots, columns)
    sample_rows(e_ref, h_ref, surf_ref, sampled)


def electric_kernel(
    e_ref, h_ref, face_x, face_y, face_z, eps_ref, dense, e_out, out_x, out_y, out_z, rates
):
    curls = electric_curl(h_ref, face_x, face_y, face_z)
    scaled = time_step * eps_ref[...]
    inversion = dense[3]
    power = jnp.zeros_like(inversion)
    for comp in range(3):
        field = e_ref[comp]
        rate = dense[comp] + gain_push * inversion * field
        power = power + field * rate
        rates[comp] = rate
        e_out[comp] = field + scaled * (curls[comp] - rate)
    rates[3] = power
    first_layers(e_out, out_x, out_y, out_z)


def paired(ref, comp):
    return jnp.concatenate(
        [ref[comp, pl.ds(0, HALF, 2), :], ref[comp, pl.ds(1, HALF, 2), :]], axis=1
    )


def stacked(fields):
    return jnp.concatenate(
        split_parts(jnp.concatenate([paired(ref, comp) for ref, comp in fields], axis=0)), axis=0
    )


def gather_lines(values, offsets, width):
    hits = wide_hits(offsets, width)
    tall = tall_hits(offsets, width)
    picked = jnp.dot(values, hits, preferred_element_type=F32)
    lines = []
    for field in range(6):
        rows = slice(field * HALF, (field + 1) * HALF)
        both = picked[rows] + picked[6 * HALF :][rows]
        lines.append(jnp.sum(jnp.where(tall, both, 0.0), axis=0, keepdims=True))
    return lines


TAKE = 16


def drive_kernel(e_old, e_new, placed, drives, values):
    values[...] = stacked([(ref, comp) for ref in (e_old, e_new) for comp in range(3)])

    def group(index, carry):
        lines = placed[pl.ds(TAKE * index, TAKE)]
        offsets = jnp.concatenate([lines[slot : slot + 1] for slot in range(TAKE)], axis=1)
        got = gather_lines(values[...], offsets, TAKE * CZ)
        for field in range(6):
            for slot in range(TAKE):
                drives[field, pl.ds(TAKE * index + slot, 1)] = got[field][
                    :, slot * CZ : (slot + 1) * CZ
                ]
        return carry

    lax.fori_loop(0, SLOTS // TAKE, group, 0)


def sample_rows(e_ref, h_ref, surf_ref, sampled):
    values = stacked([(ref, comp) for ref in (e_ref, h_ref) for comp in range(3)])
    got = gather_lines(values, surf_ref[...], CZ)
    sampled[...] = jnp.zeros_like(sampled)
    for field in range(6):
        sampled[field : field + 1] = got[field]


def times(left, right):
    return (left[0] * right[0] - left[1] * right[1], left[1] * right[0] + left[0] * right[1])


def phase_kernel(
    count_ref,
    owner_hbm,
    offsets_ref,
    surf_ref,
    units_ref,
    h_hbm,
    eps_hbm,
    pump_hbm,
    far_hbm,
    placed,
    surf_out,
    starts,
    turn,
    factors,
    h_out,
    eps_out,
    pump_out,
    far_out,
    owner_ref,
    sems,
):
    own = pl.ds(pl.multiple_of(FAR * lax.axis_index("gy"), 8), FAR)
    copies = [
        pltpu.make_async_copy(source, target, sems.at[place])
        for place, (source, target) in enumerate(
            (
                (owner_hbm, owner_ref),
                (h_hbm, h_out),
                (eps_hbm, eps_out),
                (pump_hbm, pump_out),
                (far_hbm.at[own], far_out),
            )
        )
    ]
    for copy in copies:
        copy.start()
    lanes = lax.broadcasted_iota(jnp.int32, (8, DIRS), 1)
    omega = freq_low + freq_pitch * (lanes & (FREQ - 1)).astype(F32)
    moment = omega * jnp.where(lanes < FREQ, time_step, 2.0 * time_step)
    for place, value in enumerate((jnp.cos(moment), jnp.sin(moment))):
        factors[place] = jnp.transpose(jnp.broadcast_to(value[0:1], (DIRS, DIRS)))
    cells = surf_ref[...]
    surf_out[...] = cells
    rows = cells >> 7
    layer = (rows * 2731) >> 16
    cell_x = lax.axis_index("gx") * CX + layer
    cell_y = lax.axis_index("gy") * CY + (rows - CY * layer)
    cell_z = lax.axis_index("gz") * CZ + (cells & (CZ - 1))
    along = jnp.zeros((CZ, DIRS), F32)
    for axis, (cell, size) in enumerate(((cell_x, 128), (cell_y, 192), (cell_z, 256))):
        place = cell.astype(F32) - 0.5 * (size - 1)
        column = jnp.transpose(jnp.broadcast_to(place, (CZ, CZ)))
        along = along + column * units_ref[axis : axis + 1]
    angle = (0.25 * freq_pitch) * along
    square = angle * angle
    cosine = 1.0 + square * (
        -1 / 2 + square * (1 / 24 + square * (-1 / 720 + square * (1 / 40320)))
    )
    sine = angle * (
        1.0 + square * (-1 / 6 + square * (1 / 120 + square * (-1 / 5040 + square * (1 / 362880))))
    )
    two = times((cosine, sine), (cosine, sine))
    powers = {1: times(two, two)}
    for power in (2, 4, 8, 16, 32):
        powers[power] = times(powers[power // 2], powers[power // 2])
    low_start = times(times(powers[16], powers[8]), times(powers[4], powers[2]))
    high_start = times(low_start, powers[32])
    turn[0], turn[1] = powers[1]
    starts[0], starts[1] = low_start
    starts[2], starts[3] = high_start
    for copy in copies:
        copy.wait()
    count = count_ref[0]
    for slot in range(SLOTS):
        line = offsets_ref[slot : slot + 1]
        placed[pl.ds(owner_ref[0, slot], 1)] = jnp.where(slot < count, line, -1)


FAR = 48
LOAD = 48


def partner(step):
    index = lax.axis_index("gx")
    return (index >> 2) ^ step, (index & 3) ^ step


def chunk(drives, owner_x):
    return drives[:, pl.ds(pl.multiple_of(8 * owner_x, 8), 8)]


def pick(tiles, pairs):
    rows = row_index(8, CZ) >> 1
    result = jnp.zeros((8, CZ), F32)
    for tile, (taken, put) in zip(tiles, pairs):
        moved = pltpu.roll(tile, (2 * put - 2 * taken + 8) & 7, 0)
        result = jnp.where(rows == put, moved, result)
    return result


def fold_kernel(pieces, drives, total, *loads):
    total[...] = jnp.sum(pieces[...], axis=0)
    for step in (1, 2, 3):
        load = loads[step - 1]
        load[0:FAR] = total[...]
        load[FAR:] = chunk(drives, partner(step)[0]).reshape(LOAD, CZ)


def relay_kernel(total_in, drives, one, two, three, total, kept, *loads):
    total[...] = (total_in[...] + one[0:FAR]) + (two[0:FAR] + three[0:FAR])
    held = [chunk(drives, partner(0)[0]).reshape(LOAD, CZ)]
    held += [arrived[FAR:] for arrived in (one, two, three)]
    for step in range(4):
        target = partner(step)[1]
        out, first = (loads[step - 1], FAR) if step else (kept, 0)
        if step:
            out[0:FAR] = total[...]
        for field in range(6):
            tiles = [value[8 * field : 8 * field + 8] for value in held]
            start = first + 8 * field
            out[start : start + 8] = pick(tiles, [(target, source) for source in range(4)])


def finish_kernel(total_in, kept, one, two, three, far_ref, spread_out, back):
    total = (total_in[...] + one[0:FAR]) + (two[0:FAR] + three[0:FAR])
    total = far_ref[...] + total
    for peer in range(8):
        spread_out[peer] = total
    held = [kept[...]] + [arrived[FAR:] for arrived in (one, two, three)]
    for source in range(4):
        rows = pl.ds(pl.multiple_of(8 * partner(source)[0], 8), 8)
        for field in range(6):
            tiles = [value[8 * field : 8 * field + 8] for value in held]
            back[field, rows] = pick(tiles, [(source, partner(step)[1]) for step in range(4)])


def final_kernel(
    e_ref,
    h_ref,
    face_x,
    face_y,
    face_z,
    eps_ref,
    rates,
    dense,
    surf_ref,
    early_ref,
    starts,
    turn,
    factors,
    e_out,
    keep_out,
    send_out,
    late,
    now,
):
    curls = electric_curl(h_ref, face_x, face_y, face_z)
    scaled = time_step * eps_ref[...]
    later = dense[3] + (2.0 * time_step * cross_rate) * rates[3]
    for comp in range(3):
        field = e_ref[comp]
        polar = dense[comp] + time_step * rates[comp]
        rate = keep_rate * rates[comp] - spring * polar + gain_push * later * field
        e_out[comp] = field + scaled * (curls[comp] - rate)
    sample_rows(e_out, h_ref, surf_ref, late)
    scale = 1.0 / math.sqrt(STEPS * CZ * 256)
    high, low = split_parts(scale * jnp.concatenate([early_ref[...], late[...]], axis=0))
    left = jnp.concatenate(
        [
            jnp.concatenate([high, high], axis=1),
            jnp.concatenate([low, jnp.zeros_like(low)], axis=1),
        ],
        axis=0,
    )
    own = lax.axis_index("gz")
    for side, out in ((1, send_out), (0, keep_out)):
        target = lax.rem(own + side, 2)
        now[0] = starts[2 * target]
        now[1] = starts[2 * target + 1]
        for freq in range(FREQ // 2):
            here = (now[0], now[1])
            re_high, re_low = split_parts(here[0])
            im_high, im_low = split_parts(here[1])
            right = jnp.concatenate(
                [
                    jnp.concatenate([re_high, im_high], axis=1),
                    jnp.concatenate([re_low, im_low], axis=1),
                ],
                axis=0,
            )
            now[0], now[1] = times(here, (turn[0], turn[1]))
            both = jnp.dot(left, right, preferred_element_type=F32)
            both = both[0:16] + both[16:32]
            real = jnp.zeros((8, DIRS), F32)
            imag = jnp.zeros((8, DIRS), F32)
            for step in range(STEPS):
                row = pl.ds(step * FREQ + target * (FREQ // 2) + freq, 1)
                cosine = factors[0, row]
                sine = factors[1, row]
                upper = both[8 * step : 8 * step + 8, 0:DIRS]
                under = both[8 * step : 8 * step + 8, DIRS:]
                real = real + (cosine * upper + sine * under)
                imag = imag + (cosine * under - sine * upper)
            for comp in range(6):
                row = comp * (FREQ // 2) + freq
                out[row : row + 1] = real[comp : comp + 1]
                row = (comp + 6) * (FREQ // 2) + freq
                out[row : row + 1] = imag[comp : comp + 1]


def atoms_kernel(state_ref, pump_ref, drives, out):
    polar = [state_ref[c] for c in range(3)]
    rate = [state_ref[3 + c] for c in range(3)]
    ground, lower, lasing, upper = [state_ref[6 + level] for level in range(4)]
    pump = pump_ref[...]
    for step in range(STEPS):
        drive = [drives[3 * step + c] for c in range(3)]
        inversion = lasing - lower
        power = jnp.zeros_like(pump)
        for c in range(3):
            rate[c] = (
                (1.0 - half) * rate[c]
                + time_step
                * (coupling * inversion * drive[c] - omega_rest * omega_rest * polar[c])
            ) / (1.0 + half)
            polar[c] = polar[c] + time_step * rate[c]
            power = power + drive[c] * rate[c]
        upper_new = upper + time_step * (pump * ground - upper / upper_life)
        lasing_new = lasing + time_step * (
            upper / upper_life - lasing / lasing_life + cross_rate * power
        )
        lower_new = lower + time_step * (
            lasing / lasing_life - lower / lower_life - cross_rate * power
        )
        ground = ground + time_step * (lower / lower_life - pump * ground)
        lower, lasing, upper = lower_new, lasing_new, upper_new
    for place, value in enumerate(polar + rate + [ground, lower, lasing, upper]):
        out[place] = value


def store_kernel(e_ref, h_ref, e_out, h_out):
    e_out[...] = e_ref[...]
    h_out[...] = h_ref[...]


def directions(count):
    index = np.arange(count, dtype=np.float32)
    cosine = np.float32(1.0) - np.float32(2.0) * (index + np.float32(0.5)) / np.float32(count)
    sine = np.sqrt(np.float32(1.0) - cosine * cosine)
    azimuth = (np.float32(golden) * index).astype(np.float64)
    rows = np.zeros((8, count), np.float32)
    rows[0] = sine * np.cos(azimuth).astype(np.float32)
    rows[1] = sine * np.sin(azimuth).astype(np.float32)
    rows[2] = cosine
    return rows


def local(
    efield,
    hfield,
    inv_eps,
    gain_state,
    pump,
    gain_offsets,
    gain_count,
    block_owner,
    surf_offsets,
    far_acc,
):
    dense = shape(3, ROWS, CZ)
    faces = (shape(2, CY, CZ), shape(2, CX, CZ), shape(2, ROWS, CZ))
    down = [[((i + 1) % n, i) for i in range(n)] for n in (16, 8, 2)]
    up = [[(i, (i + 1) % n) for i in range(n)] for n in (16, 8, 2)]
    vmem = pl.BlockSpec(memory_space=pltpu.VMEM)

    hbm = pl.BlockSpec(memory_space=pltpu.HBM)

    def shifted(parts, perms):
        return [
            lax.ppermute(part, axis, perm)
            for part, axis, perm in zip(parts, ("gx", "gy", "gz"), perms)
        ]

    *near, packed, e_old, state = call(
        prepare_kernel,
        faces + (shape(SLOTS // 2, 16, CZ), dense, shape(10, SLOTS, CZ)),
        stay(
            efield.reshape(3, ROWS, CZ),
            jnp.transpose(gain_state.reshape(SLOTS, 10, CZ), (1, 0, 2)),
        ),
        in_specs=[hbm] * 2,
        scratch=[pltpu.SemaphoreType.DMA((2,))],
        name="prepare",
    )
    near = shifted(near, down)
    fields = lax.all_to_all(packed, "gx", 0, 0, tiled=True)
    placed, surf, starts, turn, factors, h_old, eps, pumps, far_part = call(
        phase_kernel,
        (
            shape(SLOTS, CZ, dtype=jnp.int32),
            shape(1, CZ, dtype=jnp.int32),
            shape(4, CZ, DIRS),
            shape(2, CZ, DIRS),
            shape(2, STEPS * FREQ, DIRS),
            dense,
            shape(ROWS, CZ),
            shape(SLOTS, CZ),
            shape(FAR, DIRS),
        ),
        [gain_count.reshape(1)]
        + stay(
            block_owner.reshape(1, SLOTS),
            gain_offsets.reshape(SLOTS, CZ),
            surf_offsets.reshape(1, CZ),
            jnp.asarray(directions(DIRS)),
            hfield.reshape(3, ROWS, CZ),
            inv_eps.reshape(ROWS, CZ),
            pump.reshape(SLOTS, CZ),
            jnp.transpose(far_acc, (1, 0, 2)).reshape(8 * FAR, DIRS),
        ),
        in_specs=[pl.BlockSpec(memory_space=pltpu.SMEM), hbm, vmem, vmem, vmem] + [hbm] * 4,
        scratch=[pltpu.SMEM((1, SLOTS), jnp.int32), pltpu.SemaphoreType.DMA((5,))],
        moved=MIB // 4,
        name="phase",
    )
    h_one, *edge = call(
        magnetic_kernel,
        (dense,) + faces,
        (e_old, h_old, *near),
        flops=10**11,
        moved=100 * MIB,
        name="magnetic",
    )
    edge = shifted(edge, up)
    spread_now = call(
        functools.partial(scatter_kernel, 0),
        shape(4, ROWS, CZ),
        (placed, fields),
        scratch=SCATTER,
        name="scatter",
    )
    e_one, *near, rates = call(
        electric_kernel,
        (dense,) + faces + (shape(4, ROWS, CZ),),
        (e_old, h_one, *edge, eps, spread_now),
        name="electric",
    )
    near = shifted(near, down)
    spread_next, early = call(
        scatter_sample_kernel,
        (shape(4, ROWS, CZ), shape(8, CZ)),
        (placed, fields, e_one, h_one, surf),
        scratch=SCATTER,
        name="scatter2",
    )
    *near, spread_next = lax.optimization_barrier((*near, spread_next))
    h_two, *edge = call(magnetic_kernel, (dense,) + faces, (e_one, h_one, *near), name="magnetic2")
    edge = shifted(edge, up)
    e_seen, h_two = lax.optimization_barrier((e_one, h_two))
    drives = call(
        drive_kernel,
        shape(6, SLOTS, CZ),
        (e_old, e_seen, placed),
        scratch=[pltpu.VMEM((12 * HALF, WIDE), BF16)],
        name="drive",
    )
    *edge, drives = lax.optimization_barrier((*edge, drives))
    part = shape(12 * FREQ // 2, DIRS)
    e_two, keep, send = call(
        final_kernel,
        (dense, part, part),
        (e_one, h_two, *edge, eps, rates, spread_next, surf, early, starts, turn, factors),
        scratch=[pltpu.VMEM((8, CZ), F32), pltpu.VMEM((2, CZ, DIRS), F32)],
        name="final",
    )
    chip = keep + lax.ppermute(send, "gz", down[2])
    pieces = lax.all_to_all(chip.reshape(8, FAR, DIRS), "gy", 0, 0, tiled=True)
    load = shape(FAR + LOAD, CZ)
    total, *loads = call(
        fold_kernel, (shape(FAR, DIRS),) + (load,) * 3, (pieces, drives), name="fold"
    )
    loads = [
        lax.ppermute(
            value, "gx", [(a * 4 + z, (a ^ k) * 4 + z) for a in range(4) for z in range(4)]
        )
        for k, value in enumerate(loads, 1)
    ]
    total, kept, *loads = call(
        relay_kernel,
        (shape(FAR, DIRS), shape(LOAD, CZ)) + (load,) * 3,
        (total, drives, *loads),
        name="relay",
    )
    loads = [
        lax.ppermute(
            value, "gx", [(a * 4 + z, a * 4 + (z ^ k)) for a in range(4) for z in range(4)]
        )
        for k, value in enumerate(loads, 1)
    ]
    e_out, h_out = call(store_kernel, (dense, dense), (e_two, h_two), name="store")
    copies, back = call(
        finish_kernel,
        (shape(8, FAR, DIRS), shape(6, SLOTS, CZ)),
        (total, kept, *loads, far_part),
        name="finish",
    )
    state_out = call(
        atoms_kernel,
        shape(10, SLOTS, CZ),
        (state, pumps, back),
        name="atoms",
    )
    copies, state_out, e_out, h_out = lax.optimization_barrier((copies, state_out, e_out, h_out))
    gathered = lax.all_to_all(copies, "gy", 0, 0, tiled=True)
    far_out = jnp.transpose(gathered.reshape(12, FREQ // 2, DIRS), (1, 0, 2))
    return (
        e_out.reshape(efield.shape),
        h_out.reshape(hfield.shape),
        jnp.transpose(state_out, (1, 0, 2)).reshape(gain_state.shape),
        far_out,
    )


def solution(mesh):
    placed = (
        P(None, "gx", "gy", "gz"),
        P(None, "gx", "gy", "gz"),
        P("gx", "gy", "gz"),
        P("gx", "gy", "gz", None, None, None),
        P("gx", "gy", "gz", None, None),
        P("gx", "gy", "gz", None, None),
        P("gx", "gy", "gz"),
        P("gx", "gy", "gz", None),
        P("gx", "gy", "gz", None),
        P("gz", None, None),
    )
    return jax.shard_map(
        local,
        mesh=mesh,
        in_specs=placed,
        out_specs=(
            P(None, "gx", "gy", "gz"),
            P(None, "gx", "gy", "gz"),
            P("gx", "gy", "gz", None, None, None),
            P("gz", None, None),
        ),
        check_vma=False,
    )
```

```python
import math

import jax
import jax.numpy as jnp
import numpy as np
from jax import lax
from jax.experimental import pallas as pl
from jax.experimental.pallas import tpu as pltpu
from jax.sharding import PartitionSpec as P

FREQ = 64
STEPS = 2
CX = 8
CY = 24
CZ = 128
ROWS = CX * CY
SLOTS = 32
DIRS = 128

time_step = 0.5
damping = 0.1
omega_rest = 1.0
coupling = 0.5
cross_rate = 0.3
upper_life = 2.0
lasing_life = 20.0
lower_life = 2.0
freq_low = 0.3
freq_pitch = 0.01
golden = 2.399963229728653

half = 0.5 * damping * time_step
keep_rate = (1.0 - half) / (1.0 + half)
spring = time_step * omega_rest * omega_rest / (1.0 + half)
gain_push = time_step * coupling / (1.0 + half)

F32 = jnp.float32
BF16 = jnp.bfloat16
MIB = 1 << 20


def shape(*dims, dtype=F32):
    return jax.ShapeDtypeStruct(dims, dtype)


def call(kernel, outs, args, in_specs=None, scratch=(), vmem=16, flops=0, moved=2 * MIB, name=None):
    return pl.pallas_call(
        kernel,
        out_shape=outs,
        in_specs=in_specs or [pl.BlockSpec(memory_space=pltpu.VMEM)] * len(args),
        scratch_shapes=scratch,
        compiler_params=pltpu.CompilerParams(vmem_limit_bytes=vmem * MIB),
        cost_estimate=pl.CostEstimate(flops=flops, bytes_accessed=moved, transcendentals=0),
        name=name,
    )(*args)


def stay(*values):
    return [pltpu.with_memory_space_constraint(value, pltpu.HBM) for value in values]


def split_parts(value):
    high = value.astype(BF16)
    low = (value - high.astype(F32)).astype(BF16)
    return high, low


def row_index(count, width):
    return lax.broadcasted_iota(jnp.int32, (count, width), 0)


def lane_index(count):
    return lax.broadcasted_iota(jnp.int32, (count, CZ), 1)


def ahead_x(field, face):
    return jnp.concatenate([field[CY:], face], axis=0)


def behind_x(field, face):
    return jnp.concatenate([face, field[:-CY]], axis=0)


def spread(face):
    return jnp.broadcast_to(face[:, None, :], (CX, CY, CZ)).reshape(ROWS, CZ)


def ahead_y(field, face, last):
    return jnp.where(last, spread(face), pltpu.roll(field, ROWS - 1, 0))


def behind_y(field, face, first):
    return jnp.where(first, spread(face), pltpu.roll(field, 1, 0))


def ahead_z(field, other, lane):
    return pltpu.roll(jnp.where(lane == 0, other, field), CZ - 1, 1)


def behind_z(field, other, lane):
    return pltpu.roll(jnp.where(lane == CZ - 1, other, field), 1, 1)


def row_in_brick():
    rows = row_index(ROWS, CZ)
    return rows - CY * ((rows * 2731) >> 16)


def first_layers(field_ref, out_x, out_y, out_z):
    out_x[0] = field_ref[1, 0:CY]
    out_x[1] = field_ref[2, 0:CY]
    for place, comp in ((0, 0), (1, 2)):
        for layer in range(CX):
            out_y[place, layer : layer + 1] = field_ref[comp, layer * CY : layer * CY + 1]
    out_z[0] = field_ref[0]
    out_z[1] = field_ref[1]


def last_layers(field_ref, out_x, out_y, out_z):
    out_x[0] = field_ref[1, ROWS - CY : ROWS]
    out_x[1] = field_ref[2, ROWS - CY : ROWS]
    for place, comp in ((0, 0), (1, 2)):
        for layer in range(CX):
            row = layer * CY + CY - 1
            out_y[place, layer : layer + 1] = field_ref[comp, row : row + 1]
    out_z[0] = field_ref[0]
    out_z[1] = field_ref[1]


def inside(faces, ahead):
    kept = []
    for face, axis in zip(faces, ("gx", "gy", "gz")):
        index = lax.axis_index(axis)
        real = index < lax.axis_size(axis) - 1 if ahead else index > 0
        kept.append([jnp.where(real, face[place], 0.0) for place in range(2)])
    return kept


def prepare_kernel(e_hbm, state_hbm, out_x, out_y, out_z, packed, e_out, state, sems):
    copies = [
        pltpu.make_async_copy(state_hbm, state, sems.at[0]),
        pltpu.make_async_copy(e_hbm, e_out, sems.at[1]),
    ]
    for copy in copies:
        copy.start()
    copies[0].wait()
    lower, lasing, upper = state[7], state[8], state[9]
    lasing_free = lasing + time_step * (upper / upper_life - lasing / lasing_life)
    lower_free = lower + time_step * (lasing / lasing_life - lower / lower_life)
    polar = [state[comp] for comp in range(3)]
    free = [keep_rate * state[3 + comp] - spring * polar[comp] for comp in range(3)]
    for field, value in enumerate(free + [lasing - lower] + polar + [lasing_free - lower_free]):
        for owner in range(SLOTS // 2):
            packed[owner, 2 * field : 2 * field + 2] = value[2 * owner : 2 * owner + 2]
    copies[1].wait()
    first_layers(e_out, out_x, out_y, out_z)


def magnetic_kernel(e_ref, h_ref, face_x, face_y, face_z, h_out, out_x, out_y, out_z):
    lane = lane_index(ROWS)
    last = row_in_brick() == CY - 1
    face_x, face_y, face_z = inside((face_x, face_y, face_z), True)
    ex, ey, ez = e_ref[0], e_ref[1], e_ref[2]
    first = (ahead_y(ez, face_y[1], last) - ez) - (ahead_z(ey, face_z[1], lane) - ey)
    second = (ahead_z(ex, face_z[0], lane) - ex) - (ahead_x(ez, face_x[1]) - ez)
    third = (ahead_x(ey, face_x[0]) - ey) - (ahead_y(ex, face_y[0], last) - ex)
    h_out[0] = h_ref[0] - time_step * first
    h_out[1] = h_ref[1] - time_step * second
    h_out[2] = h_ref[2] - time_step * third
    last_layers(h_out, out_x, out_y, out_z)


def electric_curl(h_ref, face_x, face_y, face_z):
    lane = lane_index(ROWS)
    start = row_in_brick() == 0
    face_x, face_y, face_z = inside((face_x, face_y, face_z), False)
    hx, hy, hz = h_ref[0], h_ref[1], h_ref[2]
    first = (hz - behind_y(hz, face_y[1], start)) - (hy - behind_z(hy, face_z[1], lane))
    second = (hx - behind_z(hx, face_z[0], lane)) - (hz - behind_x(hz, face_x[1]))
    third = (hy - behind_x(hy, face_x[0])) - (hx - behind_y(hx, face_y[0], start))
    return first, second, third


HALF = ROWS // 2
WIDE = 2 * CZ


def wide_hits(offsets, width):
    hits = row_index(WIDE, width) == (offsets & (WIDE - 1))
    return hits.astype(F32).astype(BF16)


def tall_hits(offsets, width):
    return row_index(HALF, width) == (offsets >> 8)


def place_fields(first, fields_ref, dense, tall, spots, columns):
    for slot in range(SLOTS):
        across = slice(slot * CZ, (slot + 1) * CZ)
        hits = tall[:, across].reshape(6, 16, CZ)
        values = fields_ref[slot // 2, pl.ds(2 * first + slot % 2, 4, 2), :]
        for place, part in enumerate(split_parts(values)):
            part = part.astype(F32)
            for field in range(4):
                row = jnp.broadcast_to(part[field : field + 1], (16, CZ)).astype(BF16)
                top = (4 * place + field) * HALF
                spots[top : top + HALF, across] = (hits * row[None]).reshape(HALF, CZ)
    total = lax.dot_general(
        spots[...], columns[...], (((1,), (1,)), ((), ())), preferred_element_type=F32
    )
    total = total[: 4 * HALF] + total[4 * HALF :]
    for field in range(4):
        got = total[field * HALF : (field + 1) * HALF]
        dense[field, pl.ds(0, HALF, 2), :] = got[:, :CZ]
        dense[field, pl.ds(1, HALF, 2), :] = got[:, CZ:]


def scatter_kernel(placed, fields_ref, dense, tall, columns, spots):
    for slot in range(SLOTS):
        line = placed[slot : slot + 1]
        across = slice(slot * CZ, (slot + 1) * CZ)
        columns[:, across] = wide_hits(line, CZ)
        tall[:, across] = tall_hits(line, CZ).astype(F32).astype(BF16)
    place_fields(0, fields_ref, dense, tall, spots, columns)


def scatter_sample_kernel(
    fields_ref, tall, columns, e_ref, h_ref, surf_ref, dense, sampled, spots
):
    place_fields(4, fields_ref, dense, tall, spots, columns)
    sample_rows(e_ref, h_ref, surf_ref, sampled)


def electric_kernel(
    e_ref, h_ref, face_x, face_y, face_z, eps_ref, dense, e_out, out_x, out_y, out_z, rates
):
    curls = electric_curl(h_ref, face_x, face_y, face_z)
    scaled = time_step * eps_ref[...]
    inversion = dense[3]
    power = jnp.zeros_like(inversion)
    for comp in range(3):
        field = e_ref[comp]
        rate = dense[comp] + gain_push * inversion * field
        power = power + field * rate
        rates[comp] = rate
        e_out[comp] = field + scaled * (curls[comp] - rate)
    rates[3] = power
    first_layers(e_out, out_x, out_y, out_z)


def paired(ref, comp):
    return jnp.concatenate(
        [ref[comp, pl.ds(0, HALF, 2), :], ref[comp, pl.ds(1, HALF, 2), :]], axis=1
    )


def stacked(fields):
    return jnp.concatenate(
        split_parts(jnp.concatenate([paired(ref, comp) for ref, comp in fields], axis=0)), axis=0
    )


def gather_lines(values, hits, offsets, width):
    tall = tall_hits(offsets, width)
    picked = jnp.dot(values, hits, preferred_element_type=F32)
    lines = []
    for field in range(6):
        rows = slice(field * HALF, (field + 1) * HALF)
        both = picked[rows] + picked[6 * HALF :][rows]
        lines.append(jnp.sum(jnp.where(tall, both, 0.0), axis=0, keepdims=True))
    return lines


TAKE = 16


def drive_kernel(e_old, e_new, placed, columns, drives, values):
    values[...] = stacked([(ref, comp) for ref in (e_old, e_new) for comp in range(3)])
    for group in range(0, SLOTS, TAKE):
        offsets = jnp.concatenate([placed[group + n : group + n + 1] for n in range(TAKE)], axis=1)
        hits = columns[:, group * CZ : (group + TAKE) * CZ]
        got = gather_lines(values[...], hits, offsets, TAKE * CZ)
        for field in range(6):
            for slot in range(TAKE):
                drives[field, group + slot : group + slot + 1] = got[field][
                    :, slot * CZ : (slot + 1) * CZ
                ]


def sample_rows(e_ref, h_ref, surf_ref, sampled):
    values = stacked([(ref, comp) for ref in (e_ref, h_ref) for comp in range(3)])
    offsets = surf_ref[...]
    got = gather_lines(values, wide_hits(offsets, CZ), offsets, CZ)
    sampled[...] = jnp.zeros_like(sampled)
    for field in range(6):
        sampled[field : field + 1] = got[field]


def times(left, right):
    return (left[0] * right[0] - left[1] * right[1], left[1] * right[0] + left[0] * right[1])


def phase_kernel(
    count_ref,
    owner_hbm,
    offsets_hbm,
    surf_hbm,
    units_hbm,
    h_hbm,
    eps_hbm,
    pump_hbm,
    far_hbm,
    placed,
    surf_out,
    starts,
    turn,
    factors,
    h_out,
    eps_out,
    pump_out,
    far_out,
    owner_ref,
    offsets_ref,
    units_ref,
    sems,
):
    own = pl.ds(pl.multiple_of(FAR * lax.axis_index("gy"), 8), FAR)
    copies = [
        pltpu.make_async_copy(source, target, sems.at[place])
        for place, (source, target) in enumerate(
            (
                (surf_hbm, surf_out),
                (units_hbm, units_ref),
                (owner_hbm, owner_ref),
                (offsets_hbm, offsets_ref),
                (h_hbm, h_out),
                (eps_hbm, eps_out),
                (pump_hbm, pump_out),
                (far_hbm.at[own], far_out),
            )
        )
    ]
    for copy in copies:
        copy.start()
    lanes = lax.broadcasted_iota(jnp.int32, (8, DIRS), 1)
    omega = freq_low + freq_pitch * (lanes & (FREQ - 1)).astype(F32)
    moment = omega * jnp.where(lanes < FREQ, time_step, 2.0 * time_step)
    for place, value in enumerate((jnp.cos(moment), jnp.sin(moment))):
        factors[place] = jnp.transpose(jnp.broadcast_to(value[0:1], (DIRS, DIRS)))
    copies[0].wait()
    copies[1].wait()
    cells = surf_out[...]
    rows = cells >> 7
    layer = (rows * 2731) >> 16
    cell_x = lax.axis_index("gx") * CX + layer
    cell_y = lax.axis_index("gy") * CY + (rows - CY * layer)
    cell_z = lax.axis_index("gz") * CZ + (cells & (CZ - 1))
    along = jnp.zeros((CZ, DIRS), F32)
    for axis, (cell, size) in enumerate(((cell_x, 128), (cell_y, 192), (cell_z, 256))):
        place = cell.astype(F32) - 0.5 * (size - 1)
        column = jnp.transpose(jnp.broadcast_to(place, (CZ, CZ)))
        along = along + column * units_ref[axis : axis + 1]
    angle = (0.25 * freq_pitch) * along
    square = angle * angle
    cosine = 1.0 + square * (
        -1 / 2 + square * (1 / 24 + square * (-1 / 720 + square * (1 / 40320)))
    )
    sine = angle * (
        1.0 + square * (-1 / 6 + square * (1 / 120 + square * (-1 / 5040 + square * (1 / 362880))))
    )
    two = times((cosine, sine), (cosine, sine))
    powers = {1: times(two, two)}
    for power in (2, 4, 8, 16, 32):
        powers[power] = times(powers[power // 2], powers[power // 2])
    low_start = times(times(powers[16], powers[8]), times(powers[4], powers[2]))
    high_start = times(low_start, powers[32])
    turn[0], turn[1] = powers[1]
    starts[0], starts[1] = low_start
    starts[2], starts[3] = high_start
    for copy in copies[2:]:
        copy.wait()
    count = count_ref[0]
    for slot in range(SLOTS):
        line = offsets_ref[slot : slot + 1]
        placed[pl.ds(owner_ref[0, slot], 1)] = jnp.where(slot < count, line, -1)


FAR = 48
LOAD = 48


def partner(step):
    index = lax.axis_index("gx")
    return (index >> 2) ^ step, (index & 3) ^ step


def chunk(drives, owner_x):
    return drives[:, pl.ds(pl.multiple_of(8 * owner_x, 8), 8)]


def pick(tiles, pairs):
    rows = row_index(8, CZ) >> 1
    result = jnp.zeros((8, CZ), F32)
    for tile, (taken, put) in zip(tiles, pairs):
        moved = pltpu.roll(tile, (2 * put - 2 * taken + 8) & 7, 0)
        result = jnp.where(rows == put, moved, result)
    return result


def fold_kernel(pieces, drives, total, *loads):
    total[...] = jnp.sum(pieces[...], axis=0)
    for step in (1, 2, 3):
        load = loads[step - 1]
        load[0:FAR] = total[...]
        load[FAR:] = chunk(drives, partner(step)[0]).reshape(LOAD, CZ)


def relay_kernel(total_in, drives, one, two, three, total, kept, *loads):
    total[...] = (total_in[...] + one[0:FAR]) + (two[0:FAR] + three[0:FAR])
    held = [chunk(drives, partner(0)[0]).reshape(LOAD, CZ)]
    held += [arrived[FAR:] for arrived in (one, two, three)]
    for step in range(4):
        target = partner(step)[1]
        out, first = (loads[step - 1], FAR) if step else (kept, 0)
        if step:
            out[0:FAR] = total[...]
        for field in range(6):
            tiles = [value[8 * field : 8 * field + 8] for value in held]
            start = first + 8 * field
            out[start : start + 8] = pick(tiles, [(target, source) for source in range(4)])


def finish_kernel(total_in, kept, one, two, three, far_ref, spread_out, back):
    total = (total_in[...] + one[0:FAR]) + (two[0:FAR] + three[0:FAR])
    total = far_ref[...] + total
    for peer in range(8):
        spread_out[peer] = total
    held = [kept[...]] + [arrived[FAR:] for arrived in (one, two, three)]
    for source in range(4):
        rows = pl.ds(pl.multiple_of(8 * partner(source)[0], 8), 8)
        for field in range(6):
            tiles = [value[8 * field : 8 * field + 8] for value in held]
            back[field, rows] = pick(tiles, [(source, partner(step)[1]) for step in range(4)])


def final_kernel(
    e_ref,
    h_ref,
    face_x,
    face_y,
    face_z,
    eps_ref,
    rates,
    dense,
    surf_ref,
    early_ref,
    starts,
    turn,
    factors,
    e_out,
    keep_out,
    send_out,
    late,
    now,
):
    curls = electric_curl(h_ref, face_x, face_y, face_z)
    scaled = time_step * eps_ref[...]
    later = dense[3] + (2.0 * time_step * cross_rate) * rates[3]
    for comp in range(3):
        field = e_ref[comp]
        polar = dense[comp] + time_step * rates[comp]
        rate = keep_rate * rates[comp] - spring * polar + gain_push * later * field
        e_out[comp] = field + scaled * (curls[comp] - rate)
    sample_rows(e_out, h_ref, surf_ref, late)
    scale = 1.0 / math.sqrt(STEPS * CZ * 256)
    high, low = split_parts(scale * jnp.concatenate([early_ref[...], late[...]], axis=0))
    left = jnp.concatenate(
        [
            jnp.concatenate([high, high], axis=1),
            jnp.concatenate([low, jnp.zeros_like(low)], axis=1),
        ],
        axis=0,
    )
    own = lax.axis_index("gz")
    for side, out in ((1, send_out), (0, keep_out)):
        target = lax.rem(own + side, 2)
        now[0] = starts[2 * target]
        now[1] = starts[2 * target + 1]
        for freq in range(FREQ // 2):
            here = (now[0], now[1])
            re_high, re_low = split_parts(here[0])
            im_high, im_low = split_parts(here[1])
            right = jnp.concatenate(
                [
                    jnp.concatenate([re_high, im_high], axis=1),
                    jnp.concatenate([re_low, im_low], axis=1),
                ],
                axis=0,
            )
            now[0], now[1] = times(here, (turn[0], turn[1]))
            both = jnp.dot(left, right, preferred_element_type=F32)
            both = both[0:16] + both[16:32]
            real = jnp.zeros((8, DIRS), F32)
            imag = jnp.zeros((8, DIRS), F32)
            for step in range(STEPS):
                row = pl.ds(step * FREQ + target * (FREQ // 2) + freq, 1)
                cosine = factors[0, row]
                sine = factors[1, row]
                upper = both[8 * step : 8 * step + 8, 0:DIRS]
                under = both[8 * step : 8 * step + 8, DIRS:]
                real = real + (cosine * upper + sine * under)
                imag = imag + (cosine * under - sine * upper)
            for comp in range(6):
                row = comp * (FREQ // 2) + freq
                out[row : row + 1] = real[comp : comp + 1]
                row = (comp + 6) * (FREQ // 2) + freq
                out[row : row + 1] = imag[comp : comp + 1]


def atoms_kernel(state_ref, pump_ref, drives, out):
    polar = [state_ref[c] for c in range(3)]
    rate = [state_ref[3 + c] for c in range(3)]
    ground, lower, lasing, upper = [state_ref[6 + level] for level in range(4)]
    pump = pump_ref[...]
    for step in range(STEPS):
        drive = [drives[3 * step + c] for c in range(3)]
        inversion = lasing - lower
        power = jnp.zeros_like(pump)
        for c in range(3):
            rate[c] = (
                (1.0 - half) * rate[c]
                + time_step
                * (coupling * inversion * drive[c] - omega_rest * omega_rest * polar[c])
            ) / (1.0 + half)
            polar[c] = polar[c] + time_step * rate[c]
            power = power + drive[c] * rate[c]
        upper_new = upper + time_step * (pump * ground - upper / upper_life)
        lasing_new = lasing + time_step * (
            upper / upper_life - lasing / lasing_life + cross_rate * power
        )
        lower_new = lower + time_step * (
            lasing / lasing_life - lower / lower_life - cross_rate * power
        )
        ground = ground + time_step * (lower / lower_life - pump * ground)
        lower, lasing, upper = lower_new, lasing_new, upper_new
    for place, value in enumerate(polar + rate + [ground, lower, lasing, upper]):
        out[place] = value


def store_kernel(e_ref, h_ref, e_out, h_out):
    e_out[...] = e_ref[...]
    h_out[...] = h_ref[...]


def directions(count):
    index = np.arange(count, dtype=np.float32)
    cosine = np.float32(1.0) - np.float32(2.0) * (index + np.float32(0.5)) / np.float32(count)
    sine = np.sqrt(np.float32(1.0) - cosine * cosine)
    azimuth = (np.float32(golden) * index).astype(np.float64)
    rows = np.zeros((8, count), np.float32)
    rows[0] = sine * np.cos(azimuth).astype(np.float32)
    rows[1] = sine * np.sin(azimuth).astype(np.float32)
    rows[2] = cosine
    return rows


def local(
    efield,
    hfield,
    inv_eps,
    gain_state,
    pump,
    gain_offsets,
    gain_count,
    block_owner,
    surf_offsets,
    far_acc,
):
    dense = shape(3, ROWS, CZ)
    faces = (shape(2, CY, CZ), shape(2, CX, CZ), shape(2, ROWS, CZ))
    down = [[((i + 1) % n, i) for i in range(n)] for n in (16, 8, 2)]
    up = [[(i, (i + 1) % n) for i in range(n)] for n in (16, 8, 2)]
    vmem = pl.BlockSpec(memory_space=pltpu.VMEM)

    hbm = pl.BlockSpec(memory_space=pltpu.HBM)

    def shifted(parts, perms):
        return [
            lax.ppermute(part, axis, perm)
            for part, axis, perm in zip(parts, ("gx", "gy", "gz"), perms)
        ]

    *near, packed, e_old, state = call(
        prepare_kernel,
        faces + (shape(SLOTS // 2, 16, CZ), dense, shape(10, SLOTS, CZ)),
        stay(
            efield.reshape(3, ROWS, CZ),
            jnp.transpose(gain_state.reshape(SLOTS, 10, CZ), (1, 0, 2)),
        ),
        in_specs=[hbm] * 2,
        scratch=[pltpu.SemaphoreType.DMA((2,))],
        name="prepare",
    )
    near = shifted(near, down)
    fields = lax.all_to_all(packed, "gx", 0, 0, tiled=True)
    placed, surf, starts, turn, factors, h_old, eps, pumps, far_part = call(
        phase_kernel,
        (
            shape(SLOTS, CZ, dtype=jnp.int32),
            shape(1, CZ, dtype=jnp.int32),
            shape(4, CZ, DIRS),
            shape(2, CZ, DIRS),
            shape(2, STEPS * FREQ, DIRS),
            dense,
            shape(ROWS, CZ),
            shape(SLOTS, CZ),
            shape(FAR, DIRS),
        ),
        [gain_count.reshape(1)]
        + stay(
            block_owner.reshape(1, SLOTS),
            gain_offsets.reshape(SLOTS, CZ),
            surf_offsets.reshape(1, CZ),
            jnp.asarray(directions(DIRS)),
            hfield.reshape(3, ROWS, CZ),
            inv_eps.reshape(ROWS, CZ),
            pump.reshape(SLOTS, CZ),
            jnp.transpose(far_acc, (1, 0, 2)).reshape(8 * FAR, DIRS),
        ),
        in_specs=[pl.BlockSpec(memory_space=pltpu.SMEM)] + [hbm] * 8,
        scratch=[
            pltpu.SMEM((1, SLOTS), jnp.int32),
            pltpu.VMEM((SLOTS, CZ), jnp.int32),
            pltpu.VMEM((8, DIRS), F32),
            pltpu.SemaphoreType.DMA((8,)),
        ],
        moved=MIB // 4,
        name="phase",
    )
    h_one, *edge = call(
        magnetic_kernel,
        (dense,) + faces,
        (e_old, h_old, *near),
        flops=10**11,
        moved=100 * MIB,
        name="magnetic",
    )
    edge = shifted(edge, up)
    spots = pltpu.VMEM((8 * HALF, SLOTS * CZ), BF16)
    spread_now, tall, columns = call(
        scatter_kernel,
        (
            shape(4, ROWS, CZ),
            shape(HALF, SLOTS * CZ, dtype=BF16),
            shape(WIDE, SLOTS * CZ, dtype=BF16),
        ),
        (placed, fields),
        scratch=[spots],
        name="scatter",
    )
    e_one, *near, rates = call(
        electric_kernel,
        (dense,) + faces + (shape(4, ROWS, CZ),),
        (e_old, h_one, *edge, eps, spread_now),
        name="electric",
    )
    near = shifted(near, down)
    spread_next, early = call(
        scatter_sample_kernel,
        (shape(4, ROWS, CZ), shape(8, CZ)),
        (fields, tall, columns, e_one, h_one, surf),
        scratch=[spots],
        name="scatter2",
    )
    *near, spread_next = lax.optimization_barrier((*near, spread_next))
    h_two, *edge = call(magnetic_kernel, (dense,) + faces, (e_one, h_one, *near), name="magnetic2")
    edge = shifted(edge, up)
    e_seen, h_two = lax.optimization_barrier((e_one, h_two))
    drives = call(
        drive_kernel,
        shape(6, SLOTS, CZ),
        (e_old, e_seen, placed, columns),
        scratch=[pltpu.VMEM((12 * HALF, WIDE), BF16)],
        name="drive",
    )
    *edge, drives = lax.optimization_barrier((*edge, drives))
    part = shape(12 * FREQ // 2, DIRS)
    e_two, keep, send = call(
        final_kernel,
        (dense, part, part),
        (e_one, h_two, *edge, eps, rates, spread_next, surf, early, starts, turn, factors),
        scratch=[pltpu.VMEM((8, CZ), F32), pltpu.VMEM((2, CZ, DIRS), F32)],
        name="final",
    )
    chip = keep + lax.ppermute(send, "gz", down[2])
    pieces = lax.all_to_all(chip.reshape(8, FAR, DIRS), "gy", 0, 0, tiled=True)
    load = shape(FAR + LOAD, CZ)
    total, *loads = call(
        fold_kernel, (shape(FAR, DIRS),) + (load,) * 3, (pieces, drives), name="fold"
    )
    loads = [
        lax.ppermute(
            value, "gx", [(a * 4 + z, (a ^ k) * 4 + z) for a in range(4) for z in range(4)]
        )
        for k, value in enumerate(loads, 1)
    ]
    total, kept, *loads = call(
        relay_kernel,
        (shape(FAR, DIRS), shape(LOAD, CZ)) + (load,) * 3,
        (total, drives, *loads),
        name="relay",
    )
    loads = [
        lax.ppermute(
            value, "gx", [(a * 4 + z, a * 4 + (z ^ k)) for a in range(4) for z in range(4)]
        )
        for k, value in enumerate(loads, 1)
    ]
    e_out, h_out = call(store_kernel, (dense, dense), (e_two, h_two), name="store")
    copies, back = call(
        finish_kernel,
        (shape(8, FAR, DIRS), shape(6, SLOTS, CZ)),
        (total, kept, *loads, far_part),
        name="finish",
    )
    state_out = call(
        atoms_kernel,
        shape(10, SLOTS, CZ),
        (state, pumps, back),
        name="atoms",
    )
    copies, state_out, e_out, h_out = lax.optimization_barrier((copies, state_out, e_out, h_out))
    gathered = lax.all_to_all(copies, "gy", 0, 0, tiled=True)
    far_out = jnp.transpose(gathered.reshape(12, FREQ // 2, DIRS), (1, 0, 2))
    return (
        e_out.reshape(efield.shape),
        h_out.reshape(hfield.shape),
        jnp.transpose(state_out, (1, 0, 2)).reshape(gain_state.shape),
        far_out,
    )


def solution(mesh):
    placed = (
        P(None, "gx", "gy", "gz"),
        P(None, "gx", "gy", "gz"),
        P("gx", "gy", "gz"),
        P("gx", "gy", "gz", None, None, None),
        P("gx", "gy", "gz", None, None),
        P("gx", "gy", "gz", None, None),
        P("gx", "gy", "gz"),
        P("gx", "gy", "gz", None),
        P("gx", "gy", "gz", None),
        P("gz", None, None),
    )
    return jax.shard_map(
        local,
        mesh=mesh,
        in_specs=placed,
        out_specs=(
            P(None, "gx", "gy", "gz"),
            P(None, "gx", "gy", "gz"),
            P("gx", "gy", "gz", None, None, None),
            P("gz", None, None),
        ),
        check_vma=False,
    )
```

```python
import math

import jax
import jax.numpy as jnp
import numpy as np
from jax import lax
from jax.experimental import pallas as pl
from jax.experimental.pallas import tpu as pltpu
from jax.sharding import PartitionSpec as P

FREQ = 64
STEPS = 2
CX = 8
CY = 24
CZ = 128
ROWS = CX * CY
SLOTS = 32
DIRS = 128

time_step = 0.5
damping = 0.1
omega_rest = 1.0
coupling = 0.5
cross_rate = 0.3
upper_life = 2.0
lasing_life = 20.0
lower_life = 2.0
freq_low = 0.3
freq_pitch = 0.01
golden = 2.399963229728653

half = 0.5 * damping * time_step
keep_rate = (1.0 - half) / (1.0 + half)
spring = time_step * omega_rest * omega_rest / (1.0 + half)
gain_push = time_step * coupling / (1.0 + half)

F32 = jnp.float32
BF16 = jnp.bfloat16
MIB = 1 << 20


def shape(*dims, dtype=F32):
    return jax.ShapeDtypeStruct(dims, dtype)


def call(kernel, outs, args, in_specs=None, scratch=(), vmem=16, flops=0, moved=2 * MIB, name=None):
    return pl.pallas_call(
        kernel,
        out_shape=outs,
        in_specs=in_specs or [pl.BlockSpec(memory_space=pltpu.VMEM)] * len(args),
        scratch_shapes=scratch,
        compiler_params=pltpu.CompilerParams(vmem_limit_bytes=vmem * MIB),
        cost_estimate=pl.CostEstimate(flops=flops, bytes_accessed=moved, transcendentals=0),
        name=name,
    )(*args)


def stay(*values):
    return [pltpu.with_memory_space_constraint(value, pltpu.HBM) for value in values]


def split_parts(value):
    high = value.astype(BF16)
    low = (value - high.astype(F32)).astype(BF16)
    return high, low


def row_index(count, width):
    return lax.broadcasted_iota(jnp.int32, (count, width), 0)


def lane_index(count):
    return lax.broadcasted_iota(jnp.int32, (count, CZ), 1)


def ahead_x(field, face):
    return jnp.concatenate([field[CY:], face], axis=0)


def behind_x(field, face):
    return jnp.concatenate([face, field[:-CY]], axis=0)


def spread(face):
    return jnp.broadcast_to(face[:, None, :], (CX, CY, CZ)).reshape(ROWS, CZ)


def ahead_y(field, face, last):
    return jnp.where(last, spread(face), pltpu.roll(field, ROWS - 1, 0))


def behind_y(field, face, first):
    return jnp.where(first, spread(face), pltpu.roll(field, 1, 0))


def ahead_z(field, other, lane):
    return pltpu.roll(jnp.where(lane == 0, other, field), CZ - 1, 1)


def behind_z(field, other, lane):
    return pltpu.roll(jnp.where(lane == CZ - 1, other, field), 1, 1)


def row_in_brick():
    rows = row_index(ROWS, CZ)
    return rows - CY * ((rows * 2731) >> 16)


def first_layers(field_ref, out_x, out_y, out_z):
    out_x[0] = field_ref[1, 0:CY]
    out_x[1] = field_ref[2, 0:CY]
    for place, comp in ((0, 0), (1, 2)):
        for layer in range(CX):
            out_y[place, layer : layer + 1] = field_ref[comp, layer * CY : layer * CY + 1]
    out_z[0] = field_ref[0]
    out_z[1] = field_ref[1]


def last_layers(field_ref, out_x, out_y, out_z):
    out_x[0] = field_ref[1, ROWS - CY : ROWS]
    out_x[1] = field_ref[2, ROWS - CY : ROWS]
    for place, comp in ((0, 0), (1, 2)):
        for layer in range(CX):
            row = layer * CY + CY - 1
            out_y[place, layer : layer + 1] = field_ref[comp, row : row + 1]
    out_z[0] = field_ref[0]
    out_z[1] = field_ref[1]


def inside(faces, ahead):
    kept = []
    for face, axis in zip(faces, ("gx", "gy", "gz")):
        index = lax.axis_index(axis)
        real = index < lax.axis_size(axis) - 1 if ahead else index > 0
        kept.append([jnp.where(real, face[place], 0.0) for place in range(2)])
    return kept


def prepare_kernel(e_hbm, state_hbm, out_x, out_y, out_z, packed, e_out, state, sems):
    copies = [
        pltpu.make_async_copy(state_hbm, state, sems.at[0]),
        pltpu.make_async_copy(e_hbm, e_out, sems.at[1]),
    ]
    for copy in copies:
        copy.start()
    copies[0].wait()
    lower, lasing, upper = state[7], state[8], state[9]
    lasing_free = lasing + time_step * (upper / upper_life - lasing / lasing_life)
    lower_free = lower + time_step * (lasing / lasing_life - lower / lower_life)
    polar = [state[comp] for comp in range(3)]
    free = [keep_rate * state[3 + comp] - spring * polar[comp] for comp in range(3)]
    for field, value in enumerate(free + [lasing - lower] + polar + [lasing_free - lower_free]):
        for owner in range(SLOTS // 2):
            packed[owner, 2 * field : 2 * field + 2] = value[2 * owner : 2 * owner + 2]
    copies[1].wait()
    first_layers(e_out, out_x, out_y, out_z)


def magnetic_kernel(e_ref, h_ref, face_x, face_y, face_z, h_out, out_x, out_y, out_z):
    lane = lane_index(ROWS)
    last = row_in_brick() == CY - 1
    face_x, face_y, face_z = inside((face_x, face_y, face_z), True)
    ex, ey, ez = e_ref[0], e_ref[1], e_ref[2]
    first = (ahead_y(ez, face_y[1], last) - ez) - (ahead_z(ey, face_z[1], lane) - ey)
    second = (ahead_z(ex, face_z[0], lane) - ex) - (ahead_x(ez, face_x[1]) - ez)
    third = (ahead_x(ey, face_x[0]) - ey) - (ahead_y(ex, face_y[0], last) - ex)
    h_out[0] = h_ref[0] - time_step * first
    h_out[1] = h_ref[1] - time_step * second
    h_out[2] = h_ref[2] - time_step * third
    last_layers(h_out, out_x, out_y, out_z)


def electric_curl(h_ref, face_x, face_y, face_z):
    lane = lane_index(ROWS)
    start = row_in_brick() == 0
    face_x, face_y, face_z = inside((face_x, face_y, face_z), False)
    hx, hy, hz = h_ref[0], h_ref[1], h_ref[2]
    first = (hz - behind_y(hz, face_y[1], start)) - (hy - behind_z(hy, face_z[1], lane))
    second = (hx - behind_z(hx, face_z[0], lane)) - (hz - behind_x(hz, face_x[1]))
    third = (hy - behind_x(hy, face_x[0])) - (hx - behind_y(hx, face_y[0], start))
    return first, second, third


HALF = ROWS // 2
WIDE = 2 * CZ


def wide_hits(offsets, width):
    hits = row_index(WIDE, width) == (offsets & (WIDE - 1))
    return hits.astype(F32).astype(BF16)


def tall_hits(offsets, width):
    return row_index(HALF, width) == (offsets >> 8)


def place_fields(first, fields_ref, dense, tall, spots, columns):
    for slot in range(SLOTS):
        across = slice(slot * CZ, (slot + 1) * CZ)
        hits = tall[:, across].reshape(6, 16, CZ)
        values = fields_ref[slot // 2, pl.ds(2 * first + slot % 2, 4, 2), :]
        for place, part in enumerate(split_parts(values)):
            part = part.astype(F32)
            for field in range(4):
                row = jnp.broadcast_to(part[field : field + 1], (16, CZ)).astype(BF16)
                top = (4 * place + field) * HALF
                spots[top : top + HALF, across] = (hits * row[None]).reshape(HALF, CZ)
    total = lax.dot_general(
        spots[...], columns[...], (((1,), (1,)), ((), ())), preferred_element_type=F32
    )
    total = total[: 4 * HALF] + total[4 * HALF :]
    for field in range(4):
        got = total[field * HALF : (field + 1) * HALF]
        dense[field, pl.ds(0, HALF, 2), :] = got[:, :CZ]
        dense[field, pl.ds(1, HALF, 2), :] = got[:, CZ:]


def scatter_kernel(placed, fields_ref, dense, tall, columns, spots):
    for slot in range(SLOTS):
        line = placed[slot : slot + 1]
        across = slice(slot * CZ, (slot + 1) * CZ)
        columns[:, across] = wide_hits(line, CZ)
        tall[:, across] = tall_hits(line, CZ).astype(F32).astype(BF16)
    place_fields(0, fields_ref, dense, tall, spots, columns)


def scatter_sample_kernel(
    fields_ref, tall, columns, e_ref, h_ref, surf_ref, dense, sampled, spots
):
    place_fields(4, fields_ref, dense, tall, spots, columns)
    sample_rows(e_ref, h_ref, surf_ref, sampled)


def electric_kernel(
    e_ref, h_ref, face_x, face_y, face_z, eps_ref, dense, e_out, out_x, out_y, out_z, rates
):
    curls = electric_curl(h_ref, face_x, face_y, face_z)
    scaled = time_step * eps_ref[...]
    inversion = dense[3]
    power = jnp.zeros_like(inversion)
    for comp in range(3):
        field = e_ref[comp]
        rate = dense[comp] + gain_push * inversion * field
        power = power + field * rate
        rates[comp] = rate
        e_out[comp] = field + scaled * (curls[comp] - rate)
    rates[3] = power
    first_layers(e_out, out_x, out_y, out_z)


def paired(ref, comp):
    return jnp.concatenate(
        [ref[comp, pl.ds(0, HALF, 2), :], ref[comp, pl.ds(1, HALF, 2), :]], axis=1
    )


def stacked(fields):
    return jnp.concatenate(
        split_parts(jnp.concatenate([paired(ref, comp) for ref, comp in fields], axis=0)), axis=0
    )


def gather_lines(values, hits, offsets, width):
    tall = tall_hits(offsets, width)
    picked = jnp.dot(values, hits, preferred_element_type=F32)
    lines = []
    for field in range(6):
        rows = slice(field * HALF, (field + 1) * HALF)
        both = picked[rows] + picked[6 * HALF :][rows]
        lines.append(jnp.sum(jnp.where(tall, both, 0.0), axis=0, keepdims=True))
    return lines


TAKE = 16


def drive_kernel(e_old, e_new, placed, columns, drives, values):
    values[...] = stacked([(ref, comp) for ref in (e_old, e_new) for comp in range(3)])
    for group in range(0, SLOTS, TAKE):
        offsets = jnp.concatenate([placed[group + n : group + n + 1] for n in range(TAKE)], axis=1)
        hits = columns[:, group * CZ : (group + TAKE) * CZ]
        got = gather_lines(values[...], hits, offsets, TAKE * CZ)
        for field in range(6):
            for slot in range(TAKE):
                drives[field, group + slot : group + slot + 1] = got[field][
                    :, slot * CZ : (slot + 1) * CZ
                ]


def sample_rows(e_ref, h_ref, surf_ref, sampled):
    values = stacked([(ref, comp) for ref in (e_ref, h_ref) for comp in range(3)])
    offsets = surf_ref[...]
    got = gather_lines(values, wide_hits(offsets, CZ), offsets, CZ)
    sampled[...] = jnp.zeros_like(sampled)
    for field in range(6):
        sampled[field : field + 1] = got[field]


def times(left, right):
    return (left[0] * right[0] - left[1] * right[1], left[1] * right[0] + left[0] * right[1])


def phase_kernel(
    count_ref,
    owner_hbm,
    offsets_hbm,
    surf_hbm,
    units_hbm,
    h_hbm,
    eps_hbm,
    pump_hbm,
    far_hbm,
    placed,
    surf_out,
    starts,
    turn,
    factors,
    h_out,
    eps_out,
    pump_out,
    far_out,
    owner_ref,
    offsets_ref,
    units_ref,
    sems,
):
    own = pl.ds(pl.multiple_of(FAR * lax.axis_index("gy"), 8), FAR)
    copies = [
        pltpu.make_async_copy(source, target, sems.at[place])
        for place, (source, target) in enumerate(
            (
                (surf_hbm, surf_out),
                (units_hbm, units_ref),
                (owner_hbm, owner_ref),
                (offsets_hbm, offsets_ref),
                (h_hbm, h_out),
                (eps_hbm, eps_out),
                (pump_hbm, pump_out),
                (far_hbm.at[own], far_out),
            )
        )
    ]
    for copy in copies:
        copy.start()
    lanes = lax.broadcasted_iota(jnp.int32, (8, DIRS), 1)
    omega = freq_low + freq_pitch * (lanes & (FREQ - 1)).astype(F32)
    moment = omega * jnp.where(lanes < FREQ, time_step, 2.0 * time_step)
    for place, value in enumerate((jnp.cos(moment), jnp.sin(moment))):
        factors[place] = jnp.transpose(jnp.broadcast_to(value[0:1], (DIRS, DIRS)))
    copies[0].wait()
    copies[1].wait()
    cells = surf_out[...]
    rows = cells >> 7
    layer = (rows * 2731) >> 16
    cell_x = lax.axis_index("gx") * CX + layer
    cell_y = lax.axis_index("gy") * CY + (rows - CY * layer)
    cell_z = lax.axis_index("gz") * CZ + (cells & (CZ - 1))
    along = jnp.zeros((CZ, DIRS), F32)
    for axis, (cell, size) in enumerate(((cell_x, 128), (cell_y, 192), (cell_z, 256))):
        place = cell.astype(F32) - 0.5 * (size - 1)
        column = jnp.transpose(jnp.broadcast_to(place, (CZ, CZ)))
        along = along + column * units_ref[axis : axis + 1]
    angle = (0.25 * freq_pitch) * along
    square = angle * angle
    cosine = 1.0 + square * (
        -1 / 2 + square * (1 / 24 + square * (-1 / 720 + square * (1 / 40320)))
    )
    sine = angle * (
        1.0 + square * (-1 / 6 + square * (1 / 120 + square * (-1 / 5040 + square * (1 / 362880))))
    )
    two = times((cosine, sine), (cosine, sine))
    powers = {1: times(two, two)}
    for power in (2, 4, 8, 16, 32):
        powers[power] = times(powers[power // 2], powers[power // 2])
    low_start = times(times(powers[16], powers[8]), times(powers[4], powers[2]))
    high_start = times(low_start, powers[32])
    turn[0], turn[1] = powers[1]
    starts[0], starts[1] = low_start
    starts[2], starts[3] = high_start
    for copy in copies[2:]:
        copy.wait()
    count = count_ref[0]
    for slot in range(SLOTS):
        line = offsets_ref[slot : slot + 1]
        placed[pl.ds(owner_ref[0, slot], 1)] = jnp.where(slot < count, line, -1)


FAR = 48
LOAD = 48


def partner(step):
    index = lax.axis_index("gx")
    return (index >> 2) ^ step, (index & 3) ^ step


def chunk(drives, owner_x):
    return drives[:, pl.ds(pl.multiple_of(8 * owner_x, 8), 8)]


def pick(tiles, pairs):
    rows = row_index(8, CZ) >> 1
    result = jnp.zeros((8, CZ), F32)
    for tile, (taken, put) in zip(tiles, pairs):
        moved = pltpu.roll(tile, (2 * put - 2 * taken + 8) & 7, 0)
        result = jnp.where(rows == put, moved, result)
    return result


def fold_kernel(pieces, drives, total, *loads):
    total[...] = jnp.sum(pieces[...], axis=0)
    for step in (1, 2, 3):
        load = loads[step - 1]
        load[0:FAR] = total[...]
        load[FAR : FAR + LOAD] = chunk(drives, partner(step)[0]).reshape(LOAD, CZ)
    loads[1][FAR + LOAD :] = jnp.zeros((8, CZ), F32)


def relay_kernel(total_in, drives, one, two, three, total, kept, *loads):
    total[...] = (total_in[...] + one[0:FAR]) + (two[0:FAR] + three[0:FAR])
    held = [chunk(drives, partner(0)[0]).reshape(LOAD, CZ)]
    held += [arrived[FAR : FAR + LOAD] for arrived in (one, two, three)]
    for step in range(4):
        target = partner(step)[1]
        out, first = (loads[step - 1], FAR) if step else (kept, 0)
        if step:
            out[0:FAR] = total[...]
        for field in range(6):
            tiles = [value[8 * field : 8 * field + 8] for value in held]
            start = first + 8 * field
            out[start : start + 8] = pick(tiles, [(target, source) for source in range(4)])
    loads[1][FAR + LOAD :] = jnp.zeros((8, CZ), F32)


def finish_kernel(total_in, kept, one, two, three, far_ref, spread_out, back):
    total = (total_in[...] + one[0:FAR]) + (two[0:FAR] + three[0:FAR])
    total = far_ref[...] + total
    for peer in range(8):
        spread_out[peer] = total
    held = [kept[...]] + [arrived[FAR : FAR + LOAD] for arrived in (one, two, three)]
    for source in range(4):
        rows = pl.ds(pl.multiple_of(8 * partner(source)[0], 8), 8)
        for field in range(6):
            tiles = [value[8 * field : 8 * field + 8] for value in held]
            back[field, rows] = pick(tiles, [(source, partner(step)[1]) for step in range(4)])


def final_kernel(
    e_ref,
    h_ref,
    face_x,
    face_y,
    face_z,
    eps_ref,
    rates,
    dense,
    surf_ref,
    early_ref,
    starts,
    turn,
    factors,
    e_out,
    keep_out,
    send_out,
    late,
    now,
):
    curls = electric_curl(h_ref, face_x, face_y, face_z)
    scaled = time_step * eps_ref[...]
    later = dense[3] + (2.0 * time_step * cross_rate) * rates[3]
    for comp in range(3):
        field = e_ref[comp]
        polar = dense[comp] + time_step * rates[comp]
        rate = keep_rate * rates[comp] - spring * polar + gain_push * later * field
        e_out[comp] = field + scaled * (curls[comp] - rate)
    sample_rows(e_out, h_ref, surf_ref, late)
    scale = 1.0 / math.sqrt(STEPS * CZ * 256)
    high, low = split_parts(scale * jnp.concatenate([early_ref[...], late[...]], axis=0))
    left = jnp.concatenate(
        [
            jnp.concatenate([high, high], axis=1),
            jnp.concatenate([low, jnp.zeros_like(low)], axis=1),
        ],
        axis=0,
    )
    own = lax.axis_index("gz")
    for side, out in ((1, send_out), (0, keep_out)):
        target = lax.rem(own + side, 2)
        now[0] = starts[2 * target]
        now[1] = starts[2 * target + 1]
        for freq in range(FREQ // 2):
            here = (now[0], now[1])
            re_high, re_low = split_parts(here[0])
            im_high, im_low = split_parts(here[1])
            right = jnp.concatenate(
                [
                    jnp.concatenate([re_high, im_high], axis=1),
                    jnp.concatenate([re_low, im_low], axis=1),
                ],
                axis=0,
            )
            now[0], now[1] = times(here, (turn[0], turn[1]))
            both = jnp.dot(left, right, preferred_element_type=F32)
            both = both[0:16] + both[16:32]
            real = jnp.zeros((8, DIRS), F32)
            imag = jnp.zeros((8, DIRS), F32)
            for step in range(STEPS):
                row = pl.ds(step * FREQ + target * (FREQ // 2) + freq, 1)
                cosine = factors[0, row]
                sine = factors[1, row]
                upper = both[8 * step : 8 * step + 8, 0:DIRS]
                under = both[8 * step : 8 * step + 8, DIRS:]
                real = real + (cosine * upper + sine * under)
                imag = imag + (cosine * under - sine * upper)
            for comp in range(6):
                row = comp * (FREQ // 2) + freq
                out[row : row + 1] = real[comp : comp + 1]
                row = (comp + 6) * (FREQ // 2) + freq
                out[row : row + 1] = imag[comp : comp + 1]


def atoms_kernel(state_ref, pump_ref, drives, out):
    polar = [state_ref[c] for c in range(3)]
    rate = [state_ref[3 + c] for c in range(3)]
    ground, lower, lasing, upper = [state_ref[6 + level] for level in range(4)]
    pump = pump_ref[...]
    for step in range(STEPS):
        drive = [drives[3 * step + c] for c in range(3)]
        inversion = lasing - lower
        power = jnp.zeros_like(pump)
        for c in range(3):
            rate[c] = (
                (1.0 - half) * rate[c]
                + time_step
                * (coupling * inversion * drive[c] - omega_rest * omega_rest * polar[c])
            ) / (1.0 + half)
            polar[c] = polar[c] + time_step * rate[c]
            power = power + drive[c] * rate[c]
        upper_new = upper + time_step * (pump * ground - upper / upper_life)
        lasing_new = lasing + time_step * (
            upper / upper_life - lasing / lasing_life + cross_rate * power
        )
        lower_new = lower + time_step * (
            lasing / lasing_life - lower / lower_life - cross_rate * power
        )
        ground = ground + time_step * (lower / lower_life - pump * ground)
        lower, lasing, upper = lower_new, lasing_new, upper_new
    for place, value in enumerate(polar + rate + [ground, lower, lasing, upper]):
        out[place] = value


def store_kernel(e_ref, h_ref, e_out, h_out):
    e_out[...] = e_ref[...]
    h_out[...] = h_ref[...]


def directions(count):
    index = np.arange(count, dtype=np.float32)
    cosine = np.float32(1.0) - np.float32(2.0) * (index + np.float32(0.5)) / np.float32(count)
    sine = np.sqrt(np.float32(1.0) - cosine * cosine)
    azimuth = (np.float32(golden) * index).astype(np.float64)
    rows = np.zeros((8, count), np.float32)
    rows[0] = sine * np.cos(azimuth).astype(np.float32)
    rows[1] = sine * np.sin(azimuth).astype(np.float32)
    rows[2] = cosine
    return rows


def local(
    efield,
    hfield,
    inv_eps,
    gain_state,
    pump,
    gain_offsets,
    gain_count,
    block_owner,
    surf_offsets,
    far_acc,
):
    dense = shape(3, ROWS, CZ)
    faces = (shape(2, CY, CZ), shape(2, CX, CZ), shape(2, ROWS, CZ))
    down = [[((i + 1) % n, i) for i in range(n)] for n in (16, 8, 2)]
    up = [[(i, (i + 1) % n) for i in range(n)] for n in (16, 8, 2)]
    vmem = pl.BlockSpec(memory_space=pltpu.VMEM)

    hbm = pl.BlockSpec(memory_space=pltpu.HBM)

    def shifted(parts, perms):
        return [
            lax.ppermute(part, axis, perm)
            for part, axis, perm in zip(parts, ("gx", "gy", "gz"), perms)
        ]

    *near, packed, e_old, state = call(
        prepare_kernel,
        faces + (shape(SLOTS // 2, 16, CZ), dense, shape(10, SLOTS, CZ)),
        stay(
            efield.reshape(3, ROWS, CZ),
            jnp.transpose(gain_state.reshape(SLOTS, 10, CZ), (1, 0, 2)),
        ),
        in_specs=[hbm] * 2,
        scratch=[pltpu.SemaphoreType.DMA((2,))],
        name="prepare",
    )
    near = shifted(near, down)
    fields = lax.all_to_all(packed, "gx", 0, 0, tiled=True)
    placed, surf, starts, turn, factors, h_old, eps, pumps, far_part = call(
        phase_kernel,
        (
            shape(SLOTS, CZ, dtype=jnp.int32),
            shape(1, CZ, dtype=jnp.int32),
            shape(4, CZ, DIRS),
            shape(2, CZ, DIRS),
            shape(2, STEPS * FREQ, DIRS),
            dense,
            shape(ROWS, CZ),
            shape(SLOTS, CZ),
            shape(FAR, DIRS),
        ),
        [gain_count.reshape(1)]
        + stay(
            block_owner.reshape(1, SLOTS),
            gain_offsets.reshape(SLOTS, CZ),
            surf_offsets.reshape(1, CZ),
            jnp.asarray(directions(DIRS)),
            hfield.reshape(3, ROWS, CZ),
            inv_eps.reshape(ROWS, CZ),
            pump.reshape(SLOTS, CZ),
            jnp.transpose(far_acc, (1, 0, 2)).reshape(8 * FAR, DIRS),
        ),
        in_specs=[pl.BlockSpec(memory_space=pltpu.SMEM)] + [hbm] * 8,
        scratch=[
            pltpu.SMEM((1, SLOTS), jnp.int32),
            pltpu.VMEM((SLOTS, CZ), jnp.int32),
            pltpu.VMEM((8, DIRS), F32),
            pltpu.SemaphoreType.DMA((8,)),
        ],
        moved=MIB // 4,
        name="phase",
    )
    h_one, *edge = call(
        magnetic_kernel,
        (dense,) + faces,
        (e_old, h_old, *near),
        flops=10**11,
        moved=100 * MIB,
        name="magnetic",
    )
    edge = shifted(edge, up)
    spots = pltpu.VMEM((8 * HALF, SLOTS * CZ), BF16)
    spread_now, tall, columns = call(
        scatter_kernel,
        (
            shape(4, ROWS, CZ),
            shape(HALF, SLOTS * CZ, dtype=BF16),
            shape(WIDE, SLOTS * CZ, dtype=BF16),
        ),
        (placed, fields),
        scratch=[spots],
        name="scatter",
    )
    e_one, *near, rates = call(
        electric_kernel,
        (dense,) + faces + (shape(4, ROWS, CZ),),
        (e_old, h_one, *edge, eps, spread_now),
        name="electric",
    )
    near = shifted(near, down)
    spread_next, early = call(
        scatter_sample_kernel,
        (shape(4, ROWS, CZ), shape(8, CZ)),
        (fields, tall, columns, e_one, h_one, surf),
        scratch=[spots],
        name="scatter2",
    )
    *near, spread_next = lax.optimization_barrier((*near, spread_next))
    h_two, *edge = call(magnetic_kernel, (dense,) + faces, (e_one, h_one, *near), name="magnetic2")
    edge = shifted(edge, up)
    e_seen, h_two = lax.optimization_barrier((e_one, h_two))
    drives = call(
        drive_kernel,
        shape(6, SLOTS, CZ),
        (e_old, e_seen, placed, columns),
        scratch=[pltpu.VMEM((12 * HALF, WIDE), BF16)],
        name="drive",
    )
    *edge, drives = lax.optimization_barrier((*edge, drives))
    part = shape(12 * FREQ // 2, DIRS)
    e_two, keep, send = call(
        final_kernel,
        (dense, part, part),
        (e_one, h_two, *edge, eps, rates, spread_next, surf, early, starts, turn, factors),
        scratch=[pltpu.VMEM((8, CZ), F32), pltpu.VMEM((2, CZ, DIRS), F32)],
        name="final",
    )
    chip = keep + lax.ppermute(send, "gz", down[2])
    pieces = lax.all_to_all(chip.reshape(8, FAR, DIRS), "gy", 0, 0, tiled=True)
    loads = tuple(shape(FAR + LOAD + 8 * (step == 2), CZ) for step in (1, 2, 3))
    total, *sent = call(
        fold_kernel, (shape(FAR, DIRS),) + loads, (pieces, drives), name="fold"
    )
    got = [
        lax.ppermute(
            value, "gx", [(a * 4 + z, (a ^ k) * 4 + z) for a in range(4) for z in range(4)]
        )
        for k, value in enumerate(sent, 1)
    ]
    total, kept, *sent = call(
        relay_kernel,
        (shape(FAR, DIRS), shape(LOAD, CZ)) + loads,
        (total, drives, *got),
        name="relay",
    )
    got = [
        lax.ppermute(
            value, "gx", [(a * 4 + z, a * 4 + (z ^ k)) for a in range(4) for z in range(4)]
        )
        for k, value in enumerate(sent, 1)
    ]
    e_out, h_out = call(store_kernel, (dense, dense), (e_two, h_two), name="store")
    copies, back = call(
        finish_kernel,
        (shape(8, FAR, DIRS), shape(6, SLOTS, CZ)),
        (total, kept, *got, far_part),
        name="finish",
    )
    state_out = call(
        atoms_kernel,
        shape(10, SLOTS, CZ),
        (state, pumps, back),
        name="atoms",
    )
    copies, state_out, e_out, h_out = lax.optimization_barrier((copies, state_out, e_out, h_out))
    gathered = lax.all_to_all(copies, "gy", 0, 0, tiled=True)
    far_out = jnp.transpose(gathered.reshape(12, FREQ // 2, DIRS), (1, 0, 2))
    return (
        e_out.reshape(efield.shape),
        h_out.reshape(hfield.shape),
        jnp.transpose(state_out, (1, 0, 2)).reshape(gain_state.shape),
        far_out,
    )


def solution(mesh):
    placed = (
        P(None, "gx", "gy", "gz"),
        P(None, "gx", "gy", "gz"),
        P("gx", "gy", "gz"),
        P("gx", "gy", "gz", None, None, None),
        P("gx", "gy", "gz", None, None),
        P("gx", "gy", "gz", None, None),
        P("gx", "gy", "gz"),
        P("gx", "gy", "gz", None),
        P("gx", "gy", "gz", None),
        P("gz", None, None),
    )
    return jax.shard_map(
        local,
        mesh=mesh,
        in_specs=placed,
        out_specs=(
            P(None, "gx", "gy", "gz"),
            P(None, "gx", "gy", "gz"),
            P("gx", "gy", "gz", None, None, None),
            P("gz", None, None),
        ),
        check_vma=False,
    )
```

```python
import math

import jax
import jax.numpy as jnp
import numpy as np
from jax import lax
from jax.experimental import pallas as pl
from jax.experimental.pallas import tpu as pltpu
from jax.sharding import PartitionSpec as P

FREQ = 64
STEPS = 2
CX = 8
CY = 24
CZ = 128
ROWS = CX * CY
SLOTS = 32
DIRS = 128

time_step = 0.5
damping = 0.1
omega_rest = 1.0
coupling = 0.5
cross_rate = 0.3
upper_life = 2.0
lasing_life = 20.0
lower_life = 2.0
freq_low = 0.3
freq_pitch = 0.01
golden = 2.399963229728653

half = 0.5 * damping * time_step
keep_rate = (1.0 - half) / (1.0 + half)
spring = time_step * omega_rest * omega_rest / (1.0 + half)
gain_push = time_step * coupling / (1.0 + half)

F32 = jnp.float32
BF16 = jnp.bfloat16
MIB = 1 << 20


def shape(*dims, dtype=F32):
    return jax.ShapeDtypeStruct(dims, dtype)


def call(kernel, outs, args, in_specs=None, scratch=(), vmem=16, flops=0, moved=2 * MIB, name=None):
    return pl.pallas_call(
        kernel,
        out_shape=outs,
        in_specs=in_specs or [pl.BlockSpec(memory_space=pltpu.VMEM)] * len(args),
        scratch_shapes=scratch,
        compiler_params=pltpu.CompilerParams(vmem_limit_bytes=vmem * MIB),
        cost_estimate=pl.CostEstimate(flops=flops, bytes_accessed=moved, transcendentals=0),
        name=name,
    )(*args)


def stay(*values):
    return [pltpu.with_memory_space_constraint(value, pltpu.HBM) for value in values]


def split_parts(value):
    high = value.astype(BF16)
    low = (value - high.astype(F32)).astype(BF16)
    return high, low


def row_index(count, width):
    return lax.broadcasted_iota(jnp.int32, (count, width), 0)


def lane_index(count):
    return lax.broadcasted_iota(jnp.int32, (count, CZ), 1)


def ahead_x(field, face):
    return jnp.concatenate([field[CY:], face], axis=0)


def behind_x(field, face):
    return jnp.concatenate([face, field[:-CY]], axis=0)


def spread(face):
    return jnp.broadcast_to(face[:, None, :], (CX, CY, CZ)).reshape(ROWS, CZ)


def ahead_y(field, face, last):
    return jnp.where(last, spread(face), pltpu.roll(field, ROWS - 1, 0))


def behind_y(field, face, first):
    return jnp.where(first, spread(face), pltpu.roll(field, 1, 0))


def ahead_z(field, other, lane):
    return pltpu.roll(jnp.where(lane == 0, other, field), CZ - 1, 1)


def behind_z(field, other, lane):
    return pltpu.roll(jnp.where(lane == CZ - 1, other, field), 1, 1)


def row_in_brick():
    rows = row_index(ROWS, CZ)
    return rows - CY * ((rows * 2731) >> 16)


def first_layers(field_ref, out_x, out_y, out_z):
    out_x[0] = field_ref[1, 0:CY]
    out_x[1] = field_ref[2, 0:CY]
    for place, comp in ((0, 0), (1, 2)):
        for layer in range(CX):
            out_y[place, layer : layer + 1] = field_ref[comp, layer * CY : layer * CY + 1]
    out_z[0] = field_ref[0]
    out_z[1] = field_ref[1]


def last_layers(field_ref, out_x, out_y, out_z):
    out_x[0] = field_ref[1, ROWS - CY : ROWS]
    out_x[1] = field_ref[2, ROWS - CY : ROWS]
    for place, comp in ((0, 0), (1, 2)):
        for layer in range(CX):
            row = layer * CY + CY - 1
            out_y[place, layer : layer + 1] = field_ref[comp, row : row + 1]
    out_z[0] = field_ref[0]
    out_z[1] = field_ref[1]


def inside(faces, ahead):
    kept = []
    for face, axis in zip(faces, ("gx", "gy", "gz")):
        index = lax.axis_index(axis)
        real = index < lax.axis_size(axis) - 1 if ahead else index > 0
        kept.append([jnp.where(real, face[place], 0.0) for place in range(2)])
    return kept


def prepare_kernel(e_hbm, state_hbm, out_x, out_y, out_z, packed, e_out, state, sems):
    copies = [
        pltpu.make_async_copy(state_hbm, state, sems.at[0]),
        pltpu.make_async_copy(e_hbm, e_out, sems.at[1]),
    ]
    for copy in copies:
        copy.start()
    copies[0].wait()
    lower, lasing, upper = state[7], state[8], state[9]
    lasing_free = lasing + time_step * (upper / upper_life - lasing / lasing_life)
    lower_free = lower + time_step * (lasing / lasing_life - lower / lower_life)
    polar = [state[comp] for comp in range(3)]
    free = [keep_rate * state[3 + comp] - spring * polar[comp] for comp in range(3)]
    for field, value in enumerate(free + [lasing - lower] + polar + [lasing_free - lower_free]):
        for owner in range(SLOTS // 2):
            packed[owner, 2 * field : 2 * field + 2] = value[2 * owner : 2 * owner + 2]
    copies[1].wait()
    first_layers(e_out, out_x, out_y, out_z)


def magnetic_kernel(e_ref, h_ref, face_x, face_y, face_z, h_out, out_x, out_y, out_z):
    lane = lane_index(ROWS)
    last = row_in_brick() == CY - 1
    face_x, face_y, face_z = inside((face_x, face_y, face_z), True)
    ex, ey, ez = e_ref[0], e_ref[1], e_ref[2]
    first = (ahead_y(ez, face_y[1], last) - ez) - (ahead_z(ey, face_z[1], lane) - ey)
    second = (ahead_z(ex, face_z[0], lane) - ex) - (ahead_x(ez, face_x[1]) - ez)
    third = (ahead_x(ey, face_x[0]) - ey) - (ahead_y(ex, face_y[0], last) - ex)
    h_out[0] = h_ref[0] - time_step * first
    h_out[1] = h_ref[1] - time_step * second
    h_out[2] = h_ref[2] - time_step * third
    last_layers(h_out, out_x, out_y, out_z)


def electric_curl(h_ref, face_x, face_y, face_z):
    lane = lane_index(ROWS)
    start = row_in_brick() == 0
    face_x, face_y, face_z = inside((face_x, face_y, face_z), False)
    hx, hy, hz = h_ref[0], h_ref[1], h_ref[2]
    first = (hz - behind_y(hz, face_y[1], start)) - (hy - behind_z(hy, face_z[1], lane))
    second = (hx - behind_z(hx, face_z[0], lane)) - (hz - behind_x(hz, face_x[1]))
    third = (hy - behind_x(hy, face_x[0])) - (hx - behind_y(hx, face_y[0], start))
    return first, second, third


HALF = ROWS // 2
WIDE = 2 * CZ


def wide_hits(offsets, width):
    hits = row_index(WIDE, width) == (offsets & (WIDE - 1))
    return hits.astype(F32).astype(BF16)


def tall_hits(offsets, width):
    return row_index(HALF, width) == (offsets >> 8)


def place_fields(first, fields_ref, dense, tall, spots, columns):
    for slot in range(SLOTS):
        across = slice(slot * CZ, (slot + 1) * CZ)
        hits = tall[:, across].reshape(6, 16, CZ)
        values = fields_ref[slot // 2, pl.ds(2 * first + slot % 2, 4, 2), :]
        for place, part in enumerate(split_parts(values)):
            part = part.astype(F32)
            for field in range(4):
                row = jnp.broadcast_to(part[field : field + 1], (16, CZ)).astype(BF16)
                top = (4 * place + field) * HALF
                spots[top : top + HALF, across] = (hits * row[None]).reshape(HALF, CZ)
    total = lax.dot_general(
        spots[...], columns[...], (((1,), (1,)), ((), ())), preferred_element_type=F32
    )
    total = total[: 4 * HALF] + total[4 * HALF :]
    for field in range(4):
        got = total[field * HALF : (field + 1) * HALF]
        dense[field, pl.ds(0, HALF, 2), :] = got[:, :CZ]
        dense[field, pl.ds(1, HALF, 2), :] = got[:, CZ:]


def scatter_kernel(placed, fields_ref, dense, tall, columns, spots):
    for slot in range(SLOTS):
        line = placed[slot : slot + 1]
        across = slice(slot * CZ, (slot + 1) * CZ)
        columns[:, across] = wide_hits(line, CZ)
        tall[:, across] = tall_hits(line, CZ).astype(F32).astype(BF16)
    place_fields(0, fields_ref, dense, tall, spots, columns)


def scatter_sample_kernel(
    fields_ref, tall, columns, e_ref, h_ref, surf_ref, dense, sampled, spots
):
    place_fields(4, fields_ref, dense, tall, spots, columns)
    sample_rows(e_ref, h_ref, surf_ref, sampled)


def electric_kernel(
    e_ref, h_ref, face_x, face_y, face_z, eps_ref, dense, e_out, out_x, out_y, out_z, rates
):
    curls = electric_curl(h_ref, face_x, face_y, face_z)
    scaled = time_step * eps_ref[...]
    inversion = dense[3]
    power = jnp.zeros_like(inversion)
    for comp in range(3):
        field = e_ref[comp]
        rate = dense[comp] + gain_push * inversion * field
        power = power + field * rate
        rates[comp] = rate
        e_out[comp] = field + scaled * (curls[comp] - rate)
    rates[3] = power
    first_layers(e_out, out_x, out_y, out_z)


def paired(ref, comp):
    return jnp.concatenate(
        [ref[comp, pl.ds(0, HALF, 2), :], ref[comp, pl.ds(1, HALF, 2), :]], axis=1
    )


def stacked(fields):
    return jnp.concatenate(
        split_parts(jnp.concatenate([paired(ref, comp) for ref, comp in fields], axis=0)), axis=0
    )


def gather_lines(values, hits, offsets, width):
    tall = tall_hits(offsets, width)
    picked = jnp.dot(values, hits, preferred_element_type=F32)
    lines = []
    for field in range(6):
        rows = slice(field * HALF, (field + 1) * HALF)
        both = picked[rows] + picked[6 * HALF :][rows]
        lines.append(jnp.sum(jnp.where(tall, both, 0.0), axis=0, keepdims=True))
    return lines


TAKE = 16


def drive_kernel(e_old, e_new, placed, columns, drives, values):
    values[...] = stacked([(ref, comp) for ref in (e_old, e_new) for comp in range(3)])
    for group in range(0, SLOTS, TAKE):
        offsets = jnp.concatenate([placed[group + n : group + n + 1] for n in range(TAKE)], axis=1)
        hits = columns[:, group * CZ : (group + TAKE) * CZ]
        got = gather_lines(values[...], hits, offsets, TAKE * CZ)
        for field in range(6):
            for slot in range(TAKE):
                drives[field, group + slot : group + slot + 1] = got[field][
                    :, slot * CZ : (slot + 1) * CZ
                ]


def sample_rows(e_ref, h_ref, surf_ref, sampled):
    values = stacked([(ref, comp) for ref in (e_ref, h_ref) for comp in range(3)])
    offsets = surf_ref[...]
    got = gather_lines(values, wide_hits(offsets, CZ), offsets, CZ)
    sampled[...] = jnp.zeros_like(sampled)
    for field in range(6):
        sampled[field : field + 1] = got[field]


def times(left, right):
    return (left[0] * right[0] - left[1] * right[1], left[1] * right[0] + left[0] * right[1])


def phase_kernel(
    count_ref,
    owner_hbm,
    offsets_hbm,
    surf_hbm,
    units_hbm,
    h_hbm,
    eps_hbm,
    pump_hbm,
    far_hbm,
    placed,
    surf_out,
    starts,
    turn,
    factors,
    h_out,
    eps_out,
    pump_out,
    far_out,
    owner_ref,
    offsets_ref,
    units_ref,
    sems,
):
    own = pl.ds(pl.multiple_of(FAR * lax.axis_index("gy"), 8), FAR)
    copies = [
        pltpu.make_async_copy(source, target, sems.at[place])
        for place, (source, target) in enumerate(
            (
                (surf_hbm, surf_out),
                (units_hbm, units_ref),
                (owner_hbm, owner_ref),
                (offsets_hbm, offsets_ref),
                (h_hbm, h_out),
                (eps_hbm, eps_out),
                (pump_hbm, pump_out),
                (far_hbm.at[own], far_out),
            )
        )
    ]
    for copy in copies:
        copy.start()
    lanes = lax.broadcasted_iota(jnp.int32, (8, DIRS), 1)
    omega = freq_low + freq_pitch * (lanes & (FREQ - 1)).astype(F32)
    moment = omega * jnp.where(lanes < FREQ, time_step, 2.0 * time_step)
    for place, value in enumerate((jnp.cos(moment), jnp.sin(moment))):
        factors[place] = jnp.transpose(jnp.broadcast_to(value[0:1], (DIRS, DIRS)))
    copies[0].wait()
    copies[1].wait()
    cells = surf_out[...]
    rows = cells >> 7
    layer = (rows * 2731) >> 16
    cell_x = lax.axis_index("gx") * CX + layer
    cell_y = lax.axis_index("gy") * CY + (rows - CY * layer)
    cell_z = lax.axis_index("gz") * CZ + (cells & (CZ - 1))
    along = jnp.zeros((CZ, DIRS), F32)
    for axis, (cell, size) in enumerate(((cell_x, 128), (cell_y, 192), (cell_z, 256))):
        place = cell.astype(F32) - 0.5 * (size - 1)
        column = jnp.transpose(jnp.broadcast_to(place, (CZ, CZ)))
        along = along + column * units_ref[axis : axis + 1]
    angle = (0.25 * freq_pitch) * along
    square = angle * angle
    cosine = 1.0 + square * (
        -1 / 2 + square * (1 / 24 + square * (-1 / 720 + square * (1 / 40320)))
    )
    sine = angle * (
        1.0 + square * (-1 / 6 + square * (1 / 120 + square * (-1 / 5040 + square * (1 / 362880))))
    )
    two = times((cosine, sine), (cosine, sine))
    powers = {1: times(two, two)}
    for power in (2, 4, 8, 16, 32):
        powers[power] = times(powers[power // 2], powers[power // 2])
    low_start = times(times(powers[16], powers[8]), times(powers[4], powers[2]))
    high_start = times(low_start, powers[32])
    turn[0], turn[1] = powers[1]
    starts[0], starts[1] = low_start
    starts[2], starts[3] = high_start
    for copy in copies[2:]:
        copy.wait()
    count = count_ref[0]
    for slot in range(SLOTS):
        line = offsets_ref[slot : slot + 1]
        placed[pl.ds(owner_ref[0, slot], 1)] = jnp.where(slot < count, line, -1)


FAR = 48
LOAD = 48


def partner(step):
    index = lax.axis_index("gx")
    return (index >> 2) ^ step, (index & 3) ^ step


def chunk(drives, owner_x):
    return drives[:, pl.ds(pl.multiple_of(8 * owner_x, 8), 8)]


def pick(tiles, pairs):
    rows = row_index(8, CZ) >> 1
    result = jnp.zeros((8, CZ), F32)
    for tile, (taken, put) in zip(tiles, pairs):
        moved = pltpu.roll(tile, (2 * put - 2 * taken + 8) & 7, 0)
        result = jnp.where(rows == put, moved, result)
    return result


def fold_kernel(pieces, drives, total, *loads):
    total[...] = jnp.sum(pieces[...], axis=0)
    for step in (1, 2, 3):
        load = loads[step - 1]
        load[0:FAR] = total[...]
        load[FAR : FAR + LOAD] = chunk(drives, partner(step)[0]).reshape(LOAD, CZ)
    loads[1][FAR + LOAD :] = jnp.zeros((8, CZ), F32)


def relay_kernel(total_in, drives, one, two, three, total, kept, *loads):
    total[...] = (total_in[...] + one[0:FAR]) + (two[0:FAR] + three[0:FAR])
    held = [chunk(drives, partner(0)[0]).reshape(LOAD, CZ)]
    held += [arrived[FAR : FAR + LOAD] for arrived in (one, two, three)]
    for step in range(4):
        target = partner(step)[1]
        out, first = (loads[step - 1], FAR) if step else (kept, 0)
        if step:
            out[0:FAR] = total[...]
        for field in range(6):
            tiles = [value[8 * field : 8 * field + 8] for value in held]
            start = first + 8 * field
            out[start : start + 8] = pick(tiles, [(target, source) for source in range(4)])
    loads[1][FAR + LOAD :] = jnp.zeros((8, CZ), F32)


def finish_kernel(total_in, kept, one, two, three, far_ref, spread_out, back):
    total = (total_in[...] + one[0:FAR]) + (two[0:FAR] + three[0:FAR])
    total = far_ref[...] + total
    for peer in range(8):
        spread_out[peer] = total
    held = [kept[...]] + [arrived[FAR : FAR + LOAD] for arrived in (one, two, three)]
    for source in range(4):
        rows = pl.ds(pl.multiple_of(8 * partner(source)[0], 8), 8)
        for field in range(6):
            tiles = [value[8 * field : 8 * field + 8] for value in held]
            back[field, rows] = pick(tiles, [(source, partner(step)[1]) for step in range(4)])


def final_kernel(
    e_ref,
    h_ref,
    face_x,
    face_y,
    face_z,
    eps_ref,
    rates,
    dense,
    surf_ref,
    early_ref,
    starts,
    turn,
    factors,
    e_out,
    left_out,
    send_out,
    late,
    now,
):
    curls = electric_curl(h_ref, face_x, face_y, face_z)
    scaled = time_step * eps_ref[...]
    later = dense[3] + (2.0 * time_step * cross_rate) * rates[3]
    for comp in range(3):
        field = e_ref[comp]
        polar = dense[comp] + time_step * rates[comp]
        rate = keep_rate * rates[comp] - spring * polar + gain_push * later * field
        e_out[comp] = field + scaled * (curls[comp] - rate)
    sample_rows(e_out, h_ref, surf_ref, late)
    scale = 1.0 / math.sqrt(STEPS * CZ * 256)
    high, low = split_parts(scale * jnp.concatenate([early_ref[...], late[...]], axis=0))
    left = jnp.concatenate(
        [
            jnp.concatenate([high, high], axis=1),
            jnp.concatenate([low, jnp.zeros_like(low)], axis=1),
        ],
        axis=0,
    )
    left_out[...] = left
    far_half(1, left, starts, turn, factors, send_out, now)


def keep_kernel(left, starts, turn, factors, keep_out, now):
    far_half(0, left[...], starts, turn, factors, keep_out, now)


def far_half(side, left, starts, turn, factors, out, now):
    target = lax.rem(lax.axis_index("gz") + side, 2)
    now[0] = starts[2 * target]
    now[1] = starts[2 * target + 1]
    for freq in range(FREQ // 2):
        here = (now[0], now[1])
        re_high, re_low = split_parts(here[0])
        im_high, im_low = split_parts(here[1])
        right = jnp.concatenate(
            [
                jnp.concatenate([re_high, im_high], axis=1),
                jnp.concatenate([re_low, im_low], axis=1),
            ],
            axis=0,
        )
        if freq < FREQ // 2 - 1:
            now[0], now[1] = times(here, (turn[0], turn[1]))
        both = jnp.dot(left, right, preferred_element_type=F32)
        both = both[0:16] + both[16:32]
        real = jnp.zeros((8, DIRS), F32)
        imag = jnp.zeros((8, DIRS), F32)
        for step in range(STEPS):
            row = pl.ds(step * FREQ + target * (FREQ // 2) + freq, 1)
            cosine = factors[0, row]
            sine = factors[1, row]
            upper = both[8 * step : 8 * step + 8, 0:DIRS]
            under = both[8 * step : 8 * step + 8, DIRS:]
            real = real + (cosine * upper + sine * under)
            imag = imag + (cosine * under - sine * upper)
        for comp in range(6):
            row = comp * (FREQ // 2) + freq
            out[row : row + 1] = real[comp : comp + 1]
            row = (comp + 6) * (FREQ // 2) + freq
            out[row : row + 1] = imag[comp : comp + 1]


def atoms_kernel(state_ref, pump_ref, drives, out):
    polar = [state_ref[c] for c in range(3)]
    rate = [state_ref[3 + c] for c in range(3)]
    ground, lower, lasing, upper = [state_ref[6 + level] for level in range(4)]
    pump = pump_ref[...]
    for step in range(STEPS):
        drive = [drives[3 * step + c] for c in range(3)]
        inversion = lasing - lower
        power = jnp.zeros_like(pump)
        for c in range(3):
            rate[c] = (
                (1.0 - half) * rate[c]
                + time_step
                * (coupling * inversion * drive[c] - omega_rest * omega_rest * polar[c])
            ) / (1.0 + half)
            polar[c] = polar[c] + time_step * rate[c]
            power = power + drive[c] * rate[c]
        upper_new = upper + time_step * (pump * ground - upper / upper_life)
        lasing_new = lasing + time_step * (
            upper / upper_life - lasing / lasing_life + cross_rate * power
        )
        lower_new = lower + time_step * (
            lasing / lasing_life - lower / lower_life - cross_rate * power
        )
        ground = ground + time_step * (lower / lower_life - pump * ground)
        lower, lasing, upper = lower_new, lasing_new, upper_new
    for place, value in enumerate(polar + rate + [ground, lower, lasing, upper]):
        out[place] = value


def store_kernel(e_ref, h_ref, e_out, h_out):
    e_out[...] = e_ref[...]
    h_out[...] = h_ref[...]


def directions(count):
    index = np.arange(count, dtype=np.float32)
    cosine = np.float32(1.0) - np.float32(2.0) * (index + np.float32(0.5)) / np.float32(count)
    sine = np.sqrt(np.float32(1.0) - cosine * cosine)
    azimuth = (np.float32(golden) * index).astype(np.float64)
    rows = np.zeros((8, count), np.float32)
    rows[0] = sine * np.cos(azimuth).astype(np.float32)
    rows[1] = sine * np.sin(azimuth).astype(np.float32)
    rows[2] = cosine
    return rows


def local(
    efield,
    hfield,
    inv_eps,
    gain_state,
    pump,
    gain_offsets,
    gain_count,
    block_owner,
    surf_offsets,
    far_acc,
):
    dense = shape(3, ROWS, CZ)
    faces = (shape(2, CY, CZ), shape(2, CX, CZ), shape(2, ROWS, CZ))
    down = [[((i + 1) % n, i) for i in range(n)] for n in (16, 8, 2)]
    up = [[(i, (i + 1) % n) for i in range(n)] for n in (16, 8, 2)]
    vmem = pl.BlockSpec(memory_space=pltpu.VMEM)

    hbm = pl.BlockSpec(memory_space=pltpu.HBM)

    def shifted(parts, perms):
        return [
            lax.ppermute(part, axis, perm)
            for part, axis, perm in zip(parts, ("gx", "gy", "gz"), perms)
        ]

    *near, packed, e_old, state = call(
        prepare_kernel,
        faces + (shape(SLOTS // 2, 16, CZ), dense, shape(10, SLOTS, CZ)),
        stay(
            efield.reshape(3, ROWS, CZ),
            jnp.transpose(gain_state.reshape(SLOTS, 10, CZ), (1, 0, 2)),
        ),
        in_specs=[hbm] * 2,
        scratch=[pltpu.SemaphoreType.DMA((2,))],
        name="prepare",
    )
    near = shifted(near, down)
    fields = lax.all_to_all(packed, "gx", 0, 0, tiled=True)
    placed, surf, starts, turn, factors, h_old, eps, pumps, far_part = call(
        phase_kernel,
        (
            shape(SLOTS, CZ, dtype=jnp.int32),
            shape(1, CZ, dtype=jnp.int32),
            shape(4, CZ, DIRS),
            shape(2, CZ, DIRS),
            shape(2, STEPS * FREQ, DIRS),
            dense,
            shape(ROWS, CZ),
            shape(SLOTS, CZ),
            shape(FAR, DIRS),
        ),
        [gain_count.reshape(1)]
        + stay(
            block_owner.reshape(1, SLOTS),
            gain_offsets.reshape(SLOTS, CZ),
            surf_offsets.reshape(1, CZ),
            jnp.asarray(directions(DIRS)),
            hfield.reshape(3, ROWS, CZ),
            inv_eps.reshape(ROWS, CZ),
            pump.reshape(SLOTS, CZ),
            jnp.transpose(far_acc, (1, 0, 2)).reshape(8 * FAR, DIRS),
        ),
        in_specs=[pl.BlockSpec(memory_space=pltpu.SMEM)] + [hbm] * 8,
        scratch=[
            pltpu.SMEM((1, SLOTS), jnp.int32),
            pltpu.VMEM((SLOTS, CZ), jnp.int32),
            pltpu.VMEM((8, DIRS), F32),
            pltpu.SemaphoreType.DMA((8,)),
        ],
        moved=MIB // 4,
        name="phase",
    )
    h_one, *edge = call(
        magnetic_kernel,
        (dense,) + faces,
        (e_old, h_old, *near),
        flops=10**11,
        moved=100 * MIB,
        name="magnetic",
    )
    edge = shifted(edge, up)
    spots = pltpu.VMEM((8 * HALF, SLOTS * CZ), BF16)
    spread_now, tall, columns = call(
        scatter_kernel,
        (
            shape(4, ROWS, CZ),
            shape(HALF, SLOTS * CZ, dtype=BF16),
            shape(WIDE, SLOTS * CZ, dtype=BF16),
        ),
        (placed, fields),
        scratch=[spots],
        name="scatter",
    )
    e_one, *near, rates = call(
        electric_kernel,
        (dense,) + faces + (shape(4, ROWS, CZ),),
        (e_old, h_one, *edge, eps, spread_now),
        name="electric",
    )
    near = shifted(near, down)
    spread_next, early = call(
        scatter_sample_kernel,
        (shape(4, ROWS, CZ), shape(8, CZ)),
        (fields, tall, columns, e_one, h_one, surf),
        scratch=[spots],
        name="scatter2",
    )
    *near, spread_next = lax.optimization_barrier((*near, spread_next))
    h_two, *edge = call(magnetic_kernel, (dense,) + faces, (e_one, h_one, *near), name="magnetic2")
    edge = shifted(edge, up)
    e_seen, h_two = lax.optimization_barrier((e_one, h_two))
    drives = call(
        drive_kernel,
        shape(6, SLOTS, CZ),
        (e_old, e_seen, placed, columns),
        scratch=[pltpu.VMEM((12 * HALF, WIDE), BF16)],
        name="drive",
    )
    *edge, drives = lax.optimization_barrier((*edge, drives))
    part = shape(12 * FREQ // 2, DIRS)
    hold = pltpu.VMEM((2, CZ, DIRS), F32)
    e_two, left, send = call(
        final_kernel,
        (dense, shape(32, 2 * CZ, dtype=BF16), part),
        (e_one, h_two, *edge, eps, rates, spread_next, surf, early, starts, turn, factors),
        scratch=[pltpu.VMEM((8, CZ), F32), hold],
        name="final",
    )
    send = lax.ppermute(send, "gz", down[2])
    keep = call(
        keep_kernel, part, (left, starts, turn, factors), scratch=[hold], flops=10**10, name="keep"
    )
    chip = keep + send
    pieces = lax.all_to_all(chip.reshape(8, FAR, DIRS), "gy", 0, 0, tiled=True)
    loads = tuple(shape(FAR + LOAD + 8 * (step == 2), CZ) for step in (1, 2, 3))
    total, *sent = call(
        fold_kernel, (shape(FAR, DIRS),) + loads, (pieces, drives), name="fold"
    )
    got = [
        lax.ppermute(
            value, "gx", [(a * 4 + z, (a ^ k) * 4 + z) for a in range(4) for z in range(4)]
        )
        for k, value in enumerate(sent, 1)
    ]
    total, kept, *sent = call(
        relay_kernel,
        (shape(FAR, DIRS), shape(LOAD, CZ)) + loads,
        (total, drives, *got),
        name="relay",
    )
    got = [
        lax.ppermute(
            value, "gx", [(a * 4 + z, a * 4 + (z ^ k)) for a in range(4) for z in range(4)]
        )
        for k, value in enumerate(sent, 1)
    ]
    e_out, h_out = call(store_kernel, (dense, dense), (e_two, h_two), name="store")
    copies, back = call(
        finish_kernel,
        (shape(8, FAR, DIRS), shape(6, SLOTS, CZ)),
        (total, kept, *got, far_part),
        name="finish",
    )
    state_out = call(
        atoms_kernel,
        shape(10, SLOTS, CZ),
        (state, pumps, back),
        name="atoms",
    )
    copies, state_out, e_out, h_out = lax.optimization_barrier((copies, state_out, e_out, h_out))
    gathered = lax.all_to_all(copies, "gy", 0, 0, tiled=True)
    far_out = jnp.transpose(gathered.reshape(12, FREQ // 2, DIRS), (1, 0, 2))
    return (
        e_out.reshape(efield.shape),
        h_out.reshape(hfield.shape),
        jnp.transpose(state_out, (1, 0, 2)).reshape(gain_state.shape),
        far_out,
    )


def solution(mesh):
    placed = (
        P(None, "gx", "gy", "gz"),
        P(None, "gx", "gy", "gz"),
        P("gx", "gy", "gz"),
        P("gx", "gy", "gz", None, None, None),
        P("gx", "gy", "gz", None, None),
        P("gx", "gy", "gz", None, None),
        P("gx", "gy", "gz"),
        P("gx", "gy", "gz", None),
        P("gx", "gy", "gz", None),
        P("gz", None, None),
    )
    return jax.shard_map(
        local,
        mesh=mesh,
        in_specs=placed,
        out_specs=(
            P(None, "gx", "gy", "gz"),
            P(None, "gx", "gy", "gz"),
            P("gx", "gy", "gz", None, None, None),
            P("gz", None, None),
        ),
        check_vma=False,
    )
```

```python
import math

import jax
import jax.numpy as jnp
import numpy as np
from jax import lax
from jax.experimental import pallas as pl
from jax.experimental.pallas import tpu as pltpu
from jax.sharding import PartitionSpec as P

FREQ = 64
STEPS = 2
CX = 8
CY = 24
CZ = 128
ROWS = CX * CY
SLOTS = 32
DIRS = 128

time_step = 0.5
damping = 0.1
omega_rest = 1.0
coupling = 0.5
cross_rate = 0.3
upper_life = 2.0
lasing_life = 20.0
lower_life = 2.0
freq_low = 0.3
freq_pitch = 0.01
golden = 2.399963229728653

half = 0.5 * damping * time_step
keep_rate = (1.0 - half) / (1.0 + half)
spring = time_step * omega_rest * omega_rest / (1.0 + half)
gain_push = time_step * coupling / (1.0 + half)

F32 = jnp.float32
BF16 = jnp.bfloat16
MIB = 1 << 20


def shape(*dims, dtype=F32):
    return jax.ShapeDtypeStruct(dims, dtype)


def call(kernel, outs, args, in_specs=None, scratch=(), vmem=16, flops=0, moved=2 * MIB, name=None):
    return pl.pallas_call(
        kernel,
        out_shape=outs,
        in_specs=in_specs or [pl.BlockSpec(memory_space=pltpu.VMEM)] * len(args),
        scratch_shapes=scratch,
        compiler_params=pltpu.CompilerParams(vmem_limit_bytes=vmem * MIB),
        cost_estimate=pl.CostEstimate(flops=flops, bytes_accessed=moved, transcendentals=0),
        name=name,
    )(*args)


def stay(*values):
    return [pltpu.with_memory_space_constraint(value, pltpu.HBM) for value in values]


def split_parts(value):
    high = value.astype(BF16)
    low = (value - high.astype(F32)).astype(BF16)
    return high, low


def row_index(count, width):
    return lax.broadcasted_iota(jnp.int32, (count, width), 0)


def lane_index(count):
    return lax.broadcasted_iota(jnp.int32, (count, CZ), 1)


def ahead_x(field, face):
    return jnp.concatenate([field[CY:], face], axis=0)


def behind_x(field, face):
    return jnp.concatenate([face, field[:-CY]], axis=0)


def spread(face):
    return jnp.broadcast_to(face[:, None, :], (CX, CY, CZ)).reshape(ROWS, CZ)


def ahead_y(field, face, last):
    return jnp.where(last, spread(face), pltpu.roll(field, ROWS - 1, 0))


def behind_y(field, face, first):
    return jnp.where(first, spread(face), pltpu.roll(field, 1, 0))


def ahead_z(field, other, lane):
    return pltpu.roll(jnp.where(lane == 0, other, field), CZ - 1, 1)


def behind_z(field, other, lane):
    return pltpu.roll(jnp.where(lane == CZ - 1, other, field), 1, 1)


def row_in_brick():
    rows = row_index(ROWS, CZ)
    return rows - CY * ((rows * 2731) >> 16)


def first_layers(field_ref, out_x, out_y, out_z):
    out_x[0] = field_ref[1, 0:CY]
    out_x[1] = field_ref[2, 0:CY]
    for place, comp in ((0, 0), (1, 2)):
        for layer in range(CX):
            out_y[place, layer : layer + 1] = field_ref[comp, layer * CY : layer * CY + 1]
    out_z[0] = field_ref[0]
    out_z[1] = field_ref[1]


def last_layers(field_ref, out_x, out_y, out_z):
    out_x[0] = field_ref[1, ROWS - CY : ROWS]
    out_x[1] = field_ref[2, ROWS - CY : ROWS]
    for place, comp in ((0, 0), (1, 2)):
        for layer in range(CX):
            row = layer * CY + CY - 1
            out_y[place, layer : layer + 1] = field_ref[comp, row : row + 1]
    out_z[0] = field_ref[0]
    out_z[1] = field_ref[1]


def inside(faces, ahead):
    kept = []
    for face, axis in zip(faces, ("gx", "gy", "gz")):
        index = lax.axis_index(axis)
        real = index < lax.axis_size(axis) - 1 if ahead else index > 0
        kept.append([jnp.where(real, face[place], 0.0) for place in range(2)])
    return kept


def prepare_kernel(e_hbm, state_hbm, out_x, out_y, out_z, e_out, state, sems):
    copies = [
        pltpu.make_async_copy(e_hbm, e_out, sems.at[0]),
        pltpu.make_async_copy(state_hbm, state, sems.at[1]),
    ]
    for copy in copies:
        copy.start()
    copies[0].wait()
    first_layers(e_out, out_x, out_y, out_z)
    copies[1].wait()


def pack_kernel(state, packed):
    lower, lasing, upper = state[7], state[8], state[9]
    lasing_free = lasing + time_step * (upper / upper_life - lasing / lasing_life)
    lower_free = lower + time_step * (lasing / lasing_life - lower / lower_life)
    polar = [state[comp] for comp in range(3)]
    free = [keep_rate * state[3 + comp] - spring * polar[comp] for comp in range(3)]
    for field, value in enumerate(free + [lasing - lower] + polar + [lasing_free - lower_free]):
        for owner in range(SLOTS // 2):
            packed[owner, 2 * field : 2 * field + 2] = value[2 * owner : 2 * owner + 2]


def magnetic_kernel(e_ref, h_ref, face_x, face_y, face_z, h_out, out_x, out_y, out_z):
    lane = lane_index(ROWS)
    last = row_in_brick() == CY - 1
    face_x, face_y, face_z = inside((face_x, face_y, face_z), True)
    ex, ey, ez = e_ref[0], e_ref[1], e_ref[2]
    first = (ahead_y(ez, face_y[1], last) - ez) - (ahead_z(ey, face_z[1], lane) - ey)
    second = (ahead_z(ex, face_z[0], lane) - ex) - (ahead_x(ez, face_x[1]) - ez)
    third = (ahead_x(ey, face_x[0]) - ey) - (ahead_y(ex, face_y[0], last) - ex)
    h_out[0] = h_ref[0] - time_step * first
    h_out[1] = h_ref[1] - time_step * second
    h_out[2] = h_ref[2] - time_step * third
    last_layers(h_out, out_x, out_y, out_z)


def electric_curl(h_ref, face_x, face_y, face_z):
    lane = lane_index(ROWS)
    start = row_in_brick() == 0
    face_x, face_y, face_z = inside((face_x, face_y, face_z), False)
    hx, hy, hz = h_ref[0], h_ref[1], h_ref[2]
    first = (hz - behind_y(hz, face_y[1], start)) - (hy - behind_z(hy, face_z[1], lane))
    second = (hx - behind_z(hx, face_z[0], lane)) - (hz - behind_x(hz, face_x[1]))
    third = (hy - behind_x(hy, face_x[0])) - (hx - behind_y(hx, face_y[0], start))
    return first, second, third


HALF = ROWS // 2
WIDE = 2 * CZ


def wide_hits(offsets, width):
    hits = row_index(WIDE, width) == (offsets & (WIDE - 1))
    return hits.astype(F32).astype(BF16)


def tall_hits(offsets, width):
    return row_index(HALF, width) == (offsets >> 8)


def place_fields(first, fields_ref, dense, tall, spots, columns):
    for slot in range(SLOTS):
        across = slice(slot * CZ, (slot + 1) * CZ)
        hits = tall[:, across].reshape(6, 16, CZ)
        values = fields_ref[slot // 2, pl.ds(2 * first + slot % 2, 4, 2), :]
        for place, part in enumerate(split_parts(values)):
            part = part.astype(F32)
            for field in range(4):
                row = jnp.broadcast_to(part[field : field + 1], (16, CZ)).astype(BF16)
                top = (4 * place + field) * HALF
                spots[top : top + HALF, across] = (hits * row[None]).reshape(HALF, CZ)
    total = lax.dot_general(
        spots[...], columns[...], (((1,), (1,)), ((), ())), preferred_element_type=F32
    )
    total = total[: 4 * HALF] + total[4 * HALF :]
    for field in range(4):
        got = total[field * HALF : (field + 1) * HALF]
        dense[field, pl.ds(0, HALF, 2), :] = got[:, :CZ]
        dense[field, pl.ds(1, HALF, 2), :] = got[:, CZ:]


def scatter_kernel(placed, fields_ref, dense, tall, columns, spots):
    for slot in range(SLOTS):
        line = placed[slot : slot + 1]
        across = slice(slot * CZ, (slot + 1) * CZ)
        columns[:, across] = wide_hits(line, CZ)
        tall[:, across] = tall_hits(line, CZ).astype(F32).astype(BF16)
    place_fields(0, fields_ref, dense, tall, spots, columns)


def scatter_sample_kernel(
    fields_ref, tall, columns, e_ref, h_ref, surf_ref, dense, sampled, spots
):
    place_fields(4, fields_ref, dense, tall, spots, columns)
    sample_rows(e_ref, h_ref, surf_ref, sampled)


def electric_kernel(
    e_ref, h_ref, face_x, face_y, face_z, eps_ref, dense, e_out, out_x, out_y, out_z, rates
):
    curls = electric_curl(h_ref, face_x, face_y, face_z)
    scaled = time_step * eps_ref[...]
    inversion = dense[3]
    power = jnp.zeros_like(inversion)
    for comp in range(3):
        field = e_ref[comp]
        rate = dense[comp] + gain_push * inversion * field
        power = power + field * rate
        rates[comp] = rate
        e_out[comp] = field + scaled * (curls[comp] - rate)
    rates[3] = power
    first_layers(e_out, out_x, out_y, out_z)


def paired(ref, comp):
    return jnp.concatenate(
        [ref[comp, pl.ds(0, HALF, 2), :], ref[comp, pl.ds(1, HALF, 2), :]], axis=1
    )


def stacked(fields):
    return jnp.concatenate(
        split_parts(jnp.concatenate([paired(ref, comp) for ref, comp in fields], axis=0)), axis=0
    )


def gather_lines(values, hits, offsets, width):
    tall = tall_hits(offsets, width)
    picked = jnp.dot(values, hits, preferred_element_type=F32)
    lines = []
    for field in range(6):
        rows = slice(field * HALF, (field + 1) * HALF)
        both = picked[rows] + picked[6 * HALF :][rows]
        lines.append(jnp.sum(jnp.where(tall, both, 0.0), axis=0, keepdims=True))
    return lines


TAKE = 16


def drive_kernel(e_old, e_new, placed, columns, drives, values):
    values[...] = stacked([(ref, comp) for ref in (e_old, e_new) for comp in range(3)])
    for group in range(0, SLOTS, TAKE):
        offsets = jnp.concatenate([placed[group + n : group + n + 1] for n in range(TAKE)], axis=1)
        hits = columns[:, group * CZ : (group + TAKE) * CZ]
        got = gather_lines(values[...], hits, offsets, TAKE * CZ)
        for field in range(6):
            for slot in range(TAKE):
                drives[field, group + slot : group + slot + 1] = got[field][
                    :, slot * CZ : (slot + 1) * CZ
                ]


def sample_rows(e_ref, h_ref, surf_ref, sampled):
    values = stacked([(ref, comp) for ref in (e_ref, h_ref) for comp in range(3)])
    offsets = surf_ref[...]
    got = gather_lines(values, wide_hits(offsets, CZ), offsets, CZ)
    sampled[...] = jnp.zeros_like(sampled)
    for field in range(6):
        sampled[field : field + 1] = got[field]


def times(left, right):
    return (left[0] * right[0] - left[1] * right[1], left[1] * right[0] + left[0] * right[1])


def phase_kernel(
    count_ref,
    owner_hbm,
    offsets_hbm,
    surf_hbm,
    units_hbm,
    h_hbm,
    eps_hbm,
    pump_hbm,
    far_hbm,
    placed,
    surf_out,
    starts,
    turn,
    factors,
    h_out,
    eps_out,
    pump_out,
    far_out,
    owner_ref,
    offsets_ref,
    units_ref,
    sems,
):
    own = pl.ds(pl.multiple_of(FAR * lax.axis_index("gy"), 8), FAR)
    copies = [
        pltpu.make_async_copy(source, target, sems.at[place])
        for place, (source, target) in enumerate(
            (
                (surf_hbm, surf_out),
                (units_hbm, units_ref),
                (owner_hbm, owner_ref),
                (offsets_hbm, offsets_ref),
                (h_hbm, h_out),
                (eps_hbm, eps_out),
                (pump_hbm, pump_out),
                (far_hbm.at[own], far_out),
            )
        )
    ]
    for copy in copies:
        copy.start()
    lanes = lax.broadcasted_iota(jnp.int32, (8, DIRS), 1)
    omega = freq_low + freq_pitch * (lanes & (FREQ - 1)).astype(F32)
    moment = omega * jnp.where(lanes < FREQ, time_step, 2.0 * time_step)
    for place, value in enumerate((jnp.cos(moment), jnp.sin(moment))):
        factors[place] = jnp.transpose(jnp.broadcast_to(value[0:1], (DIRS, DIRS)))
    copies[0].wait()
    copies[1].wait()
    cells = surf_out[...]
    rows = cells >> 7
    layer = (rows * 2731) >> 16
    cell_x = lax.axis_index("gx") * CX + layer
    cell_y = lax.axis_index("gy") * CY + (rows - CY * layer)
    cell_z = lax.axis_index("gz") * CZ + (cells & (CZ - 1))
    along = jnp.zeros((CZ, DIRS), F32)
    for axis, (cell, size) in enumerate(((cell_x, 128), (cell_y, 192), (cell_z, 256))):
        place = cell.astype(F32) - 0.5 * (size - 1)
        column = jnp.transpose(jnp.broadcast_to(place, (CZ, CZ)))
        along = along + column * units_ref[axis : axis + 1]
    angle = (0.25 * freq_pitch) * along
    square = angle * angle
    cosine = 1.0 + square * (
        -1 / 2 + square * (1 / 24 + square * (-1 / 720 + square * (1 / 40320)))
    )
    sine = angle * (
        1.0 + square * (-1 / 6 + square * (1 / 120 + square * (-1 / 5040 + square * (1 / 362880))))
    )
    two = times((cosine, sine), (cosine, sine))
    powers = {1: times(two, two)}
    for power in (2, 4, 8, 16, 32):
        powers[power] = times(powers[power // 2], powers[power // 2])
    low_start = times(times(powers[16], powers[8]), times(powers[4], powers[2]))
    high_start = times(low_start, powers[32])
    turn[0], turn[1] = powers[1]
    starts[0], starts[1] = low_start
    starts[2], starts[3] = high_start
    for copy in copies[2:]:
        copy.wait()
    count = count_ref[0]
    for slot in range(SLOTS):
        line = offsets_ref[slot : slot + 1]
        placed[pl.ds(owner_ref[0, slot], 1)] = jnp.where(slot < count, line, -1)


FAR = 48
LOAD = 48


def partner(step):
    index = lax.axis_index("gx")
    return (index >> 2) ^ step, (index & 3) ^ step


def chunk(drives, owner_x):
    return drives[:, pl.ds(pl.multiple_of(8 * owner_x, 8), 8)]


def pick(tiles, pairs):
    rows = row_index(8, CZ) >> 1
    result = jnp.zeros((8, CZ), F32)
    for tile, (taken, put) in zip(tiles, pairs):
        moved = pltpu.roll(tile, (2 * put - 2 * taken + 8) & 7, 0)
        result = jnp.where(rows == put, moved, result)
    return result


def fold_kernel(pieces, drives, total, *loads):
    total[...] = jnp.sum(pieces[...], axis=0)
    for step in (1, 2, 3):
        load = loads[step - 1]
        load[0:FAR] = total[...]
        load[FAR : FAR + LOAD] = chunk(drives, partner(step)[0]).reshape(LOAD, CZ)
    loads[1][FAR + LOAD :] = jnp.zeros((8, CZ), F32)


def relay_kernel(total_in, drives, one, two, three, total, kept, *loads):
    total[...] = (total_in[...] + one[0:FAR]) + (two[0:FAR] + three[0:FAR])
    held = [chunk(drives, partner(0)[0]).reshape(LOAD, CZ)]
    held += [arrived[FAR : FAR + LOAD] for arrived in (one, two, three)]
    for step in range(4):
        target = partner(step)[1]
        out, first = (loads[step - 1], FAR) if step else (kept, 0)
        if step:
            out[0:FAR] = total[...]
        for field in range(6):
            tiles = [value[8 * field : 8 * field + 8] for value in held]
            start = first + 8 * field
            out[start : start + 8] = pick(tiles, [(target, source) for source in range(4)])
    loads[1][FAR + LOAD :] = jnp.zeros((8, CZ), F32)


def finish_kernel(total_in, kept, one, two, three, far_ref, spread_out, back):
    total = (total_in[...] + one[0:FAR]) + (two[0:FAR] + three[0:FAR])
    total = far_ref[...] + total
    for peer in range(8):
        spread_out[peer] = total
    held = [kept[...]] + [arrived[FAR : FAR + LOAD] for arrived in (one, two, three)]
    for source in range(4):
        rows = pl.ds(pl.multiple_of(8 * partner(source)[0], 8), 8)
        for field in range(6):
            tiles = [value[8 * field : 8 * field + 8] for value in held]
            back[field, rows] = pick(tiles, [(source, partner(step)[1]) for step in range(4)])


def final_kernel(
    e_ref,
    h_ref,
    face_x,
    face_y,
    face_z,
    eps_ref,
    rates,
    dense,
    surf_ref,
    early_ref,
    starts,
    turn,
    factors,
    e_out,
    left_out,
    send_out,
    late,
    now,
):
    curls = electric_curl(h_ref, face_x, face_y, face_z)
    scaled = time_step * eps_ref[...]
    later = dense[3] + (2.0 * time_step * cross_rate) * rates[3]
    for comp in range(3):
        field = e_ref[comp]
        polar = dense[comp] + time_step * rates[comp]
        rate = keep_rate * rates[comp] - spring * polar + gain_push * later * field
        e_out[comp] = field + scaled * (curls[comp] - rate)
    sample_rows(e_out, h_ref, surf_ref, late)
    scale = 1.0 / math.sqrt(STEPS * CZ * 256)
    high, low = split_parts(scale * jnp.concatenate([early_ref[...], late[...]], axis=0))
    left = jnp.concatenate(
        [
            jnp.concatenate([high, high], axis=1),
            jnp.concatenate([low, jnp.zeros_like(low)], axis=1),
        ],
        axis=0,
    )
    left_out[...] = left
    far_half(1, left, starts, turn, factors, send_out, now)


def keep_kernel(left, starts, turn, factors, keep_out, now):
    far_half(0, left[...], starts, turn, factors, keep_out, now)


def far_half(side, left, starts, turn, factors, out, now):
    target = lax.rem(lax.axis_index("gz") + side, 2)
    now[0] = starts[2 * target]
    now[1] = starts[2 * target + 1]
    for freq in range(FREQ // 2):
        here = (now[0], now[1])
        re_high, re_low = split_parts(here[0])
        im_high, im_low = split_parts(here[1])
        right = jnp.concatenate(
            [
                jnp.concatenate([re_high, im_high], axis=1),
                jnp.concatenate([re_low, im_low], axis=1),
            ],
            axis=0,
        )
        if freq < FREQ // 2 - 1:
            now[0], now[1] = times(here, (turn[0], turn[1]))
        both = jnp.dot(left, right, preferred_element_type=F32)
        both = both[0:16] + both[16:32]
        real = jnp.zeros((8, DIRS), F32)
        imag = jnp.zeros((8, DIRS), F32)
        for step in range(STEPS):
            row = pl.ds(step * FREQ + target * (FREQ // 2) + freq, 1)
            cosine = factors[0, row]
            sine = factors[1, row]
            upper = both[8 * step : 8 * step + 8, 0:DIRS]
            under = both[8 * step : 8 * step + 8, DIRS:]
            real = real + (cosine * upper + sine * under)
            imag = imag + (cosine * under - sine * upper)
        for comp in range(6):
            row = comp * (FREQ // 2) + freq
            out[row : row + 1] = real[comp : comp + 1]
            row = (comp + 6) * (FREQ // 2) + freq
            out[row : row + 1] = imag[comp : comp + 1]


def atoms_kernel(state_ref, pump_ref, drives, far_ref, out, far_out):
    far_out[...] = far_ref[...]
    polar = [state_ref[c] for c in range(3)]
    rate = [state_ref[3 + c] for c in range(3)]
    ground, lower, lasing, upper = [state_ref[6 + level] for level in range(4)]
    pump = pump_ref[...]
    for step in range(STEPS):
        drive = [drives[3 * step + c] for c in range(3)]
        inversion = lasing - lower
        power = jnp.zeros_like(pump)
        for c in range(3):
            rate[c] = (
                (1.0 - half) * rate[c]
                + time_step
                * (coupling * inversion * drive[c] - omega_rest * omega_rest * polar[c])
            ) / (1.0 + half)
            polar[c] = polar[c] + time_step * rate[c]
            power = power + drive[c] * rate[c]
        upper_new = upper + time_step * (pump * ground - upper / upper_life)
        lasing_new = lasing + time_step * (
            upper / upper_life - lasing / lasing_life + cross_rate * power
        )
        lower_new = lower + time_step * (
            lasing / lasing_life - lower / lower_life - cross_rate * power
        )
        ground = ground + time_step * (lower / lower_life - pump * ground)
        lower, lasing, upper = lower_new, lasing_new, upper_new
    for place, value in enumerate(polar + rate + [ground, lower, lasing, upper]):
        out[place] = value


def store_kernel(e_ref, h_ref, e_out, h_out):
    e_out[...] = e_ref[...]
    h_out[...] = h_ref[...]


def directions(count):
    index = np.arange(count, dtype=np.float32)
    cosine = np.float32(1.0) - np.float32(2.0) * (index + np.float32(0.5)) / np.float32(count)
    sine = np.sqrt(np.float32(1.0) - cosine * cosine)
    azimuth = (np.float32(golden) * index).astype(np.float64)
    rows = np.zeros((8, count), np.float32)
    rows[0] = sine * np.cos(azimuth).astype(np.float32)
    rows[1] = sine * np.sin(azimuth).astype(np.float32)
    rows[2] = cosine
    return rows


def local(
    efield,
    hfield,
    inv_eps,
    gain_state,
    pump,
    gain_offsets,
    gain_count,
    block_owner,
    surf_offsets,
    far_acc,
):
    dense = shape(3, ROWS, CZ)
    faces = (shape(2, CY, CZ), shape(2, CX, CZ), shape(2, ROWS, CZ))
    down = [[((i + 1) % n, i) for i in range(n)] for n in (16, 8, 2)]
    up = [[(i, (i + 1) % n) for i in range(n)] for n in (16, 8, 2)]
    vmem = pl.BlockSpec(memory_space=pltpu.VMEM)

    hbm = pl.BlockSpec(memory_space=pltpu.HBM)

    def shifted(parts, perms):
        return [
            lax.ppermute(part, axis, perm)
            for part, axis, perm in zip(parts, ("gx", "gy", "gz"), perms)
        ]

    *near, e_old, state = call(
        prepare_kernel,
        faces + (dense, shape(10, SLOTS, CZ)),
        stay(
            efield.reshape(3, ROWS, CZ),
            jnp.transpose(gain_state.reshape(SLOTS, 10, CZ), (1, 0, 2)),
        ),
        in_specs=[hbm] * 2,
        scratch=[pltpu.SemaphoreType.DMA((2,))],
        name="prepare",
    )
    near = shifted(near, down)
    packed = call(pack_kernel, shape(SLOTS // 2, 16, CZ), (state,), name="pack")
    fields = lax.all_to_all(packed, "gx", 0, 0, tiled=True)
    placed, surf, starts, turn, factors, h_old, eps, pumps, far_part = call(
        phase_kernel,
        (
            shape(SLOTS, CZ, dtype=jnp.int32),
            shape(1, CZ, dtype=jnp.int32),
            shape(4, CZ, DIRS),
            shape(2, CZ, DIRS),
            shape(2, STEPS * FREQ, DIRS),
            dense,
            shape(ROWS, CZ),
            shape(SLOTS, CZ),
            shape(FAR, DIRS),
        ),
        [gain_count.reshape(1)]
        + stay(
            block_owner.reshape(1, SLOTS),
            gain_offsets.reshape(SLOTS, CZ),
            surf_offsets.reshape(1, CZ),
            jnp.asarray(directions(DIRS)),
            hfield.reshape(3, ROWS, CZ),
            inv_eps.reshape(ROWS, CZ),
            pump.reshape(SLOTS, CZ),
            jnp.transpose(far_acc, (1, 0, 2)).reshape(8 * FAR, DIRS),
        ),
        in_specs=[pl.BlockSpec(memory_space=pltpu.SMEM)] + [hbm] * 8,
        scratch=[
            pltpu.SMEM((1, SLOTS), jnp.int32),
            pltpu.VMEM((SLOTS, CZ), jnp.int32),
            pltpu.VMEM((8, DIRS), F32),
            pltpu.SemaphoreType.DMA((8,)),
        ],
        moved=MIB // 4,
        name="phase",
    )
    h_one, *edge = call(
        magnetic_kernel,
        (dense,) + faces,
        (e_old, h_old, *near),
        flops=10**11,
        moved=100 * MIB,
        name="magnetic",
    )
    edge = shifted(edge, up)
    spots = pltpu.VMEM((8 * HALF, SLOTS * CZ), BF16)
    spread_now, tall, columns = call(
        scatter_kernel,
        (
            shape(4, ROWS, CZ),
            shape(HALF, SLOTS * CZ, dtype=BF16),
            shape(WIDE, SLOTS * CZ, dtype=BF16),
        ),
        (placed, fields),
        scratch=[spots],
        name="scatter",
    )
    e_one, *near, rates = call(
        electric_kernel,
        (dense,) + faces + (shape(4, ROWS, CZ),),
        (e_old, h_one, *edge, eps, spread_now),
        name="electric",
    )
    near = shifted(near, down)
    spread_next, early = call(
        scatter_sample_kernel,
        (shape(4, ROWS, CZ), shape(8, CZ)),
        (fields, tall, columns, e_one, h_one, surf),
        scratch=[spots],
        name="scatter2",
    )
    *near, spread_next = lax.optimization_barrier((*near, spread_next))
    h_two, *edge = call(magnetic_kernel, (dense,) + faces, (e_one, h_one, *near), name="magnetic2")
    edge = shifted(edge, up)
    e_seen, h_two = lax.optimization_barrier((e_one, h_two))
    drives = call(
        drive_kernel,
        shape(6, SLOTS, CZ),
        (e_old, e_seen, placed, columns),
        scratch=[pltpu.VMEM((12 * HALF, WIDE), BF16)],
        name="drive",
    )
    *edge, drives = lax.optimization_barrier((*edge, drives))
    part = shape(12 * FREQ // 2, DIRS)
    hold = pltpu.VMEM((2, CZ, DIRS), F32)
    e_two, left, send = call(
        final_kernel,
        (dense, shape(32, 2 * CZ, dtype=BF16), part),
        (e_one, h_two, *edge, eps, rates, spread_next, surf, early, starts, turn, factors),
        scratch=[pltpu.VMEM((8, CZ), F32), hold],
        name="final",
    )
    send = lax.ppermute(send, "gz", down[2])
    keep = call(
        keep_kernel, part, (left, starts, turn, factors), scratch=[hold], flops=10**10, name="keep"
    )
    chip = keep + send
    pieces = lax.all_to_all(chip.reshape(8, FAR, DIRS), "gy", 0, 0, tiled=True)
    loads = tuple(shape(FAR + LOAD + 8 * (step == 2), CZ) for step in (1, 2, 3))
    total, *sent = call(
        fold_kernel, (shape(FAR, DIRS),) + loads, (pieces, drives), name="fold"
    )
    got = [
        lax.ppermute(
            value, "gx", [(a * 4 + z, (a ^ k) * 4 + z) for a in range(4) for z in range(4)]
        )
        for k, value in enumerate(sent, 1)
    ]
    total, kept, *sent = call(
        relay_kernel,
        (shape(FAR, DIRS), shape(LOAD, CZ)) + loads,
        (total, drives, *got),
        name="relay",
    )
    got = [
        lax.ppermute(
            value, "gx", [(a * 4 + z, a * 4 + (z ^ k)) for a in range(4) for z in range(4)]
        )
        for k, value in enumerate(sent, 1)
    ]
    e_out, h_out = call(store_kernel, (dense, dense), (e_two, h_two), name="store")
    copies, back = call(
        finish_kernel,
        (shape(8, FAR, DIRS), shape(6, SLOTS, CZ)),
        (total, kept, *got, far_part),
        name="finish",
    )
    copies, e_out, h_out = lax.optimization_barrier((copies, e_out, h_out))
    gathered = lax.all_to_all(copies, "gy", 0, 0, tiled=True)
    back, gathered = lax.optimization_barrier((back, gathered))
    state_out, far_out = call(
        atoms_kernel,
        (shape(10, SLOTS, CZ), shape(8, FAR, DIRS)),
        (state, pumps, back, gathered),
        name="atoms",
    )
    far_out = jnp.transpose(far_out.reshape(12, FREQ // 2, DIRS), (1, 0, 2))
    return (
        e_out.reshape(efield.shape),
        h_out.reshape(hfield.shape),
        jnp.transpose(state_out, (1, 0, 2)).reshape(gain_state.shape),
        far_out,
    )


def solution(mesh):
    placed = (
        P(None, "gx", "gy", "gz"),
        P(None, "gx", "gy", "gz"),
        P("gx", "gy", "gz"),
        P("gx", "gy", "gz", None, None, None),
        P("gx", "gy", "gz", None, None),
        P("gx", "gy", "gz", None, None),
        P("gx", "gy", "gz"),
        P("gx", "gy", "gz", None),
        P("gx", "gy", "gz", None),
        P("gz", None, None),
    )
    return jax.shard_map(
        local,
        mesh=mesh,
        in_specs=placed,
        out_specs=(
            P(None, "gx", "gy", "gz"),
            P(None, "gx", "gy", "gz"),
            P("gx", "gy", "gz", None, None, None),
            P("gz", None, None),
        ),
        check_vma=False,
    )
```

```python
import math

import jax
import jax.numpy as jnp
import numpy as np
from jax import lax
from jax.experimental import pallas as pl
from jax.experimental.pallas import tpu as pltpu
from jax.sharding import PartitionSpec as P

FREQ = 64
STEPS = 2
CX = 8
CY = 24
CZ = 128
ROWS = CX * CY
SLOTS = 32
DIRS = 128

time_step = 0.5
damping = 0.1
omega_rest = 1.0
coupling = 0.5
cross_rate = 0.3
upper_life = 2.0
lasing_life = 20.0
lower_life = 2.0
freq_low = 0.3
freq_pitch = 0.01
golden = 2.399963229728653

half = 0.5 * damping * time_step
keep_rate = (1.0 - half) / (1.0 + half)
spring = time_step * omega_rest * omega_rest / (1.0 + half)
gain_push = time_step * coupling / (1.0 + half)

F32 = jnp.float32
BF16 = jnp.bfloat16
MIB = 1 << 20


def shape(*dims, dtype=F32):
    return jax.ShapeDtypeStruct(dims, dtype)


def call(kernel, outs, args, in_specs=None, scratch=(), vmem=16, flops=0, moved=2 * MIB, name=None):
    return pl.pallas_call(
        kernel,
        out_shape=outs,
        in_specs=in_specs or [pl.BlockSpec(memory_space=pltpu.VMEM)] * len(args),
        scratch_shapes=scratch,
        compiler_params=pltpu.CompilerParams(vmem_limit_bytes=vmem * MIB),
        cost_estimate=pl.CostEstimate(flops=flops, bytes_accessed=moved, transcendentals=0),
        name=name,
    )(*args)


def stay(*values):
    return [pltpu.with_memory_space_constraint(value, pltpu.HBM) for value in values]


def split_parts(value):
    high = value.astype(BF16)
    low = (value - high.astype(F32)).astype(BF16)
    return high, low


def row_index(count, width):
    return lax.broadcasted_iota(jnp.int32, (count, width), 0)


def lane_index(count):
    return lax.broadcasted_iota(jnp.int32, (count, CZ), 1)


def ahead_x(field, face):
    return jnp.concatenate([field[CY:], face], axis=0)


def behind_x(field, face):
    return jnp.concatenate([face, field[:-CY]], axis=0)


def spread(face):
    return jnp.broadcast_to(face[:, None, :], (CX, CY, CZ)).reshape(ROWS, CZ)


def ahead_y(field, face, last):
    return jnp.where(last, spread(face), pltpu.roll(field, ROWS - 1, 0))


def behind_y(field, face, first):
    return jnp.where(first, spread(face), pltpu.roll(field, 1, 0))


def ahead_z(field, other, lane):
    return pltpu.roll(jnp.where(lane == 0, other, field), CZ - 1, 1)


def behind_z(field, other, lane):
    return pltpu.roll(jnp.where(lane == CZ - 1, other, field), 1, 1)


def row_in_brick():
    rows = row_index(ROWS, CZ)
    return rows - CY * ((rows * 2731) >> 16)


def first_layers(field_ref, out_x, out_y, out_z):
    out_x[0] = field_ref[1, 0:CY]
    out_x[1] = field_ref[2, 0:CY]
    for place, comp in ((0, 0), (1, 2)):
        for layer in range(CX):
            out_y[place, layer : layer + 1] = field_ref[comp, layer * CY : layer * CY + 1]
    out_z[0] = field_ref[0]
    out_z[1] = field_ref[1]


def last_layers(field_ref, out_x, out_y, out_z):
    out_x[0] = field_ref[1, ROWS - CY : ROWS]
    out_x[1] = field_ref[2, ROWS - CY : ROWS]
    for place, comp in ((0, 0), (1, 2)):
        for layer in range(CX):
            row = layer * CY + CY - 1
            out_y[place, layer : layer + 1] = field_ref[comp, row : row + 1]
    out_z[0] = field_ref[0]
    out_z[1] = field_ref[1]


def inside(faces, ahead):
    kept = []
    for face, axis in zip(faces, ("gx", "gy", "gz")):
        index = lax.axis_index(axis)
        real = index < lax.axis_size(axis) - 1 if ahead else index > 0
        kept.append([jnp.where(real, face[place], 0.0) for place in range(2)])
    return kept


def prepare_kernel(e_hbm, state_hbm, out_x, out_y, out_z, e_out, state, sems):
    copies = [
        pltpu.make_async_copy(e_hbm, e_out, sems.at[0]),
        pltpu.make_async_copy(state_hbm, state, sems.at[1]),
    ]
    for copy in copies:
        copy.start()
    copies[0].wait()
    first_layers(e_out, out_x, out_y, out_z)
    copies[1].wait()


def pack_kernel(state, packed):
    lower, lasing, upper = state[7], state[8], state[9]
    lasing_free = lasing + time_step * (upper / upper_life - lasing / lasing_life)
    lower_free = lower + time_step * (lasing / lasing_life - lower / lower_life)
    polar = [state[comp] for comp in range(3)]
    free = [keep_rate * state[3 + comp] - spring * polar[comp] for comp in range(3)]
    for field, value in enumerate(free + [lasing - lower] + polar + [lasing_free - lower_free]):
        for owner in range(SLOTS // 2):
            packed[owner, 2 * field : 2 * field + 2] = value[2 * owner : 2 * owner + 2]


def magnetic_kernel(e_ref, h_ref, face_x, face_y, face_z, h_out, out_x, out_y, out_z):
    lane = lane_index(ROWS)
    last = row_in_brick() == CY - 1
    face_x, face_y, face_z = inside((face_x, face_y, face_z), True)
    ex, ey, ez = e_ref[0], e_ref[1], e_ref[2]
    first = (ahead_y(ez, face_y[1], last) - ez) - (ahead_z(ey, face_z[1], lane) - ey)
    second = (ahead_z(ex, face_z[0], lane) - ex) - (ahead_x(ez, face_x[1]) - ez)
    third = (ahead_x(ey, face_x[0]) - ey) - (ahead_y(ex, face_y[0], last) - ex)
    h_out[0] = h_ref[0] - time_step * first
    h_out[1] = h_ref[1] - time_step * second
    h_out[2] = h_ref[2] - time_step * third
    last_layers(h_out, out_x, out_y, out_z)


def electric_curl(h_ref, face_x, face_y, face_z):
    lane = lane_index(ROWS)
    start = row_in_brick() == 0
    face_x, face_y, face_z = inside((face_x, face_y, face_z), False)
    hx, hy, hz = h_ref[0], h_ref[1], h_ref[2]
    first = (hz - behind_y(hz, face_y[1], start)) - (hy - behind_z(hy, face_z[1], lane))
    second = (hx - behind_z(hx, face_z[0], lane)) - (hz - behind_x(hz, face_x[1]))
    third = (hy - behind_x(hy, face_x[0])) - (hx - behind_y(hx, face_y[0], start))
    return first, second, third


HALF = ROWS // 2
WIDE = 2 * CZ


def wide_hits(offsets, width):
    hits = row_index(WIDE, width) == (offsets & (WIDE - 1))
    return hits.astype(F32).astype(BF16)


def tall_hits(offsets, width):
    return row_index(HALF, width) == (offsets >> 8)


def place_fields(first, fields_ref, dense, tall, spots, columns):
    for slot in range(SLOTS):
        across = slice(slot * CZ, (slot + 1) * CZ)
        hits = tall[:, across].reshape(6, 16, CZ)
        values = fields_ref[slot // 2, pl.ds(2 * first + slot % 2, 4, 2), :]
        for place, part in enumerate(split_parts(values)):
            part = part.astype(F32)
            for field in range(4):
                row = jnp.broadcast_to(part[field : field + 1], (16, CZ)).astype(BF16)
                top = (4 * place + field) * HALF
                spots[top : top + HALF, across] = (hits * row[None]).reshape(HALF, CZ)
    total = lax.dot_general(
        spots[...], columns[...], (((1,), (1,)), ((), ())), preferred_element_type=F32
    )
    total = total[: 4 * HALF] + total[4 * HALF :]
    for field in range(4):
        got = total[field * HALF : (field + 1) * HALF]
        dense[field, pl.ds(0, HALF, 2), :] = got[:, :CZ]
        dense[field, pl.ds(1, HALF, 2), :] = got[:, CZ:]


def scatter_kernel(placed, columns, fields_ref, dense, tall, spots):
    for slot in range(SLOTS):
        line = placed[slot : slot + 1]
        across = slice(slot * CZ, (slot + 1) * CZ)
        tall[:, across] = tall_hits(line, CZ).astype(F32).astype(BF16)
    place_fields(0, fields_ref, dense, tall, spots, columns)


def scatter_sample_kernel(
    fields_ref,
    tall,
    columns,
    e_ref,
    h_ref,
    surf_ref,
    units_ref,
    dense,
    sampled,
    starts,
    turn,
    factors,
    spots,
):
    phase_tables(surf_ref, units_ref, starts, turn, factors)
    place_fields(4, fields_ref, dense, tall, spots, columns)
    sample_rows(e_ref, h_ref, surf_ref, sampled)


def electric_kernel(
    e_ref, h_ref, face_x, face_y, face_z, eps_ref, dense, e_out, out_x, out_y, out_z, rates
):
    curls = electric_curl(h_ref, face_x, face_y, face_z)
    scaled = time_step * eps_ref[...]
    inversion = dense[3]
    power = jnp.zeros_like(inversion)
    for comp in range(3):
        field = e_ref[comp]
        rate = dense[comp] + gain_push * inversion * field
        power = power + field * rate
        rates[comp] = rate
        e_out[comp] = field + scaled * (curls[comp] - rate)
    rates[3] = power
    first_layers(e_out, out_x, out_y, out_z)


def paired(ref, comp):
    return jnp.concatenate(
        [ref[comp, pl.ds(0, HALF, 2), :], ref[comp, pl.ds(1, HALF, 2), :]], axis=1
    )


def stacked(fields):
    return jnp.concatenate(
        split_parts(jnp.concatenate([paired(ref, comp) for ref, comp in fields], axis=0)), axis=0
    )


def gather_lines(values, hits, offsets, width):
    tall = tall_hits(offsets, width)
    picked = jnp.dot(values, hits, preferred_element_type=F32)
    lines = []
    for field in range(6):
        rows = slice(field * HALF, (field + 1) * HALF)
        both = picked[rows] + picked[6 * HALF :][rows]
        lines.append(jnp.sum(jnp.where(tall, both, 0.0), axis=0, keepdims=True))
    return lines


TAKE = 16


def drive_kernel(e_old, e_new, placed, columns, drives, values):
    values[...] = stacked([(ref, comp) for ref in (e_old, e_new) for comp in range(3)])
    for group in range(0, SLOTS, TAKE):
        offsets = jnp.concatenate([placed[group + n : group + n + 1] for n in range(TAKE)], axis=1)
        hits = columns[:, group * CZ : (group + TAKE) * CZ]
        got = gather_lines(values[...], hits, offsets, TAKE * CZ)
        for field in range(6):
            for slot in range(TAKE):
                drives[field, group + slot : group + slot + 1] = got[field][
                    :, slot * CZ : (slot + 1) * CZ
                ]


def sample_rows(e_ref, h_ref, surf_ref, sampled):
    values = stacked([(ref, comp) for ref in (e_ref, h_ref) for comp in range(3)])
    offsets = surf_ref[...]
    got = gather_lines(values, wide_hits(offsets, CZ), offsets, CZ)
    sampled[...] = jnp.zeros_like(sampled)
    for field in range(6):
        sampled[field : field + 1] = got[field]


def times(left, right):
    return (left[0] * right[0] - left[1] * right[1], left[1] * right[0] + left[0] * right[1])


def phase_tables(surf_ref, units_ref, starts, turn, factors):
    lanes = lax.broadcasted_iota(jnp.int32, (8, DIRS), 1)
    omega = freq_low + freq_pitch * (lanes & (FREQ - 1)).astype(F32)
    moment = omega * jnp.where(lanes < FREQ, time_step, 2.0 * time_step)
    for place, value in enumerate((jnp.cos(moment), jnp.sin(moment))):
        factors[place] = jnp.transpose(jnp.broadcast_to(value[0:1], (DIRS, DIRS)))
    cells = surf_ref[...]
    rows = cells >> 7
    layer = (rows * 2731) >> 16
    cell_x = lax.axis_index("gx") * CX + layer
    cell_y = lax.axis_index("gy") * CY + (rows - CY * layer)
    cell_z = lax.axis_index("gz") * CZ + (cells & (CZ - 1))
    along = jnp.zeros((CZ, DIRS), F32)
    for axis, (cell, size) in enumerate(((cell_x, 128), (cell_y, 192), (cell_z, 256))):
        place = cell.astype(F32) - 0.5 * (size - 1)
        column = jnp.transpose(jnp.broadcast_to(place, (CZ, CZ)))
        along = along + column * units_ref[axis : axis + 1]
    angle = (0.25 * freq_pitch) * along
    square = angle * angle
    cosine = 1.0 + square * (
        -1 / 2 + square * (1 / 24 + square * (-1 / 720 + square * (1 / 40320)))
    )
    sine = angle * (
        1.0 + square * (-1 / 6 + square * (1 / 120 + square * (-1 / 5040 + square * (1 / 362880))))
    )
    two = times((cosine, sine), (cosine, sine))
    powers = {1: times(two, two)}
    for power in (2, 4, 8, 16, 32):
        powers[power] = times(powers[power // 2], powers[power // 2])
    low_start = times(times(powers[16], powers[8]), times(powers[4], powers[2]))
    high_start = times(low_start, powers[32])
    turn[0], turn[1] = powers[1]
    starts[0], starts[1] = low_start
    starts[2], starts[3] = high_start


def phase_kernel(
    count_ref,
    owner_hbm,
    offsets_hbm,
    surf_hbm,
    h_hbm,
    eps_hbm,
    pump_hbm,
    far_hbm,
    placed,
    columns,
    surf_out,
    h_out,
    eps_out,
    pump_out,
    far_out,
    owner_ref,
    offsets_ref,
    sems,
):
    own = pl.ds(pl.multiple_of(FAR * lax.axis_index("gy"), 8), FAR)
    copies = [
        pltpu.make_async_copy(source, target, sems.at[place])
        for place, (source, target) in enumerate(
            (
                (surf_hbm, surf_out),
                (owner_hbm, owner_ref),
                (offsets_hbm, offsets_ref),
                (h_hbm, h_out),
                (eps_hbm, eps_out),
                (pump_hbm, pump_out),
                (far_hbm.at[own], far_out),
            )
        )
    ]
    for copy in copies:
        copy.start()
    for copy in copies:
        copy.wait()
    count = count_ref[0]
    for slot in range(SLOTS):
        line = offsets_ref[slot : slot + 1]
        placed[pl.ds(owner_ref[0, slot], 1)] = jnp.where(slot < count, line, -1)
    for slot in range(SLOTS):
        columns[:, slot * CZ : (slot + 1) * CZ] = wide_hits(placed[slot : slot + 1], CZ)


FAR = 48
LOAD = 48


def partner(step):
    index = lax.axis_index("gx")
    return (index >> 2) ^ step, (index & 3) ^ step


def chunk(drives, owner_x):
    return drives[:, pl.ds(pl.multiple_of(8 * owner_x, 8), 8)]


def pick(tiles, pairs):
    rows = row_index(8, CZ) >> 1
    result = jnp.zeros((8, CZ), F32)
    for tile, (taken, put) in zip(tiles, pairs):
        moved = pltpu.roll(tile, (2 * put - 2 * taken + 8) & 7, 0)
        result = jnp.where(rows == put, moved, result)
    return result


def fold_kernel(pieces, drives, total, *loads):
    total[...] = jnp.sum(pieces[...], axis=0)
    for step in (1, 2, 3):
        load = loads[step - 1]
        load[0:FAR] = total[...]
        load[FAR : FAR + LOAD] = chunk(drives, partner(step)[0]).reshape(LOAD, CZ)
    loads[1][FAR + LOAD :] = jnp.zeros((8, CZ), F32)


def relay_kernel(total_in, drives, one, two, three, total, kept, *loads):
    total[...] = (total_in[...] + one[0:FAR]) + (two[0:FAR] + three[0:FAR])
    held = [chunk(drives, partner(0)[0]).reshape(LOAD, CZ)]
    held += [arrived[FAR : FAR + LOAD] for arrived in (one, two, three)]
    for step in range(4):
        target = partner(step)[1]
        out, first = (loads[step - 1], FAR) if step else (kept, 0)
        if step:
            out[0:FAR] = total[...]
        for field in range(6):
            tiles = [value[8 * field : 8 * field + 8] for value in held]
            start = first + 8 * field
            out[start : start + 8] = pick(tiles, [(target, source) for source in range(4)])
    loads[1][FAR + LOAD :] = jnp.zeros((8, CZ), F32)


def finish_kernel(total_in, kept, one, two, three, far_ref, spread_out, back):
    total = (total_in[...] + one[0:FAR]) + (two[0:FAR] + three[0:FAR])
    total = far_ref[...] + total
    for peer in range(8):
        spread_out[peer] = total
    held = [kept[...]] + [arrived[FAR : FAR + LOAD] for arrived in (one, two, three)]
    for source in range(4):
        rows = pl.ds(pl.multiple_of(8 * partner(source)[0], 8), 8)
        for field in range(6):
            tiles = [value[8 * field : 8 * field + 8] for value in held]
            back[field, rows] = pick(tiles, [(source, partner(step)[1]) for step in range(4)])


def final_kernel(
    e_ref,
    h_ref,
    face_x,
    face_y,
    face_z,
    eps_ref,
    rates,
    dense,
    surf_ref,
    early_ref,
    starts,
    turn,
    factors,
    e_out,
    left_out,
    send_out,
    late,
    now,
):
    curls = electric_curl(h_ref, face_x, face_y, face_z)
    scaled = time_step * eps_ref[...]
    later = dense[3] + (2.0 * time_step * cross_rate) * rates[3]
    for comp in range(3):
        field = e_ref[comp]
        polar = dense[comp] + time_step * rates[comp]
        rate = keep_rate * rates[comp] - spring * polar + gain_push * later * field
        e_out[comp] = field + scaled * (curls[comp] - rate)
    sample_rows(e_out, h_ref, surf_ref, late)
    scale = 1.0 / math.sqrt(STEPS * CZ * 256)
    high, low = split_parts(scale * jnp.concatenate([early_ref[...], late[...]], axis=0))
    left = jnp.concatenate(
        [
            jnp.concatenate([high, high], axis=1),
            jnp.concatenate([low, jnp.zeros_like(low)], axis=1),
        ],
        axis=0,
    )
    left_out[...] = left
    far_half(1, left, starts, turn, factors, send_out, now)


def keep_kernel(left, starts, turn, factors, keep_out, now):
    far_half(0, left[...], starts, turn, factors, keep_out, now)


def far_half(side, left, starts, turn, factors, out, now):
    target = lax.rem(lax.axis_index("gz") + side, 2)
    now[0] = starts[2 * target]
    now[1] = starts[2 * target + 1]
    for freq in range(FREQ // 2):
        here = (now[0], now[1])
        re_high, re_low = split_parts(here[0])
        im_high, im_low = split_parts(here[1])
        right = jnp.concatenate(
            [
                jnp.concatenate([re_high, im_high], axis=1),
                jnp.concatenate([re_low, im_low], axis=1),
            ],
            axis=0,
        )
        if freq < FREQ // 2 - 1:
            now[0], now[1] = times(here, (turn[0], turn[1]))
        both = jnp.dot(left, right, preferred_element_type=F32)
        both = both[0:16] + both[16:32]
        real = jnp.zeros((8, DIRS), F32)
        imag = jnp.zeros((8, DIRS), F32)
        for step in range(STEPS):
            row = pl.ds(step * FREQ + target * (FREQ // 2) + freq, 1)
            cosine = factors[0, row]
            sine = factors[1, row]
            upper = both[8 * step : 8 * step + 8, 0:DIRS]
            under = both[8 * step : 8 * step + 8, DIRS:]
            real = real + (cosine * upper + sine * under)
            imag = imag + (cosine * under - sine * upper)
        for comp in range(6):
            row = comp * (FREQ // 2) + freq
            out[row : row + 1] = real[comp : comp + 1]
            row = (comp + 6) * (FREQ // 2) + freq
            out[row : row + 1] = imag[comp : comp + 1]


def atoms_kernel(state_ref, pump_ref, drives, far_ref, out, far_out):
    far_out[...] = far_ref[...]
    polar = [state_ref[c] for c in range(3)]
    rate = [state_ref[3 + c] for c in range(3)]
    ground, lower, lasing, upper = [state_ref[6 + level] for level in range(4)]
    pump = pump_ref[...]
    for step in range(STEPS):
        drive = [drives[3 * step + c] for c in range(3)]
        inversion = lasing - lower
        power = jnp.zeros_like(pump)
        for c in range(3):
            rate[c] = (
                (1.0 - half) * rate[c]
                + time_step
                * (coupling * inversion * drive[c] - omega_rest * omega_rest * polar[c])
            ) / (1.0 + half)
            polar[c] = polar[c] + time_step * rate[c]
            power = power + drive[c] * rate[c]
        upper_new = upper + time_step * (pump * ground - upper / upper_life)
        lasing_new = lasing + time_step * (
            upper / upper_life - lasing / lasing_life + cross_rate * power
        )
        lower_new = lower + time_step * (
            lasing / lasing_life - lower / lower_life - cross_rate * power
        )
        ground = ground + time_step * (lower / lower_life - pump * ground)
        lower, lasing, upper = lower_new, lasing_new, upper_new
    for place, value in enumerate(polar + rate + [ground, lower, lasing, upper]):
        out[place] = value


def store_kernel(e_ref, h_ref, e_out, h_out):
    e_out[...] = e_ref[...]
    h_out[...] = h_ref[...]


def directions(count):
    index = np.arange(count, dtype=np.float32)
    cosine = np.float32(1.0) - np.float32(2.0) * (index + np.float32(0.5)) / np.float32(count)
    sine = np.sqrt(np.float32(1.0) - cosine * cosine)
    azimuth = (np.float32(golden) * index).astype(np.float64)
    rows = np.zeros((8, count), np.float32)
    rows[0] = sine * np.cos(azimuth).astype(np.float32)
    rows[1] = sine * np.sin(azimuth).astype(np.float32)
    rows[2] = cosine
    return rows


def local(
    efield,
    hfield,
    inv_eps,
    gain_state,
    pump,
    gain_offsets,
    gain_count,
    block_owner,
    surf_offsets,
    far_acc,
):
    dense = shape(3, ROWS, CZ)
    faces = (shape(2, CY, CZ), shape(2, CX, CZ), shape(2, ROWS, CZ))
    down = [[((i + 1) % n, i) for i in range(n)] for n in (16, 8, 2)]
    up = [[(i, (i + 1) % n) for i in range(n)] for n in (16, 8, 2)]
    vmem = pl.BlockSpec(memory_space=pltpu.VMEM)

    hbm = pl.BlockSpec(memory_space=pltpu.HBM)

    def shifted(parts, perms):
        return [
            lax.ppermute(part, axis, perm)
            for part, axis, perm in zip(parts, ("gx", "gy", "gz"), perms)
        ]

    *near, e_old, state = call(
        prepare_kernel,
        faces + (dense, shape(10, SLOTS, CZ)),
        stay(
            efield.reshape(3, ROWS, CZ),
            jnp.transpose(gain_state.reshape(SLOTS, 10, CZ), (1, 0, 2)),
        ),
        in_specs=[hbm] * 2,
        scratch=[pltpu.SemaphoreType.DMA((2,))],
        name="prepare",
    )
    near = shifted(near, down)
    packed = call(pack_kernel, shape(SLOTS // 2, 16, CZ), (state,), name="pack")
    fields = lax.all_to_all(packed, "gx", 0, 0, tiled=True)
    placed, columns, surf, h_old, eps, pumps, far_part = call(
        phase_kernel,
        (
            shape(SLOTS, CZ, dtype=jnp.int32),
            shape(WIDE, SLOTS * CZ, dtype=BF16),
            shape(1, CZ, dtype=jnp.int32),
            dense,
            shape(ROWS, CZ),
            shape(SLOTS, CZ),
            shape(FAR, DIRS),
        ),
        [gain_count.reshape(1)]
        + stay(
            block_owner.reshape(1, SLOTS),
            gain_offsets.reshape(SLOTS, CZ),
            surf_offsets.reshape(1, CZ),
            hfield.reshape(3, ROWS, CZ),
            inv_eps.reshape(ROWS, CZ),
            pump.reshape(SLOTS, CZ),
            jnp.transpose(far_acc, (1, 0, 2)).reshape(8 * FAR, DIRS),
        ),
        in_specs=[pl.BlockSpec(memory_space=pltpu.SMEM)] + [hbm] * 7,
        scratch=[
            pltpu.SMEM((1, SLOTS), jnp.int32),
            pltpu.VMEM((SLOTS, CZ), jnp.int32),
            pltpu.SemaphoreType.DMA((7,)),
        ],
        moved=MIB // 4,
        name="phase",
    )
    h_one, *edge = call(
        magnetic_kernel,
        (dense,) + faces,
        (e_old, h_old, *near),
        flops=10**11,
        moved=100 * MIB,
        name="magnetic",
    )
    edge = shifted(edge, up)
    spots = pltpu.VMEM((8 * HALF, SLOTS * CZ), BF16)
    spread_now, tall = call(
        scatter_kernel,
        (shape(4, ROWS, CZ), shape(HALF, SLOTS * CZ, dtype=BF16)),
        (placed, columns, fields),
        scratch=[spots],
        name="scatter",
    )
    e_one, *near, rates = call(
        electric_kernel,
        (dense,) + faces + (shape(4, ROWS, CZ),),
        (e_old, h_one, *edge, eps, spread_now),
        name="electric",
    )
    near = shifted(near, down)
    spread_next, early, starts, turn, factors = call(
        scatter_sample_kernel,
        (
            shape(4, ROWS, CZ),
            shape(8, CZ),
            shape(4, CZ, DIRS),
            shape(2, CZ, DIRS),
            shape(2, STEPS * FREQ, DIRS),
        ),
        [fields, tall, columns, e_one, h_one, surf] + stay(jnp.asarray(directions(DIRS))),
        scratch=[spots],
        name="scatter2",
    )
    *near, spread_next = lax.optimization_barrier((*near, spread_next))
    h_two, *edge = call(magnetic_kernel, (dense,) + faces, (e_one, h_one, *near), name="magnetic2")
    edge = shifted(edge, up)
    e_seen, h_two = lax.optimization_barrier((e_one, h_two))
    drives = call(
        drive_kernel,
        shape(6, SLOTS, CZ),
        (e_old, e_seen, placed, columns),
        scratch=[pltpu.VMEM((12 * HALF, WIDE), BF16)],
        name="drive",
    )
    *edge, drives = lax.optimization_barrier((*edge, drives))
    part = shape(12 * FREQ // 2, DIRS)
    hold = pltpu.VMEM((2, CZ, DIRS), F32)
    e_two, left, send = call(
        final_kernel,
        (dense, shape(32, 2 * CZ, dtype=BF16), part),
        (e_one, h_two, *edge, eps, rates, spread_next, surf, early, starts, turn, factors),
        scratch=[pltpu.VMEM((8, CZ), F32), hold],
        name="final",
    )
    send = lax.ppermute(send, "gz", down[2])
    keep = call(
        keep_kernel, part, (left, starts, turn, factors), scratch=[hold], flops=10**10, name="keep"
    )
    chip = keep + send
    pieces = lax.all_to_all(chip.reshape(8, FAR, DIRS), "gy", 0, 0, tiled=True)
    loads = tuple(shape(FAR + LOAD + 8 * (step == 2), CZ) for step in (1, 2, 3))
    total, *sent = call(
        fold_kernel, (shape(FAR, DIRS),) + loads, (pieces, drives), name="fold"
    )
    got = [
        lax.ppermute(
            value, "gx", [(a * 4 + z, (a ^ k) * 4 + z) for a in range(4) for z in range(4)]
        )
        for k, value in enumerate(sent, 1)
    ]
    total, kept, *sent = call(
        relay_kernel,
        (shape(FAR, DIRS), shape(LOAD, CZ)) + loads,
        (total, drives, *got),
        name="relay",
    )
    got = [
        lax.ppermute(
            value, "gx", [(a * 4 + z, a * 4 + (z ^ k)) for a in range(4) for z in range(4)]
        )
        for k, value in enumerate(sent, 1)
    ]
    e_out, h_out = call(store_kernel, (dense, dense), (e_two, h_two), name="store")
    copies, back = call(
        finish_kernel,
        (shape(8, FAR, DIRS), shape(6, SLOTS, CZ)),
        (total, kept, *got, far_part),
        name="finish",
    )
    copies, e_out, h_out = lax.optimization_barrier((copies, e_out, h_out))
    gathered = lax.all_to_all(copies, "gy", 0, 0, tiled=True)
    back, gathered = lax.optimization_barrier((back, gathered))
    state_out, far_out = call(
        atoms_kernel,
        (shape(10, SLOTS, CZ), shape(8, FAR, DIRS)),
        (state, pumps, back, gathered),
        name="atoms",
    )
    far_out = jnp.transpose(far_out.reshape(12, FREQ // 2, DIRS), (1, 0, 2))
    return (
        e_out.reshape(efield.shape),
        h_out.reshape(hfield.shape),
        jnp.transpose(state_out, (1, 0, 2)).reshape(gain_state.shape),
        far_out,
    )


def solution(mesh):
    placed = (
        P(None, "gx", "gy", "gz"),
        P(None, "gx", "gy", "gz"),
        P("gx", "gy", "gz"),
        P("gx", "gy", "gz", None, None, None),
        P("gx", "gy", "gz", None, None),
        P("gx", "gy", "gz", None, None),
        P("gx", "gy", "gz"),
        P("gx", "gy", "gz", None),
        P("gx", "gy", "gz", None),
        P("gz", None, None),
    )
    return jax.shard_map(
        local,
        mesh=mesh,
        in_specs=placed,
        out_specs=(
            P(None, "gx", "gy", "gz"),
            P(None, "gx", "gy", "gz"),
            P("gx", "gy", "gz", None, None, None),
            P("gz", None, None),
        ),
        check_vma=False,
    )
```

```python
import math

import jax
import jax.numpy as jnp
import numpy as np
from jax import lax
from jax.experimental import pallas as pl
from jax.experimental.pallas import tpu as pltpu
from jax.sharding import PartitionSpec as P

FREQ = 64
STEPS = 2
CX = 8
CY = 24
CZ = 128
ROWS = CX * CY
SLOTS = 32
DIRS = 128

time_step = 0.5
damping = 0.1
omega_rest = 1.0
coupling = 0.5
cross_rate = 0.3
upper_life = 2.0
lasing_life = 20.0
lower_life = 2.0
freq_low = 0.3
freq_pitch = 0.01
golden = 2.399963229728653

half = 0.5 * damping * time_step
keep_rate = (1.0 - half) / (1.0 + half)
spring = time_step * omega_rest * omega_rest / (1.0 + half)
gain_push = time_step * coupling / (1.0 + half)

F32 = jnp.float32
BF16 = jnp.bfloat16
MIB = 1 << 20


def shape(*dims, dtype=F32):
    return jax.ShapeDtypeStruct(dims, dtype)


def call(kernel, outs, args, in_specs=None, scratch=(), vmem=16, flops=0, moved=2 * MIB, name=None):
    return pl.pallas_call(
        kernel,
        out_shape=outs,
        in_specs=in_specs or [pl.BlockSpec(memory_space=pltpu.VMEM)] * len(args),
        scratch_shapes=scratch,
        compiler_params=pltpu.CompilerParams(vmem_limit_bytes=vmem * MIB),
        cost_estimate=pl.CostEstimate(flops=flops, bytes_accessed=moved, transcendentals=0),
        name=name,
    )(*args)


def stay(*values):
    return [pltpu.with_memory_space_constraint(value, pltpu.HBM) for value in values]


def split_parts(value):
    high = value.astype(BF16)
    low = (value - high.astype(F32)).astype(BF16)
    return high, low


def row_index(count, width):
    return lax.broadcasted_iota(jnp.int32, (count, width), 0)


def lane_index(count):
    return lax.broadcasted_iota(jnp.int32, (count, CZ), 1)


def ahead_x(field, face):
    return jnp.concatenate([field[CY:], face], axis=0)


def behind_x(field, face):
    return jnp.concatenate([face, field[:-CY]], axis=0)


def spread(face):
    return jnp.broadcast_to(face[:, None, :], (CX, CY, CZ)).reshape(ROWS, CZ)


def ahead_y(field, face, last):
    return jnp.where(last, spread(face), pltpu.roll(field, ROWS - 1, 0))


def behind_y(field, face, first):
    return jnp.where(first, spread(face), pltpu.roll(field, 1, 0))


def ahead_z(field, other, lane):
    return pltpu.roll(jnp.where(lane == 0, other, field), CZ - 1, 1)


def behind_z(field, other, lane):
    return pltpu.roll(jnp.where(lane == CZ - 1, other, field), 1, 1)


def row_in_brick():
    rows = row_index(ROWS, CZ)
    return rows - CY * ((rows * 2731) >> 16)


def first_layers(field_ref, out_x, out_y, out_z):
    out_x[0] = field_ref[1, 0:CY]
    out_x[1] = field_ref[2, 0:CY]
    for place, comp in ((0, 0), (1, 2)):
        for layer in range(CX):
            out_y[place, layer : layer + 1] = field_ref[comp, layer * CY : layer * CY + 1]
    out_z[0] = field_ref[0]
    out_z[1] = field_ref[1]


def last_layers(field_ref, out_x, out_y, out_z):
    out_x[0] = field_ref[1, ROWS - CY : ROWS]
    out_x[1] = field_ref[2, ROWS - CY : ROWS]
    for place, comp in ((0, 0), (1, 2)):
        for layer in range(CX):
            row = layer * CY + CY - 1
            out_y[place, layer : layer + 1] = field_ref[comp, row : row + 1]
    out_z[0] = field_ref[0]
    out_z[1] = field_ref[1]


def inside(faces, ahead):
    kept = []
    for face, axis in zip(faces, ("gx", "gy", "gz")):
        index = lax.axis_index(axis)
        real = index < lax.axis_size(axis) - 1 if ahead else index > 0
        kept.append([jnp.where(real, face[place], 0.0) for place in range(2)])
    return kept


def prepare_kernel(e_hbm, state_hbm, out_x, out_y, out_z, e_out, state, sems):
    copies = [
        pltpu.make_async_copy(e_hbm, e_out, sems.at[0]),
        pltpu.make_async_copy(state_hbm, state, sems.at[1]),
    ]
    for copy in copies:
        copy.start()
    copies[0].wait()
    first_layers(e_out, out_x, out_y, out_z)
    copies[1].wait()


def pack_kernel(state, packed):
    lower, lasing, upper = state[7], state[8], state[9]
    lasing_free = lasing + time_step * (upper / upper_life - lasing / lasing_life)
    lower_free = lower + time_step * (lasing / lasing_life - lower / lower_life)
    polar = [state[comp] for comp in range(3)]
    free = [keep_rate * state[3 + comp] - spring * polar[comp] for comp in range(3)]
    for field, value in enumerate(free + [lasing - lower] + polar + [lasing_free - lower_free]):
        for owner in range(SLOTS // 2):
            packed[owner, 2 * field : 2 * field + 2] = value[2 * owner : 2 * owner + 2]


def magnetic_kernel(e_ref, h_ref, face_x, face_y, face_z, h_out, out_x, out_y, out_z):
    lane = lane_index(ROWS)
    last = row_in_brick() == CY - 1
    face_x, face_y, face_z = inside((face_x, face_y, face_z), True)
    ex, ey, ez = e_ref[0], e_ref[1], e_ref[2]
    first = (ahead_y(ez, face_y[1], last) - ez) - (ahead_z(ey, face_z[1], lane) - ey)
    second = (ahead_z(ex, face_z[0], lane) - ex) - (ahead_x(ez, face_x[1]) - ez)
    third = (ahead_x(ey, face_x[0]) - ey) - (ahead_y(ex, face_y[0], last) - ex)
    h_out[0] = h_ref[0] - time_step * first
    h_out[1] = h_ref[1] - time_step * second
    h_out[2] = h_ref[2] - time_step * third
    last_layers(h_out, out_x, out_y, out_z)


def electric_curl(h_ref, face_x, face_y, face_z):
    lane = lane_index(ROWS)
    start = row_in_brick() == 0
    face_x, face_y, face_z = inside((face_x, face_y, face_z), False)
    hx, hy, hz = h_ref[0], h_ref[1], h_ref[2]
    first = (hz - behind_y(hz, face_y[1], start)) - (hy - behind_z(hy, face_z[1], lane))
    second = (hx - behind_z(hx, face_z[0], lane)) - (hz - behind_x(hz, face_x[1]))
    third = (hy - behind_x(hy, face_x[0])) - (hx - behind_y(hx, face_y[0], start))
    return first, second, third


HALF = ROWS // 2
WIDE = 2 * CZ


def wide_hits(offsets, width):
    hits = row_index(WIDE, width) == (offsets & (WIDE - 1))
    return hits.astype(F32).astype(BF16)


def tall_hits(offsets, width):
    return row_index(HALF, width) == (offsets >> 8)


def place_fields(first, fields_ref, dense, tall, spots, columns):
    for slot in range(SLOTS):
        across = slice(slot * CZ, (slot + 1) * CZ)
        hits = tall[:, across].reshape(6, 16, CZ)
        values = fields_ref[slot // 2, pl.ds(2 * first + slot % 2, 4, 2), :]
        for place, part in enumerate(split_parts(values)):
            part = part.astype(F32)
            for field in range(4):
                row = jnp.broadcast_to(part[field : field + 1], (16, CZ)).astype(BF16)
                top = (4 * place + field) * HALF
                spots[top : top + HALF, across] = (hits * row[None]).reshape(HALF, CZ)
    total = lax.dot_general(
        spots[...], columns[...], (((1,), (1,)), ((), ())), preferred_element_type=F32
    )
    total = total[: 4 * HALF] + total[4 * HALF :]
    for field in range(4):
        got = total[field * HALF : (field + 1) * HALF]
        dense[field, pl.ds(0, HALF, 2), :] = got[:, :CZ]
        dense[field, pl.ds(1, HALF, 2), :] = got[:, CZ:]


def scatter_kernel(placed, fields_ref, dense, tall, columns, spots):
    for slot in range(SLOTS):
        line = placed[slot : slot + 1]
        across = slice(slot * CZ, (slot + 1) * CZ)
        columns[:, across] = wide_hits(line, CZ)
        tall[:, across] = tall_hits(line, CZ).astype(F32).astype(BF16)
    place_fields(0, fields_ref, dense, tall, spots, columns)


def scatter_sample_kernel(
    fields_ref, tall, columns, e_ref, h_ref, surf_ref, dense, sampled, spots
):
    place_fields(4, fields_ref, dense, tall, spots, columns)
    sample_rows(e_ref, h_ref, surf_ref, sampled)


def electric_kernel(
    e_ref, h_ref, face_x, face_y, face_z, eps_ref, dense, e_out, out_x, out_y, out_z, rates
):
    curls = electric_curl(h_ref, face_x, face_y, face_z)
    scaled = time_step * eps_ref[...]
    inversion = dense[3]
    power = jnp.zeros_like(inversion)
    for comp in range(3):
        field = e_ref[comp]
        rate = dense[comp] + gain_push * inversion * field
        power = power + field * rate
        rates[comp] = rate
        e_out[comp] = field + scaled * (curls[comp] - rate)
    rates[3] = power
    first_layers(e_out, out_x, out_y, out_z)


def paired(ref, comp):
    return jnp.concatenate(
        [ref[comp, pl.ds(0, HALF, 2), :], ref[comp, pl.ds(1, HALF, 2), :]], axis=1
    )


def stacked(fields):
    return jnp.concatenate(
        split_parts(jnp.concatenate([paired(ref, comp) for ref, comp in fields], axis=0)), axis=0
    )


def gather_lines(values, hits, offsets, width):
    tall = tall_hits(offsets, width)
    picked = jnp.dot(values, hits, preferred_element_type=F32)
    lines = []
    fields = values.shape[0] // (2 * HALF)
    for field in range(fields):
        rows = slice(field * HALF, (field + 1) * HALF)
        both = picked[rows] + picked[fields * HALF :][rows]
        lines.append(jnp.sum(jnp.where(tall, both, 0.0), axis=0, keepdims=True))
    return lines


TAKE = 16


def drive_kernel(
    e_old, e_new, placed, columns, h_ref, surf_ref, drives, seen, values
):
    seen[...] = jnp.zeros_like(seen)
    sample_field(h_ref, surf_ref, seen, 3)
    values[...] = stacked([(ref, comp) for ref in (e_old, e_new) for comp in range(3)])
    for group in range(0, SLOTS, TAKE):
        offsets = jnp.concatenate([placed[group + n : group + n + 1] for n in range(TAKE)], axis=1)
        hits = columns[:, group * CZ : (group + TAKE) * CZ]
        got = gather_lines(values[...], hits, offsets, TAKE * CZ)
        for field in range(6):
            for slot in range(TAKE):
                drives[field, group + slot : group + slot + 1] = got[field][
                    :, slot * CZ : (slot + 1) * CZ
                ]


def sample_field(ref, surf_ref, sampled, first):
    offsets = surf_ref[...]
    values = stacked([(ref, comp) for comp in range(3)])
    got = gather_lines(values, wide_hits(offsets, CZ), offsets, CZ)
    for comp in range(3):
        sampled[first + comp : first + comp + 1] = got[comp]


def sample_rows(e_ref, h_ref, surf_ref, sampled):
    values = stacked([(ref, comp) for ref in (e_ref, h_ref) for comp in range(3)])
    offsets = surf_ref[...]
    got = gather_lines(values, wide_hits(offsets, CZ), offsets, CZ)
    sampled[...] = jnp.zeros_like(sampled)
    for field in range(6):
        sampled[field : field + 1] = got[field]


def times(left, right):
    return (left[0] * right[0] - left[1] * right[1], left[1] * right[0] + left[0] * right[1])


def phase_kernel(
    count_ref,
    owner_hbm,
    offsets_hbm,
    surf_hbm,
    units_hbm,
    h_hbm,
    eps_hbm,
    pump_hbm,
    far_hbm,
    placed,
    surf_out,
    starts,
    turn,
    factors,
    h_out,
    eps_out,
    pump_out,
    far_out,
    owner_ref,
    offsets_ref,
    units_ref,
    sems,
):
    own = pl.ds(pl.multiple_of(FAR * lax.axis_index("gy"), 8), FAR)
    copies = [
        pltpu.make_async_copy(source, target, sems.at[place])
        for place, (source, target) in enumerate(
            (
                (surf_hbm, surf_out),
                (units_hbm, units_ref),
                (owner_hbm, owner_ref),
                (offsets_hbm, offsets_ref),
                (h_hbm, h_out),
                (eps_hbm, eps_out),
                (pump_hbm, pump_out),
                (far_hbm.at[own], far_out),
            )
        )
    ]
    for copy in copies:
        copy.start()
    lanes = lax.broadcasted_iota(jnp.int32, (8, DIRS), 1)
    omega = freq_low + freq_pitch * (lanes & (FREQ - 1)).astype(F32)
    moment = omega * jnp.where(lanes < FREQ, time_step, 2.0 * time_step)
    for place, value in enumerate((jnp.cos(moment), jnp.sin(moment))):
        factors[place] = jnp.transpose(jnp.broadcast_to(value[0:1], (DIRS, DIRS)))
    copies[0].wait()
    copies[1].wait()
    cells = surf_out[...]
    rows = cells >> 7
    layer = (rows * 2731) >> 16
    cell_x = lax.axis_index("gx") * CX + layer
    cell_y = lax.axis_index("gy") * CY + (rows - CY * layer)
    cell_z = lax.axis_index("gz") * CZ + (cells & (CZ - 1))
    along = jnp.zeros((CZ, DIRS), F32)
    for axis, (cell, size) in enumerate(((cell_x, 128), (cell_y, 192), (cell_z, 256))):
        place = cell.astype(F32) - 0.5 * (size - 1)
        column = jnp.transpose(jnp.broadcast_to(place, (CZ, CZ)))
        along = along + column * units_ref[axis : axis + 1]
    angle = (0.25 * freq_pitch) * along
    square = angle * angle
    cosine = 1.0 + square * (
        -1 / 2 + square * (1 / 24 + square * (-1 / 720 + square * (1 / 40320)))
    )
    sine = angle * (
        1.0 + square * (-1 / 6 + square * (1 / 120 + square * (-1 / 5040 + square * (1 / 362880))))
    )
    two = times((cosine, sine), (cosine, sine))
    powers = {1: times(two, two)}
    for power in (2, 4, 8, 16, 32):
        powers[power] = times(powers[power // 2], powers[power // 2])
    low_start = times(times(powers[16], powers[8]), times(powers[4], powers[2]))
    high_start = times(low_start, powers[32])
    turn[0], turn[1] = powers[1]
    starts[0], starts[1] = low_start
    starts[2], starts[3] = high_start
    for copy in copies[2:]:
        copy.wait()
    count = count_ref[0]
    for slot in range(SLOTS):
        line = offsets_ref[slot : slot + 1]
        placed[pl.ds(owner_ref[0, slot], 1)] = jnp.where(slot < count, line, -1)


FAR = 48
LOAD = 48


def partner(step):
    index = lax.axis_index("gx")
    return (index >> 2) ^ step, (index & 3) ^ step


def chunk(drives, owner_x):
    return drives[:, pl.ds(pl.multiple_of(8 * owner_x, 8), 8)]


def pick(tiles, pairs):
    rows = row_index(8, CZ) >> 1
    result = jnp.zeros((8, CZ), F32)
    for tile, (taken, put) in zip(tiles, pairs):
        moved = pltpu.roll(tile, (2 * put - 2 * taken + 8) & 7, 0)
        result = jnp.where(rows == put, moved, result)
    return result


def fold_kernel(pieces, drives, total, *loads):
    total[...] = jnp.sum(pieces[...], axis=0)
    for step in (1, 2, 3):
        load = loads[step - 1]
        load[0:FAR] = total[...]
        load[FAR : FAR + LOAD] = chunk(drives, partner(step)[0]).reshape(LOAD, CZ)
    loads[1][FAR + LOAD :] = jnp.zeros((8, CZ), F32)


def relay_kernel(total_in, drives, one, two, three, total, kept, *loads):
    total[...] = (total_in[...] + one[0:FAR]) + (two[0:FAR] + three[0:FAR])
    held = [chunk(drives, partner(0)[0]).reshape(LOAD, CZ)]
    held += [arrived[FAR : FAR + LOAD] for arrived in (one, two, three)]
    for step in range(4):
        target = partner(step)[1]
        out, first = (loads[step - 1], FAR) if step else (kept, 0)
        if step:
            out[0:FAR] = total[...]
        for field in range(6):
            tiles = [value[8 * field : 8 * field + 8] for value in held]
            start = first + 8 * field
            out[start : start + 8] = pick(tiles, [(target, source) for source in range(4)])
    loads[1][FAR + LOAD :] = jnp.zeros((8, CZ), F32)


def finish_kernel(total_in, kept, one, two, three, far_ref, spread_out, back):
    total = (total_in[...] + one[0:FAR]) + (two[0:FAR] + three[0:FAR])
    total = far_ref[...] + total
    for peer in range(8):
        spread_out[peer] = total
    held = [kept[...]] + [arrived[FAR : FAR + LOAD] for arrived in (one, two, three)]
    for source in range(4):
        rows = pl.ds(pl.multiple_of(8 * partner(source)[0], 8), 8)
        for field in range(6):
            tiles = [value[8 * field : 8 * field + 8] for value in held]
            back[field, rows] = pick(tiles, [(source, partner(step)[1]) for step in range(4)])


def final_kernel(
    e_ref,
    h_ref,
    face_x,
    face_y,
    face_z,
    eps_ref,
    rates,
    dense,
    surf_ref,
    early_ref,
    seen,
    starts,
    turn,
    factors,
    e_out,
    left_out,
    send_out,
    late,
    now,
):
    curls = electric_curl(h_ref, face_x, face_y, face_z)
    scaled = time_step * eps_ref[...]
    later = dense[3] + (2.0 * time_step * cross_rate) * rates[3]
    for comp in range(3):
        field = e_ref[comp]
        polar = dense[comp] + time_step * rates[comp]
        rate = keep_rate * rates[comp] - spring * polar + gain_push * later * field
        e_out[comp] = field + scaled * (curls[comp] - rate)
    late[...] = seen[...]
    sample_field(e_out, surf_ref, late, 0)
    scale = 1.0 / math.sqrt(STEPS * CZ * 256)
    high, low = split_parts(scale * jnp.concatenate([early_ref[...], late[...]], axis=0))
    left = jnp.concatenate(
        [
            jnp.concatenate([high, high], axis=1),
            jnp.concatenate([low, jnp.zeros_like(low)], axis=1),
        ],
        axis=0,
    )
    left_out[...] = left
    far_half(1, left, starts, turn, factors, send_out, now)


def keep_kernel(left, starts, turn, factors, keep_out, now):
    far_half(0, left[...], starts, turn, factors, keep_out, now)


def far_half(side, left, starts, turn, factors, out, now):
    target = lax.rem(lax.axis_index("gz") + side, 2)
    now[0] = starts[2 * target]
    now[1] = starts[2 * target + 1]
    for freq in range(FREQ // 2):
        here = (now[0], now[1])
        re_high, re_low = split_parts(here[0])
        im_high, im_low = split_parts(here[1])
        right = jnp.concatenate(
            [
                jnp.concatenate([re_high, im_high], axis=1),
                jnp.concatenate([re_low, im_low], axis=1),
            ],
            axis=0,
        )
        if freq < FREQ // 2 - 1:
            now[0], now[1] = times(here, (turn[0], turn[1]))
        both = jnp.dot(left, right, preferred_element_type=F32)
        both = both[0:16] + both[16:32]
        real = jnp.zeros((8, DIRS), F32)
        imag = jnp.zeros((8, DIRS), F32)
        for step in range(STEPS):
            row = pl.ds(step * FREQ + target * (FREQ // 2) + freq, 1)
            cosine = factors[0, row]
            sine = factors[1, row]
            upper = both[8 * step : 8 * step + 8, 0:DIRS]
            under = both[8 * step : 8 * step + 8, DIRS:]
            real = real + (cosine * upper + sine * under)
            imag = imag + (cosine * under - sine * upper)
        for comp in range(6):
            row = comp * (FREQ // 2) + freq
            out[row : row + 1] = real[comp : comp + 1]
            row = (comp + 6) * (FREQ // 2) + freq
            out[row : row + 1] = imag[comp : comp + 1]


def atoms_kernel(state_ref, pump_ref, drives, far_ref, out, far_out):
    far_out[...] = far_ref[...]
    polar = [state_ref[c] for c in range(3)]
    rate = [state_ref[3 + c] for c in range(3)]
    ground, lower, lasing, upper = [state_ref[6 + level] for level in range(4)]
    pump = pump_ref[...]
    for step in range(STEPS):
        drive = [drives[3 * step + c] for c in range(3)]
        inversion = lasing - lower
        power = jnp.zeros_like(pump)
        for c in range(3):
            rate[c] = (
                (1.0 - half) * rate[c]
                + time_step
                * (coupling * inversion * drive[c] - omega_rest * omega_rest * polar[c])
            ) / (1.0 + half)
            polar[c] = polar[c] + time_step * rate[c]
            power = power + drive[c] * rate[c]
        upper_new = upper + time_step * (pump * ground - upper / upper_life)
        lasing_new = lasing + time_step * (
            upper / upper_life - lasing / lasing_life + cross_rate * power
        )
        lower_new = lower + time_step * (
            lasing / lasing_life - lower / lower_life - cross_rate * power
        )
        ground = ground + time_step * (lower / lower_life - pump * ground)
        lower, lasing, upper = lower_new, lasing_new, upper_new
    for place, value in enumerate(polar + rate + [ground, lower, lasing, upper]):
        out[place] = value


def store_kernel(e_ref, h_ref, e_out, h_out):
    e_out[...] = e_ref[...]
    h_out[...] = h_ref[...]


def directions(count):
    index = np.arange(count, dtype=np.float32)
    cosine = np.float32(1.0) - np.float32(2.0) * (index + np.float32(0.5)) / np.float32(count)
    sine = np.sqrt(np.float32(1.0) - cosine * cosine)
    azimuth = (np.float32(golden) * index).astype(np.float64)
    rows = np.zeros((8, count), np.float32)
    rows[0] = sine * np.cos(azimuth).astype(np.float32)
    rows[1] = sine * np.sin(azimuth).astype(np.float32)
    rows[2] = cosine
    return rows


def local(
    efield,
    hfield,
    inv_eps,
    gain_state,
    pump,
    gain_offsets,
    gain_count,
    block_owner,
    surf_offsets,
    far_acc,
):
    dense = shape(3, ROWS, CZ)
    faces = (shape(2, CY, CZ), shape(2, CX, CZ), shape(2, ROWS, CZ))
    down = [[((i + 1) % n, i) for i in range(n)] for n in (16, 8, 2)]
    up = [[(i, (i + 1) % n) for i in range(n)] for n in (16, 8, 2)]
    vmem = pl.BlockSpec(memory_space=pltpu.VMEM)

    hbm = pl.BlockSpec(memory_space=pltpu.HBM)

    def shifted(parts, perms):
        return [
            lax.ppermute(part, axis, perm)
            for part, axis, perm in zip(parts, ("gx", "gy", "gz"), perms)
        ]

    *near, e_old, state = call(
        prepare_kernel,
        faces + (dense, shape(10, SLOTS, CZ)),
        stay(
            efield.reshape(3, ROWS, CZ),
            jnp.transpose(gain_state.reshape(SLOTS, 10, CZ), (1, 0, 2)),
        ),
        in_specs=[hbm] * 2,
        scratch=[pltpu.SemaphoreType.DMA((2,))],
        name="prepare",
    )
    near = shifted(near, down)
    packed = call(pack_kernel, shape(SLOTS // 2, 16, CZ), (state,), name="pack")
    fields = lax.all_to_all(packed, "gx", 0, 0, tiled=True)
    placed, surf, starts, turn, factors, h_old, eps, pumps, far_part = call(
        phase_kernel,
        (
            shape(SLOTS, CZ, dtype=jnp.int32),
            shape(1, CZ, dtype=jnp.int32),
            shape(4, CZ, DIRS),
            shape(2, CZ, DIRS),
            shape(2, STEPS * FREQ, DIRS),
            dense,
            shape(ROWS, CZ),
            shape(SLOTS, CZ),
            shape(FAR, DIRS),
        ),
        [gain_count.reshape(1)]
        + stay(
            block_owner.reshape(1, SLOTS),
            gain_offsets.reshape(SLOTS, CZ),
            surf_offsets.reshape(1, CZ),
            jnp.asarray(directions(DIRS)),
            hfield.reshape(3, ROWS, CZ),
            inv_eps.reshape(ROWS, CZ),
            pump.reshape(SLOTS, CZ),
            jnp.transpose(far_acc, (1, 0, 2)).reshape(8 * FAR, DIRS),
        ),
        in_specs=[pl.BlockSpec(memory_space=pltpu.SMEM)] + [hbm] * 8,
        scratch=[
            pltpu.SMEM((1, SLOTS), jnp.int32),
            pltpu.VMEM((SLOTS, CZ), jnp.int32),
            pltpu.VMEM((8, DIRS), F32),
            pltpu.SemaphoreType.DMA((8,)),
        ],
        moved=MIB // 4,
        name="phase",
    )
    h_one, *edge = call(
        magnetic_kernel,
        (dense,) + faces,
        (e_old, h_old, *near),
        flops=10**11,
        moved=100 * MIB,
        name="magnetic",
    )
    edge = shifted(edge, up)
    spots = pltpu.VMEM((8 * HALF, SLOTS * CZ), BF16)
    spread_now, tall, columns = call(
        scatter_kernel,
        (
            shape(4, ROWS, CZ),
            shape(HALF, SLOTS * CZ, dtype=BF16),
            shape(WIDE, SLOTS * CZ, dtype=BF16),
        ),
        (placed, fields),
        scratch=[spots],
        name="scatter",
    )
    e_one, *near, rates = call(
        electric_kernel,
        (dense,) + faces + (shape(4, ROWS, CZ),),
        (e_old, h_one, *edge, eps, spread_now),
        name="electric",
    )
    near = shifted(near, down)
    spread_next, early = call(
        scatter_sample_kernel,
        (shape(4, ROWS, CZ), shape(8, CZ)),
        (fields, tall, columns, e_one, h_one, surf),
        scratch=[spots],
        name="scatter2",
    )
    *near, spread_next = lax.optimization_barrier((*near, spread_next))
    h_two, *edge = call(magnetic_kernel, (dense,) + faces, (e_one, h_one, *near), name="magnetic2")
    edge = shifted(edge, up)
    e_seen, h_two = lax.optimization_barrier((e_one, h_two))
    drives, seen = call(
        drive_kernel,
        (shape(6, SLOTS, CZ), shape(8, CZ)),
        (e_old, e_seen, placed, columns, h_two, surf),
        scratch=[pltpu.VMEM((12 * HALF, WIDE), BF16)],
        name="drive",
    )
    *edge, drives = lax.optimization_barrier((*edge, drives))
    part = shape(12 * FREQ // 2, DIRS)
    hold = pltpu.VMEM((2, CZ, DIRS), F32)
    e_two, left, send = call(
        final_kernel,
        (dense, shape(32, 2 * CZ, dtype=BF16), part),
        (e_one, h_two, *edge, eps, rates, spread_next, surf, early, seen, starts, turn, factors),
        scratch=[pltpu.VMEM((8, CZ), F32), hold],
        name="final",
    )
    send = lax.ppermute(send, "gz", down[2])
    keep = call(
        keep_kernel, part, (left, starts, turn, factors), scratch=[hold], flops=10**10, name="keep"
    )
    chip = keep + send
    pieces = lax.all_to_all(chip.reshape(8, FAR, DIRS), "gy", 0, 0, tiled=True)
    loads = tuple(shape(FAR + LOAD + 8 * (step == 2), CZ) for step in (1, 2, 3))
    total, *sent = call(
        fold_kernel, (shape(FAR, DIRS),) + loads, (pieces, drives), name="fold"
    )
    got = [
        lax.ppermute(
            value, "gx", [(a * 4 + z, (a ^ k) * 4 + z) for a in range(4) for z in range(4)]
        )
        for k, value in enumerate(sent, 1)
    ]
    total, kept, *sent = call(
        relay_kernel,
        (shape(FAR, DIRS), shape(LOAD, CZ)) + loads,
        (total, drives, *got),
        name="relay",
    )
    got = [
        lax.ppermute(
            value, "gx", [(a * 4 + z, a * 4 + (z ^ k)) for a in range(4) for z in range(4)]
        )
        for k, value in enumerate(sent, 1)
    ]
    e_out, h_out = call(store_kernel, (dense, dense), (e_two, h_two), name="store")
    copies, back = call(
        finish_kernel,
        (shape(8, FAR, DIRS), shape(6, SLOTS, CZ)),
        (total, kept, *got, far_part),
        name="finish",
    )
    copies, e_out, h_out = lax.optimization_barrier((copies, e_out, h_out))
    gathered = lax.all_to_all(copies, "gy", 0, 0, tiled=True)
    back, gathered = lax.optimization_barrier((back, gathered))
    state_out, far_out = call(
        atoms_kernel,
        (shape(10, SLOTS, CZ), shape(8, FAR, DIRS)),
        (state, pumps, back, gathered),
        name="atoms",
    )
    far_out = jnp.transpose(far_out.reshape(12, FREQ // 2, DIRS), (1, 0, 2))
    return (
        e_out.reshape(efield.shape),
        h_out.reshape(hfield.shape),
        jnp.transpose(state_out, (1, 0, 2)).reshape(gain_state.shape),
        far_out,
    )


def solution(mesh):
    placed = (
        P(None, "gx", "gy", "gz"),
        P(None, "gx", "gy", "gz"),
        P("gx", "gy", "gz"),
        P("gx", "gy", "gz", None, None, None),
        P("gx", "gy", "gz", None, None),
        P("gx", "gy", "gz", None, None),
        P("gx", "gy", "gz"),
        P("gx", "gy", "gz", None),
        P("gx", "gy", "gz", None),
        P("gz", None, None),
    )
    return jax.shard_map(
        local,
        mesh=mesh,
        in_specs=placed,
        out_specs=(
            P(None, "gx", "gy", "gz"),
            P(None, "gx", "gy", "gz"),
            P("gx", "gy", "gz", None, None, None),
            P("gz", None, None),
        ),
        check_vma=False,
    )
```
